32 devices in a mesh: dp: 8 (over z, x), tensor: 4 (over y, core).
Axes of the slice: x: 2, y: 2, z: 4, core: 2. Of those that a mesh axis runs over, the one named last changes fastest.
Arguments:
- inputs: bfloat16 [16384, 1024], P('dp'), may hold values from -6 to 6
- w_qkv: bfloat16 [3, 1024, 1024], P(None, None, 'tensor'), may hold values from -0.1875 to 0.1875
- w_out: bfloat16 [1024, 1024], P('tensor'), may hold values from -0.1875 to 0.1875
- w_up: bfloat16 [1024, 4096], P(None, 'tensor'), may hold values from -0.1875 to 0.1875
- w_down: bfloat16 [4096, 1024], P('tensor'), may hold values from -0.09375 to 0.09375
- norm_gains: float32 [4, 1024], replicated, may hold values from 0.5 to 1.5
- norm_biases: float32 [4, 1024], replicated, may hold values from -1.5 to 1.5
- out_cot: bfloat16 [16384, 1024], P('dp'), may hold values from -6 to 6
- group_ids: int32 [16384], P('dp'), may hold values from 0 to 15
- group_weights: float32 [16], replicated, may hold values from 0.25 to 4
Outputs:
- layer_out: bfloat16 [16384, 1024], P(('dp', 'tensor'))
- input_grad: float32 [16384, 1024], P(('dp', 'tensor'))
- w_qkv_grad: float32 [3, 1024, 1024], P(None, 'dp', 'tensor')
- w_out_grad: float32 [1024, 1024], P('tensor', 'dp')
- w_up_grad: float32 [1024, 4096], P('dp', 'tensor')
- w_down_grad: float32 [4096, 1024], P('tensor', 'dp')
- gains_grad: float32 [4, 1024], P(None, ('dp', 'tensor'))
- biases_grad: float32 [4, 1024], P(None, ('dp', 'tensor'))
The draws below stay inside these ranges and needn't reach their ends.
Inputs may be any that keep to these rules, and one draw needn't show every extreme that they name: `group_ids`: each token's index into group_weights.
All inputs are finite; a program needn't handle non-finite values.
Results may differ from the reference program's by a relative error of at most 0.013.
Values may be sent and summed in bfloat16 or wider, within the bound.
No kernel may reach another device: no remote copies, remote signals or barrier semaphores. Data moves between devices by JAX's collectives and lax.ppermute only.
A program may use at most 192 MiB of HBM per device.

```python
import math
import jax
import jax.numpy as jnp
from jax import lax

D = 1024
H = 16
DH = 64
FF = 4096
SEQ = 2048
GROUPS = 16
HD = 1024
TOKENS = 16384


def set_ends(values, own_key, smallest, high):
    dims = values.shape
    spot = [jax.random.randint(jax.random.fold_in(own_key, axis), (), 0, dims[axis]) for axis in range(len(dims))]
    values = values.at[tuple(spot)].set(smallest)
    longest = dims.index(max(dims))
    spot[longest] = (spot[longest] + 1) % dims[longest]
    return values.at[tuple(spot)].set(high)


def with_spikes(values, rng, source, target, blocks, factor):
    owner, partner = [(jnp.arange(values.shape[axis_at]) // (values.shape[axis_at] // blocks)).reshape([-1 if axis == axis_at else 1 for axis in range(values.ndim)]) for axis_at in (source, target)]
    chosen = jax.random.permutation(rng, blocks)[partner]
    strong = (owner == chosen) | (owner == (partner + blocks // 2) % blocks)
    return jnp.where(strong, factor * values, values)


def steps_of(own_key, shape, split, smallest, largest):
    def one(dim, parts):
        steps = jax.random.uniform(jax.random.fold_in(jax.random.fold_in(own_key, 6), dim), (parts,), jnp.float32, smallest / len(split), largest / len(split))
        return jnp.repeat(jnp.exp(steps), shape[dim] // parts).reshape((-1,) + (1,) * (len(shape) - dim - 1))

    loudness = one(*split[0])
    for cut in split[1:]:
        loudness = loudness * one(*cut)
    return loudness


def scatter_about(stream_key, shape, spread, bound, split=(), kind=jnp.bfloat16):
    loudness = steps_of(stream_key, shape, split, -0.22, 0.18) if split else 1.0
    array = jax.random.normal(stream_key, shape, jnp.float32) * spread * loudness
    return jnp.minimum(jnp.maximum(array, -bound), bound).astype(kind)


def heavy_noise(stream_key, extent, deviation, bound, shards, heavy, kind=jnp.bfloat16):
    entries = deviation * jax.random.normal(stream_key, extent, jnp.float32)
    if shards:
        entries = entries * steps_of(stream_key, extent, shards, -0.22, 0.18)
    return jnp.clip(with_spikes(entries, jax.random.fold_in(stream_key, 3), *heavy), -bound, bound).astype(kind)


def setup_inputs(seed: int = 0) -> dict:
    keys = jax.random.split(jax.random.key(seed), 11)
    inputs = scatter_about(keys[0], (TOKENS, D), 1.0, 6.0, ((0, 8),))
    w_qkv = scatter_about(keys[1], (3, D, HD), D ** -0.5, 0.1875, ((2, 4),))
    w_out = scatter_about(keys[2], (HD, D), HD ** -0.5, 0.1875, ((0, 4),))
    w_up = scatter_about(keys[3], (D, FF), D ** -0.5, 0.1875, ((1, 4),))
    w_down = scatter_about(keys[4], (FF, D), FF ** -0.5, 0.09375, ((0, 4),))
    norm_gains = jnp.clip(1.0 + 0.1 * jax.random.normal(keys[5], (4, D), jnp.float32), 0.5, 1.5)
    norm_biases = scatter_about(keys[6], (4, D), 0.3, 1.5, (), jnp.float32)
    out_cot = heavy_noise(keys[7], (TOKENS, D), 1.0, 6.0, ((0, 8),), (0, 1, 8, 2.0))
    group_ids = set_ends(jax.random.randint(keys[8], (TOKENS,), 0, GROUPS), jax.random.fold_in(keys[8], 1), 0, GROUPS - 1).astype(jnp.int32)
    group_weights = jnp.clip(jnp.exp(jax.random.uniform(keys[9], (GROUPS,), jnp.float32, math.log(0.25), math.log(4.0))), 0.25, 4.0)
    return dict(inputs=inputs, w_qkv=w_qkv, w_out=w_out, w_up=w_up, w_down=w_down, norm_gains=norm_gains, norm_biases=norm_biases, out_cot=out_cot, group_ids=group_ids, group_weights=group_weights)


EPS = 1e-05
HIGH = lax.Precision.HIGHEST

@jax.custom_vjp
def low(v):
    return lax.optimization_barrier(v.astype(jnp.bfloat16)).astype(jnp.float32)

@jax.custom_vjp
def low_back(v):
    return v

def low_keep(v):
    return (low(v), None)

def low_pass(kept, grad):
    return (grad,)

def back_keep(v):
    return (v, None)

def back_low(kept, grad):
    return (low(grad),)
low.defvjp(low_keep, low_pass)
low_back.defvjp(back_keep, back_low)

def layer_norm(field_in, norm_gain, norm_bias):
    row_mean = lax.optimization_barrier(jnp.mean(field_in, axis=-1, keepdims=True))
    centred = field_in - row_mean
    variance = lax.optimization_barrier(jnp.mean(centred * centred, axis=-1, keepdims=True))
    return centred * lax.rsqrt(variance + EPS) * norm_gain + norm_bias

def rotary_tables(length, head_size):
    half_size = head_size // 2
    frequency = jnp.exp(jnp.arange(half_size, dtype=jnp.float32) * (-math.log(10000.0) / half_size))
    angles = jnp.arange(length, dtype=jnp.float32)[:, None] * frequency[None, :]
    return (jnp.cos(angles)[:, None, :], jnp.sin(angles)[:, None, :])

def rotate(field_in, angle_cos, angle_sin):
    half_size = field_in.shape[-1] // 2
    first_half = field_in[..., :half_size]
    second_half = field_in[..., half_size:]
    return jnp.concatenate([first_half * angle_cos - second_half * angle_sin, second_half * angle_cos + first_half * angle_sin], axis=-1)

def attend(query, key_rows, value_rows):
    length = query.shape[0]
    block_rows = min(512, length)
    blocks = length // block_rows
    score_scale = 1.0 / math.sqrt(query.shape[-1])
    key_pos = jnp.arange(length).astype(jnp.int32)

    @jax.checkpoint
    def one_block(pair):
        query_block, row_start = pair
        scores = jnp.einsum('qhd,khd->hqk', query_block, key_rows, precision=HIGH) * score_scale
        scores = low_back(scores)
        query_pos = row_start + jnp.arange(block_rows).astype(jnp.int32)
        allowed = key_pos[None, None, :] <= query_pos[None, :, None]
        scores = jnp.where(allowed, scores, -1e+30)
        row_max = lax.optimization_barrier(jnp.max(scores, axis=-1, keepdims=True))
        exp_scores = jnp.exp(scores - row_max)
        chance_low = low(exp_scores / lax.optimization_barrier(jnp.sum(exp_scores, axis=-1, keepdims=True)))
        return jnp.einsum('hqk,khd->qhd', chance_low, value_rows, precision=HIGH)
    pieces = query.reshape(blocks, block_rows, query.shape[1], query.shape[2])
    starts = (jnp.arange(blocks) * block_rows).astype(jnp.int32)
    return lax.map(one_block, (pieces, starts)).reshape(query.shape)

def layer(seq_rows, w_qkv, w_out, w_up, w_down, norm_gains, norm_biases):
    length = seq_rows.shape[0]
    angle_cos, angle_sin = rotary_tables(length, DH)
    normed = low(layer_norm(seq_rows, norm_gains[0], norm_biases[0]))
    projected = jnp.einsum('sd,cde->cse', normed, w_qkv, precision=HIGH)
    query = low(rotate(low_back(projected[0]).reshape(length, H, DH), angle_cos, angle_sin))
    key_rows = low(rotate(low_back(projected[1]).reshape(length, H, DH), angle_cos, angle_sin))
    value_rows = low(low_back(projected[2])).reshape(length, H, DH)
    attended = low(low_back(attend(query, key_rows, value_rows).reshape(length, H * DH)))
    branch = low_back(jnp.dot(attended, w_out, precision=HIGH))
    middle = seq_rows + layer_norm(branch, norm_gains[1], norm_biases[1])
    mid_normed = low(layer_norm(middle, norm_gains[2], norm_biases[2]))
    hidden_in = low_back(jnp.dot(mid_normed, w_up, precision=HIGH))
    activated = low(jax.nn.gelu(hidden_in, approximate=True))
    branch_two = low_back(jnp.dot(activated, w_down, precision=HIGH))
    return middle + layer_norm(branch_two, norm_gains[3], norm_biases[3])

def reference(inputs, w_qkv, w_out, w_up, w_down, norm_gains, norm_biases, out_cot, group_ids, group_weights):
    sequences = inputs.shape[0] // SEQ
    weight_list = (w_qkv.astype(jnp.float32), w_out.astype(jnp.float32), w_up.astype(jnp.float32), w_down.astype(jnp.float32), norm_gains.astype(jnp.float32), norm_biases.astype(jnp.float32))
    row_weight = group_weights.astype(jnp.float32)[group_ids]
    grad_out = out_cot.astype(jnp.float32) * row_weight[:, None]
    seq_inputs = inputs.astype(jnp.float32).reshape(sequences, SEQ, D)
    seq_grads = grad_out.reshape(sequences, SEQ, D)

    def one_sequence(totals, pair):
        seq_rows, seq_grad = pair
        output, pullback = jax.vjp(layer, seq_rows, weight_list[0], weight_list[1], weight_list[2], weight_list[3], weight_list[4], weight_list[5])
        grads = pullback(seq_grad)
        totals = jax.tree.map(jnp.add, totals, tuple(grads[1:]))
        return (totals, (output.astype(jnp.bfloat16), grads[0]))
    zero_totals = tuple((jnp.zeros_like(weight) for weight in weight_list))
    totals, (outputs, input_grads) = lax.scan(one_sequence, zero_totals, (seq_inputs, seq_grads))
    return (outputs.reshape(inputs.shape[0], D), input_grads.reshape(inputs.shape[0], D), totals[0], totals[1], totals[2], totals[3], totals[4], totals[5])
```

```python
import functools
import math

import jax
import jax.numpy as jnp
from jax import lax
from jax.experimental import pallas as pl
from jax.experimental.pallas import tpu as pltpu
from jax.sharding import PartitionSpec as P

DH = 64
SEQ = 2048
EPS = 1e-05
F32 = jnp.float32
BF16 = jnp.bfloat16
LANES = 128
NT = (((1,), (1,)), ((), ()))
TN = (((0,), (0,)), ((), ()))
VMEM_LIMIT = 56 * 2**20


def cost(micros, moved):
    return pl.CostEstimate(flops=int(micros * 1.1e9), bytes_accessed=moved, transcendentals=0)


def swap(field, axis, bit):
    size = lax.axis_size(axis)
    return lax.ppermute(field, axis, [(i, i ^ bit) for i in range(size)])


def core_swap(field):
    return swap(field, "tensor", 1)


def y_swap(field):
    return swap(field, "tensor", 2)


def pick(field, index, dim):
    return lax.dynamic_index_in_dim(field, index, dim, keepdims=False)


def halve(field, axis, bit, own, dim):
    sent = pick(field, 1 - own, dim).astype(BF16)
    kept = pick(field, own, dim).astype(F32)
    return kept + swap(sent, axis, bit).astype(F32)


def sum_over_dp(blocks, order):
    size = lax.axis_size("dp")
    index = lax.axis_index("dp")
    bits = [1 << k for k in range(size.bit_length() - 1)]
    todo = [bits[k] for k in order if k < len(bits)]
    todo += [b for b in bits if b not in todo]
    left = sorted(bits, reverse=True)
    tail = blocks.shape[1:]
    field = blocks
    for step, bit in enumerate(todo):
        place = left.index(bit)
        shape = (2 ** place, 2, 2 ** (len(left) - place - 1)) + tail
        own = (index // bit) % 2
        field = halve(field.reshape(shape), "dp", bit, own, 1)
        left.remove(bit)
        if step < len(todo) - 1:
            field = field.astype(BF16)
    return field.reshape(tail)


def fetch_from_y(shard):
    rows = shard.shape[0] // 4
    mine = lax.axis_index("dp") % 4
    got = y_swap(lax.dynamic_slice_in_dim(shard, mine * rows, rows, 0))
    one = swap(got, "dp", 1)
    two = swap(got, "dp", 2)
    half = rows // 2
    three_low = swap(two[:half], "dp", 1)
    three_high = swap(one[half:], "dp", 2)
    whole = jnp.zeros(shard.shape, shard.dtype)
    for piece, which in ((got, 0), (one, 1), (two, 2)):
        whole = lax.dynamic_update_slice_in_dim(whole, piece, (mine ^ which) * rows, 0)
    whole = lax.dynamic_update_slice_in_dim(whole, three_low, (mine ^ 3) * rows, 0)
    return lax.dynamic_update_slice_in_dim(whole, three_high, (mine ^ 3) * rows + half, 0)


def normalize(field):
    mean = jnp.mean(field, axis=-1, keepdims=True)
    centred = field - mean
    inverse = lax.rsqrt(jnp.mean(centred * centred, axis=-1, keepdims=True) + EPS)
    return centred * inverse, inverse


def norm_back(grad, unit, inverse, gain):
    scaled = grad * gain
    mean_one = jnp.mean(scaled, axis=-1, keepdims=True)
    mean_two = jnp.mean(scaled * unit, axis=-1, keepdims=True)
    return inverse * (scaled - mean_one - unit * mean_two)


def rotary_tables():
    half = DH // 2
    frequency = jnp.exp(jnp.arange(half, dtype=F32) * (-math.log(10000.0) / half))
    angles = jnp.arange(SEQ, dtype=F32)[:, None] * frequency[None, :]
    cosine, sine = jnp.cos(angles), jnp.sin(angles)
    return (
        jnp.concatenate([cosine] * 4, axis=1),
        jnp.concatenate([-sine, sine, -sine, sine], axis=1),
    )


def lanes_of(shape):
    return lax.broadcasted_iota(jnp.int32, shape, 1)


def partner_lanes(field):
    lane = lanes_of(field.shape)
    return jnp.where(lane % DH < DH // 2, pltpu.roll(field, 96, 1), pltpu.roll(field, 32, 1))


def rotate(field, cosine, sine):
    return field * cosine + partner_lanes(field) * sine


def rotate_back(field, cosine, sine):
    return field * cosine - partner_lanes(field) * sine


def split_three(field):
    high = field.astype(BF16).astype(F32)
    rest = field - high
    middle = rest.astype(BF16).astype(F32)
    return high, middle, rest - middle


def project_kernel(x_ref, w_ref, gain_ref, bias_ref, cos_ref, sin_ref, n_ref, q_ref, k_ref, v_ref):
    unit, unused = normalize(x_ref[...].astype(F32))
    normed = (unit * gain_ref[...] + bias_ref[...]).astype(BF16)
    n_ref[...] = normed
    rows = normed.shape[0]
    lane = lanes_of((rows, LANES))
    ones = jnp.where(lane < DH + 3, 1.0, 0.0)
    for which, out_ref in enumerate((q_ref, k_ref, v_ref)):
        both = jnp.dot(normed, w_ref[which], preferred_element_type=F32)
        for pair in range(both.shape[1] // LANES):
            field = both[:, pair * LANES : (pair + 1) * LANES]
            if which < 2:
                field = rotate(field, cos_ref[...], sin_ref[...])
            if which == 0:
                field = field * (1.0 / math.sqrt(DH))
            extra = jnp.zeros_like(field) if which == 0 else ones
            out_ref[2 * pair] = jnp.where(lane < DH, field, extra).astype(BF16)
            out_ref[2 * pair + 1] = jnp.where(lane < DH, pltpu.roll(field, DH, 1), extra).astype(BF16)


def project(inputs, w_qkv, gain, bias, cosine, sine):
    block = 256
    tokens, width = inputs.shape
    local = w_qkv.shape[2]
    heads = local // DH
    rows = lambda i: (i, 0)
    per_head = pl.BlockSpec((heads, block, LANES), lambda i: (0, i, 0))
    headed = jax.ShapeDtypeStruct((heads, tokens, LANES), BF16)
    return pl.pallas_call(
        project_kernel,
        grid=(tokens // block,),
        in_specs=[
            pl.BlockSpec((block, width), rows),
            pl.BlockSpec((3, width, local), lambda i: (0, 0, 0)),
            pl.BlockSpec((1, width), lambda i: (0, 0)),
            pl.BlockSpec((1, width), lambda i: (0, 0)),
            pl.BlockSpec((block, LANES), rows),
            pl.BlockSpec((block, LANES), rows),
        ],
        out_specs=[pl.BlockSpec((block, width), rows), per_head, per_head, per_head],
        out_shape=[jax.ShapeDtypeStruct((tokens, width), BF16), headed, headed, headed],
        compiler_params=pltpu.CompilerParams(vmem_limit_bytes=VMEM_LIMIT),
        cost_estimate=cost(8, 18 * 2**20),
        name="project",
    )(inputs, w_qkv, gain, bias, cosine, sine)


ROWS = 512
KEYS = 256


def attend_block(n, q_ref, k_ref, v_ref, out_ref, qa_ref):
    start, end = n * ROWS, (n + 1) * ROWS
    row = lax.broadcasted_iota(jnp.int32, (LANES, ROWS), 0)
    lane = lanes_of((ROWS, LANES))
    shape = (ROWS, ROWS)
    seen = lax.broadcasted_iota(jnp.int32, shape, 0) <= lax.broadcasted_iota(jnp.int32, shape, 1)
    outs = []
    for h in range(2):
        query = q_ref[h]
        last = lax.dot_general(k_ref[h, start:end, :], query, NT, preferred_element_type=F32)
        last = jnp.where(seen, last, -1e30)
        top = jnp.max(last, axis=0, keepdims=True)
        if n:
            scores = lax.dot_general(k_ref[h, :start, :], query, NT, preferred_element_type=F32)
            top = jnp.maximum(top, jnp.max(scores, axis=0, keepdims=True))
            early = jnp.exp(scores - top).astype(BF16)
        late = jnp.exp(last - top).astype(BF16)
        total = lax.dot_general(v_ref[h, start:end, :], late, TN, preferred_element_type=F32)
        if n:
            total = total + lax.dot_general(
                v_ref[h, :start, :], early, TN, preferred_element_type=F32
            )
        summed = total[DH : DH + 1, :]
        high, middle, low = split_three(-(top + jnp.log(summed)))
        extra = jnp.where(row == DH, high, jnp.where(row == DH + 1, middle, jnp.where(row == DH + 2, low, 0.0)))
        turned = jnp.transpose(jnp.where(row < DH, total * (1.0 / summed), extra))
        qa_ref[h] = jnp.where(lane < DH, query.astype(F32), turned).astype(BF16)
        outs.append(turned)
    out_ref[...] = jnp.where(lane < DH, outs[0], pltpu.roll(outs[1], DH, 1)).astype(BF16)


def attend_kernel(*refs):
    block = pl.program_id(1)
    for n in range(SEQ // ROWS):
        pl.when(block == n)(functools.partial(attend_block, n, *refs))


def attend(query, key_rows, value_rows):
    heads = query.shape[0]
    whole = pl.BlockSpec((2, SEQ, LANES), lambda p, i: (p, 0, 0))
    part = pl.BlockSpec((2, ROWS, LANES), lambda p, i: (p, i, 0))
    return pl.pallas_call(
        attend_kernel,
        grid=(heads // 2, SEQ // ROWS),
        in_specs=[part, whole, whole],
        out_specs=[pl.BlockSpec((ROWS, LANES), lambda p, i: (i, p)), part],
        out_shape=[
            jax.ShapeDtypeStruct((SEQ, heads * DH), BF16),
            jax.ShapeDtypeStruct((heads, SEQ, LANES), BF16),
        ],
        compiler_params=pltpu.CompilerParams(vmem_limit_bytes=VMEM_LIMIT),
        cost_estimate=cost(22, 9 * 2**20),
        name="attend",
    )(query, key_rows, value_rows)


def back_block(j, k_ref, v_ref, qa_ref, cos_ref, sin_ref, dk_ref, dv_ref, da_ref, dq_ref):
    start, length = j * KEYS, SEQ - j * KEYS
    rows = slice(start, start + KEYS)
    lane = lanes_of((KEYS, LANES))
    shape = (KEYS, KEYS)
    seen = lax.broadcasted_iota(jnp.int32, shape, 0) <= lax.broadcasted_iota(jnp.int32, shape, 1)
    key_grads, value_grads = [], []
    for h in range(2):
        keys, values = k_ref[h, rows, :], v_ref[h, rows, :]
        query, grad = qa_ref[h, start:, :], da_ref[h, start:, :]
        chance = jnp.exp(lax.dot_general(keys, query, NT, preferred_element_type=F32))
        first = jnp.where(seen, chance[:, :KEYS], 0.0)
        chance = jnp.concatenate([first, chance[:, KEYS:]], axis=1) if length > KEYS else first
        chance_grad = lax.dot_general(values, grad, NT, preferred_element_type=F32)
        score_grad = (chance * chance_grad).astype(BF16)
        value_grads.append(jnp.dot(chance.astype(BF16), grad, preferred_element_type=F32))
        key_grads.append(jnp.dot(score_grad, query, preferred_element_type=F32))
        turned = lax.dot_general(keys[:, :DH], score_grad, TN, preferred_element_type=F32)
        if j == 0:
            dq_ref[h] = turned
        else:
            dq_ref[h, :, start:] += turned
    key_grad = jnp.where(lane < DH, key_grads[0], pltpu.roll(key_grads[1], DH, 1))
    dk_ref[...] = rotate_back(key_grad, cos_ref[rows, :], sin_ref[rows, :]).astype(BF16)
    dv_ref[...] = jnp.where(lane < DH, value_grads[0], pltpu.roll(value_grads[1], DH, 1)).astype(BF16)


def back_kernel(
    k_ref, v_ref, qa_ref, grad_ref, out_ref, cos_ref, sin_ref, dq_ref, dk_ref, dv_ref, da_ref, turned_ref
):
    step = pl.program_id(1)
    steps = SEQ // KEYS

    @pl.when(step == 0)
    def _():
        def prepare(i, unused):
            rows = pl.ds(pl.multiple_of(i * KEYS, KEYS), KEYS)
            lane = lanes_of((KEYS, LANES))
            grad = grad_ref[rows, :].astype(F32)
            product = grad * out_ref[rows, :].astype(F32)
            for h in range(2):
                inner = jnp.sum(jnp.where(lane // DH == h, product, 0.0), axis=1, keepdims=True)
                high, middle, low = split_three(-inner)
                own = grad if h == 0 else pltpu.roll(grad, DH, 1)
                extra = jnp.where(lane == DH, high, jnp.where(lane == DH + 1, middle, jnp.where(lane == DH + 2, low, 0.0)))
                da_ref[h, rows, :] = jnp.where(lane < DH, own, extra).astype(BF16)
            return unused

        lax.fori_loop(0, steps, prepare, 0)

    for j in range(steps):
        pl.when(step == j)(
            functools.partial(
                back_block, j, k_ref, v_ref, qa_ref, cos_ref, sin_ref, dk_ref, dv_ref, da_ref, turned_ref
            )
        )

    @pl.when(step == steps - 1)
    def _():
        for i in range(steps):
            rows = slice(i * KEYS, (i + 1) * KEYS)
            both = jnp.concatenate([turned_ref[0, :, rows], turned_ref[1, :, rows]], axis=0)
            field = jnp.transpose(both) * (1.0 / math.sqrt(DH))
            dq_ref[rows, :] = rotate_back(field, cos_ref[rows, :], sin_ref[rows, :]).astype(BF16)


def attend_back(key_rows, value_rows, query_more, grad, out, cosine, sine):
    heads = key_rows.shape[0]
    whole = pl.BlockSpec((2, SEQ, LANES), lambda p, i: (p, 0, 0))
    pair = pl.BlockSpec((SEQ, LANES), lambda p, i: (0, p))
    table = pl.BlockSpec((SEQ, LANES), lambda p, i: (0, 0))
    part = pl.BlockSpec((KEYS, LANES), lambda p, i: (i, p))
    shape = jax.ShapeDtypeStruct((SEQ, heads * DH), BF16)
    return pl.pallas_call(
        back_kernel,
        grid=(heads // 2, SEQ // KEYS),
        in_specs=[whole, whole, whole, pair, pair, table, table],
        out_specs=[pair, part, part],
        out_shape=[shape, shape, shape],
        scratch_shapes=[pltpu.VMEM((2, SEQ, LANES), BF16), pltpu.VMEM((2, DH, SEQ), F32)],
        compiler_params=pltpu.CompilerParams(vmem_limit_bytes=VMEM_LIMIT),
        cost_estimate=cost(38, 13 * 2**20),
        name="attend_back",
    )(key_rows, value_rows, query_more, grad, out, cosine, sine)


def gelu_tanh(field):
    return jax.nn.gelu(field, approximate=True)


def product(left, right):
    return jnp.dot(left, right, preferred_element_type=F32)


def product_nt(left, right):
    return lax.dot_general(left, right, NT, preferred_element_type=F32)


def product_tn(left, right):
    return lax.dot_general(left, right, TN, preferred_element_type=F32)


def per_device(
    inputs, w_qkv, w_out, w_up, w_down, norm_gains, norm_biases, out_cot, group_ids, group_weights
):
    tokens, width = inputs.shape
    half, quarter = tokens // 2, tokens // 4
    place = lax.axis_index("tensor")
    y_own, core_own = place // 2, place % 2
    dp_size = lax.axis_size("dp")
    cosine, sine = rotary_tables()

    up_y = fetch_from_y(w_up)
    down_y = fetch_from_y(w_down)
    out_y = y_swap(w_out)
    outs = [w_out, out_y, core_swap(w_out), core_swap(out_y)]
    ups = [w_up, up_y, core_swap(w_up), core_swap(up_y)]
    downs = [w_down, down_y, core_swap(w_down), core_swap(down_y)]

    normed, query, key_rows, value_rows = project(
        inputs, w_qkv, norm_gains[0:1], norm_biases[0:1], cosine, sine
    )
    attended, query_more = attend(query, key_rows, value_rows)

    by_chip = attended.reshape(2, half, -1)
    mine = pick(by_chip, y_own, 0)
    theirs = y_swap(pick(by_chip, 1 - y_own, 0))
    chip_rows = jnp.concatenate([mine, theirs], axis=1)
    by_core = chip_rows.reshape(2, quarter, -1)
    row_parts = jnp.concatenate(
        [pick(by_core, core_own, 0), core_swap(pick(by_core, 1 - core_own, 0))], axis=1
    )

    branch = product(row_parts, jnp.concatenate(outs, axis=0))
    first_in = lax.dynamic_slice_in_dim(inputs, place * quarter, quarter, 0).astype(F32)
    attn_unit, attn_inverse = normalize(branch)
    middle = first_in + attn_unit * norm_gains[1] + norm_biases[1]
    mid_unit, mid_inverse = normalize(middle)
    mid_normed = (mid_unit * norm_gains[2] + norm_biases[2]).astype(BF16)
    hidden = [product(mid_normed, w) for w in ups]
    activated = [gelu_tanh(h).astype(BF16) for h in hidden]
    branch_two = sum(product(a, w) for a, w in zip(activated, downs))
    mlp_unit, mlp_inverse = normalize(branch_two)
    final_rows = middle + mlp_unit * norm_gains[3] + norm_biases[3]

    own_ids = lax.dynamic_slice_in_dim(group_ids, place * quarter, quarter, 0)
    groups = jnp.arange(group_weights.shape[0], dtype=jnp.int32)
    lookup = (own_ids[:, None] == groups[None, :]).astype(F32)
    row_weight = jnp.sum(lookup * group_weights[None, :], axis=1)
    own_cot = lax.dynamic_slice_in_dim(out_cot, place * quarter, quarter, 0)
    grad_out = own_cot.astype(F32) * row_weight[:, None]
    mlp_branch = norm_back(grad_out, mlp_unit, mlp_inverse, norm_gains[3]).astype(BF16)
    hidden_grad = []
    for h, w in zip(hidden, downs):
        unused, pullback = jax.vjp(gelu_tanh, h)
        hidden_grad.append(pullback(product_nt(mlp_branch, w))[0].astype(BF16))
    mid_grad = sum(product_nt(h, w) for h, w in zip(hidden_grad, ups))
    state_grad = grad_out + norm_back(mid_grad, mid_unit, mid_inverse, norm_gains[2])
    branch_grad = norm_back(state_grad, attn_unit, attn_inverse, norm_gains[1]).astype(BF16)

    sibling_branch = core_swap(branch_grad)
    chip_branch = jnp.where(
        core_own == 0,
        jnp.concatenate([branch_grad, sibling_branch], axis=0),
        jnp.concatenate([sibling_branch, branch_grad], axis=0),
    )
    attended_grad_y = y_swap(product_nt(chip_branch, outs[1]).astype(BF16))
    attended_grad_own = product_nt(chip_branch, outs[0]).astype(BF16)
    attended_grad = jnp.where(
        y_own == 0,
        jnp.concatenate([attended_grad_own, attended_grad_y], axis=0),
        jnp.concatenate([attended_grad_y, attended_grad_own], axis=0),
    )

    sibling_act = [core_swap(activated[2]), core_swap(activated[3])]
    sibling_mlp = core_swap(mlp_branch)
    sibling_hidden = [core_swap(hidden_grad[2]), core_swap(hidden_grad[3])]
    sibling_mid = core_swap(mid_normed)
    down_parts = [
        product_tn(activated[i], mlp_branch) + product_tn(sibling_act[i], sibling_mlp) for i in (0, 1)
    ]
    up_parts = [
        product_tn(mid_normed, hidden_grad[i]) + product_tn(sibling_mid, sibling_hidden[i]) for i in (0, 1)
    ]
    out_parts = [product_tn(rows, chip_branch) for rows in (mine, theirs)]

    def columns(field):
        return jnp.moveaxis(field.reshape(field.shape[0], dp_size, -1), 1, 0)

    def rows_of(field):
        return field.reshape((dp_size, -1) + field.shape[1:])

    def over_y(parts):
        return (parts[0] + y_swap(parts[1].astype(BF16)).astype(F32)).astype(BF16)

    down_total = sum_over_dp(columns(over_y(down_parts)), (0, 1, 2))
    up_total = sum_over_dp(rows_of(over_y(up_parts)), (0, 1, 2))
    out_total = sum_over_dp(columns(over_y(out_parts)), (0, 1, 2))

    query_grad, key_grad, value_grad = attend_back(
        key_rows, value_rows, query_more, attended_grad, attended, cosine, sine
    )
    proj_grad = jnp.concatenate([query_grad, key_grad, value_grad], axis=1)
    w_all = jnp.concatenate([w_qkv[0], w_qkv[1], w_qkv[2]], axis=1)
    in_partial = product_nt(proj_grad, w_all)
    qkv_grad = product_tn(normed, proj_grad).astype(BF16)
    qkv_total = sum_over_dp(rows_of(qkv_grad), (0, 1, 2))
    qkv_total = jnp.moveaxis(qkv_total.reshape(-1, 3, w_qkv.shape[2]), 1, 0)

    unit_all, inverse_all = normalize(inputs.astype(F32))
    gain_zero = jnp.sum(in_partial * unit_all, axis=0)
    bias_zero = jnp.sum(in_partial, axis=0)

    by_place = in_partial.reshape(2, 2, quarter, width)
    in_rows = halve(by_place, "tensor", 1, core_own, 1)
    in_rows = halve(in_rows, "tensor", 2, y_own, 0)
    unit_in, inverse_in = normalize(first_in)
    input_grad = state_grad + norm_back(in_rows, unit_in, inverse_in, norm_gains[0])

    def over_tokens(field):
        return jnp.sum(field, axis=0)

    sums = jnp.stack(
        [
            gain_zero,
            over_tokens(state_grad * attn_unit),
            over_tokens(mid_grad * mid_unit),
            over_tokens(grad_out * mlp_unit),
            bias_zero,
            over_tokens(state_grad),
            over_tokens(mid_grad),
            over_tokens(grad_out),
        ]
    )
    sums = lax.psum_scatter(sums, ("dp", "tensor"), scatter_dimension=1, tiled=True)
    return (
        final_rows.astype(BF16),
        input_grad,
        qkv_total,
        out_total,
        up_total,
        down_total,
        sums[:4],
        sums[4:],
    )


def solution(mesh):
    placed = (
        P("dp", None),
        P(None, None, "tensor"),
        P("tensor", None),
        P(None, "tensor"),
        P("tensor", None),
        P(),
        P(),
        P("dp", None),
        P("dp"),
        P(),
    )
    return jax.shard_map(
        per_device,
        mesh=mesh,
        in_specs=placed,
        out_specs=(
            P(("dp", "tensor"), None),
            P(("dp", "tensor"), None),
            P(None, "dp", "tensor"),
            P("tensor", "dp"),
            P("dp", "tensor"),
            P("tensor", "dp"),
            P(None, ("dp", "tensor")),
            P(None, ("dp", "tensor")),
        ),
        check_vma=False,
    )
```

```python
import functools
import math

import jax
import jax.numpy as jnp
import numpy as np
from jax import lax
from jax.experimental import pallas as pl
from jax.experimental.pallas import tpu as pltpu
from jax.sharding import PartitionSpec as P

DH = 64
SEQ = 2048
EPS = 1e-05
F32 = jnp.float32
BF16 = jnp.bfloat16
LANES = 128
NT = (((1,), (1,)), ((), ()))
TN = (((0,), (0,)), ((), ()))
VMEM_LIMIT = 56 * 2**20
ANY = pl.BlockSpec(memory_space=pl.ANY)


def params():
    return pltpu.CompilerParams(vmem_limit_bytes=VMEM_LIMIT)


def cost(micros, moved=2**20):
    return pl.CostEstimate(flops=int(micros * 1.1e9), bytes_accessed=moved, transcendentals=0)


def shaped(shape, kind):
    return jax.ShapeDtypeStruct(shape, kind)


def fixed(shape):
    return pl.BlockSpec(shape, lambda *unused: (0,) * len(shape))


def swap(field, axis, bit):
    size = lax.axis_size(axis)
    return lax.ppermute(field, axis, [(i, i ^ bit) for i in range(size)])


def core_swap(field):
    return swap(field, "tensor", 1)


def y_swap(field):
    return swap(field, "tensor", 2)


def pick(field, index, dim):
    return lax.dynamic_index_in_dim(field, index, dim, keepdims=False)


def total(addends):
    return sum(a.astype(F32) for a in addends)


class Blocks:
    def __init__(self, addends):
        size = lax.axis_size("dp")
        self.left = [1 << k for k in reversed(range(size.bit_length() - 1))]
        self.tail = (addends[0].shape[0] // size,) + addends[0].shape[1:]
        self.addends = [a.reshape((size,) + self.tail) for a in addends]

    def view(self, bit):
        place = self.left.index(bit)
        shape = (2**place, 2, 2 ** (len(self.left) - place - 1)) + self.tail
        return [a.reshape(shape) for a in self.addends]

    def halve(self, number):
        bit = 1 << number
        own = (lax.axis_index("dp") // bit) % 2
        views = self.view(bit)
        sent = total([pick(a, 1 - own, 1) for a in views]).astype(BF16)
        self.addends = [pick(a, own, 1) for a in views] + [swap(sent, "dp", bit)]
        self.left.remove(bit)

    def rest(self, order):
        for number in order:
            if 1 << number in self.left:
                self.halve(number)
        while self.left:
            self.halve(self.left[-1].bit_length() - 1)
        return total(self.addends).reshape(self.tail)


def sum_y_first(own, other, order):
    return Blocks([own, y_swap(other)]).rest(order)


def sum_y_second(own, other, first, order):
    own, other = Blocks([own]), Blocks([other])
    other.halve(first)
    own.halve(first)
    own.addends = own.addends + [y_swap(total(other.addends).astype(BF16))]
    return own.rest(order)


def fetch_from_y(shard):
    rows = shard.shape[0] // 4
    mine = lax.axis_index("dp") % 4
    got = y_swap(lax.dynamic_slice_in_dim(shard, mine * rows, rows, 0))
    one = swap(got, "dp", 1)
    two = swap(got, "dp", 2)
    half = rows // 2
    three_low = swap(two[:half], "dp", 1)
    three_high = swap(one[half:], "dp", 2)
    whole = jnp.zeros(shard.shape, shard.dtype)
    for piece, which in ((got, 0), (one, 1), (two, 2)):
        whole = lax.dynamic_update_slice_in_dim(whole, piece, (mine ^ which) * rows, 0)
    whole = lax.dynamic_update_slice_in_dim(whole, three_low, (mine ^ 3) * rows, 0)
    whole = lax.dynamic_update_slice_in_dim(whole, three_high, (mine ^ 3) * rows + half, 0)
    return whole, got


def normalize(field):
    mean = jnp.mean(field, axis=-1, keepdims=True)
    centred = field - mean
    inverse = lax.rsqrt(jnp.mean(centred * centred, axis=-1, keepdims=True) + EPS)
    return centred * inverse, inverse


def norm_back(grad, unit, inverse, gain):
    scaled = grad * gain
    mean_one = jnp.mean(scaled, axis=-1, keepdims=True)
    mean_two = jnp.mean(scaled * unit, axis=-1, keepdims=True)
    return inverse * (scaled - mean_one - unit * mean_two)


def rotary_tables():
    half = DH // 2
    frequency = np.exp(np.arange(half, dtype=np.float32) * np.float32(-math.log(10000.0) / half))
    angles = np.arange(SEQ, dtype=np.float32)[:, None] * frequency.astype(np.float32)[None, :]
    cosine, sine = np.cos(angles), np.sin(angles)
    return (
        jnp.asarray(np.concatenate([cosine] * 4, axis=1).astype(np.float32)),
        jnp.asarray(np.concatenate([-sine, sine, -sine, sine], axis=1).astype(np.float32)),
    )


def lanes_of(shape):
    return lax.broadcasted_iota(jnp.int32, shape, 1)


def partner_lanes(field):
    lane = lanes_of(field.shape)
    return jnp.where(lane % DH < DH // 2, pltpu.roll(field, 96, 1), pltpu.roll(field, 32, 1))


def rotate(field, cosine, sine):
    return field * cosine + partner_lanes(field) * sine


def rotate_back(field, cosine, sine):
    return field * cosine - partner_lanes(field) * sine


def split_three(field):
    high = field.astype(BF16).astype(F32)
    rest = field - high
    middle = rest.astype(BF16).astype(F32)
    return high, middle, rest - middle


def product(left, right):
    return jnp.dot(left, right, preferred_element_type=F32)


def product_nt(left, right):
    return lax.dot_general(left, right, NT, preferred_element_type=F32)


def column_sum(field):
    return jnp.sum(field, axis=0, keepdims=True)


def project_kernel(x_ref, w_ref, gain_ref, bias_ref, cos_ref, sin_ref, n_ref, q_ref, k_ref, v_ref):
    unit, unused = normalize(x_ref[...].astype(F32))
    normed = unit * gain_ref[...] + bias_ref[...]
    n_ref[...] = jnp.transpose(normed).astype(BF16)
    normed = normed.astype(BF16)
    rows = normed.shape[0]
    lane = lanes_of((rows, LANES))
    ones = jnp.where(lane < DH + 3, 1.0, 0.0)
    for which, out_ref in enumerate((q_ref, k_ref, v_ref)):
        both = product(normed, w_ref[which])
        for pair in range(both.shape[1] // LANES):
            field = both[:, pair * LANES : (pair + 1) * LANES]
            if which < 2:
                field = rotate(field, cos_ref[...], sin_ref[...])
            if which == 0:
                field = field * (1.0 / math.sqrt(DH))
            extra = jnp.zeros_like(field) if which == 0 else ones
            out_ref[2 * pair] = jnp.where(lane < DH, field, extra).astype(BF16)
            out_ref[2 * pair + 1] = jnp.where(lane < DH, pltpu.roll(field, DH, 1), extra).astype(BF16)


def project(inputs, w_qkv, gain, bias, cosine, sine):
    block = 256
    tokens, width = inputs.shape
    local = w_qkv.shape[2]
    heads = local // DH
    rows = lambda i: (i, 0)
    per_head = pl.BlockSpec((heads, block, LANES), lambda i: (0, i, 0))
    headed = shaped((heads, tokens, LANES), BF16)
    return pl.pallas_call(
        project_kernel,
        grid=(tokens // block,),
        in_specs=[
            pl.BlockSpec((block, width), rows),
            fixed((3, width, local)),
            fixed((1, width)),
            fixed((1, width)),
            pl.BlockSpec((block, LANES), rows),
            pl.BlockSpec((block, LANES), rows),
        ],
        out_specs=[pl.BlockSpec((width, block), lambda i: (0, i)), per_head, per_head, per_head],
        out_shape=[shaped((width, tokens), BF16), headed, headed, headed],
        compiler_params=params(),
        cost_estimate=cost(10),
        name="project",
    )(inputs, w_qkv, gain, bias, cosine, sine)


ROWS = 512
KEYS = 256


def attend_block(n, q_ref, k_ref, v_ref, out_ref, qa_ref):
    start, end = n * ROWS, (n + 1) * ROWS
    row = lax.broadcasted_iota(jnp.int32, (LANES, ROWS), 0)
    lane = lanes_of((ROWS, LANES))
    shape = (ROWS, ROWS)
    seen = lax.broadcasted_iota(jnp.int32, shape, 0) <= lax.broadcasted_iota(jnp.int32, shape, 1)
    outs = []
    for h in range(2):
        query = q_ref[h]
        last = lax.dot_general(k_ref[h, start:end, :], query, NT, preferred_element_type=F32)
        last = jnp.where(seen, last, -1e30)
        top = jnp.max(last, axis=0, keepdims=True)
        if n:
            scores = lax.dot_general(k_ref[h, :start, :], query, NT, preferred_element_type=F32)
            top = jnp.maximum(top, jnp.max(scores, axis=0, keepdims=True))
            early = jnp.exp(scores - top).astype(BF16)
        late = jnp.exp(last - top).astype(BF16)
        both = lax.dot_general(v_ref[h, start:end, :], late, TN, preferred_element_type=F32)
        if n:
            both = both + lax.dot_general(v_ref[h, :start, :], early, TN, preferred_element_type=F32)
        summed = both[DH : DH + 1, :]
        high, middle, low = split_three(-(top + jnp.log(summed)))
        extra = jnp.where(row == DH + 1, middle, jnp.where(row == DH + 2, low, 0.0))
        extra = jnp.where(row == DH, high, extra)
        turned = jnp.transpose(jnp.where(row < DH, both * (1.0 / summed), extra))
        qa_ref[h] = jnp.where(lane < DH, query.astype(F32), turned).astype(BF16)
        outs.append(turned)
    out_ref[...] = jnp.where(lane < DH, outs[0], pltpu.roll(outs[1], DH, 1)).astype(BF16)


def attend_kernel(*refs):
    block = pl.program_id(0)
    for n in range(SEQ // ROWS):
        pl.when(block == n)(functools.partial(attend_block, n, *refs[:3], *refs[-2:]))


def attend(pair, query, key_rows, value_rows, *deps):
    whole = pl.BlockSpec((2, SEQ, LANES), lambda i: (pair, 0, 0))
    return pl.pallas_call(
        attend_kernel,
        grid=(SEQ // ROWS,),
        in_specs=[pl.BlockSpec((2, ROWS, LANES), lambda i: (pair, i, 0)), whole, whole] + [ANY] * len(deps),
        out_specs=[
            pl.BlockSpec((ROWS, LANES), lambda i: (i, 0)),
            pl.BlockSpec((2, ROWS, LANES), lambda i: (0, i, 0)),
        ],
        out_shape=[shaped((SEQ, LANES), BF16), shaped((2, SEQ, LANES), BF16)],
        compiler_params=params(),
        cost_estimate=cost(11),
        name="attend",
    )(query, key_rows, value_rows, *deps)


def back_block(j, k_ref, v_ref, qa_ref, cos_ref, sin_ref, pg_ref, da_ref, dq_ref):
    start, length = j * KEYS, SEQ - j * KEYS
    rows = slice(start, start + KEYS)
    lane = lanes_of((KEYS, LANES))
    shape = (KEYS, KEYS)
    seen = lax.broadcasted_iota(jnp.int32, shape, 0) <= lax.broadcasted_iota(jnp.int32, shape, 1)
    key_grads, value_grads = [], []
    for h in range(2):
        keys, values = k_ref[h, rows, :], v_ref[h, rows, :]
        query, grad = qa_ref[h, start:, :], da_ref[h, start:, :]
        chance = jnp.exp(product_nt(keys, query))
        first = jnp.where(seen, chance[:, :KEYS], 0.0)
        chance = jnp.concatenate([first, chance[:, KEYS:]], axis=1) if length > KEYS else first
        score_grad = (chance * product_nt(values, grad)).astype(BF16)
        value_grads.append(product(chance.astype(BF16), grad))
        key_grads.append(product(score_grad, query))
        turned = lax.dot_general(keys[:, :DH], score_grad, TN, preferred_element_type=F32)
        if j == 0:
            dq_ref[h] = turned
        else:
            dq_ref[h, :, start:] += turned
    key_grad = jnp.where(lane < DH, key_grads[0], pltpu.roll(key_grads[1], DH, 1))
    value_grad = jnp.where(lane < DH, value_grads[0], pltpu.roll(value_grads[1], DH, 1))
    pg_ref[rows, LANES : 2 * LANES] = rotate_back(key_grad, cos_ref[rows, :], sin_ref[rows, :]).astype(BF16)
    pg_ref[rows, 2 * LANES :] = value_grad.astype(BF16)


def back_kernel(
    place_ref, k_ref, v_ref, qa_ref, g0, g1, g2, g3, out_ref, cos_ref, sin_ref, pg_ref, da_ref, turned_ref
):
    step = pl.program_id(0)
    steps = SEQ // KEYS

    @pl.when(step == 0)
    def _():
        lane = lanes_of((KEYS, LANES))
        for which, grad_ref in enumerate((g0, g1, g2, g3)):
            begin = (place_ref[0] ^ which) * (SEQ // 4)
            for i in range(SEQ // 4 // KEYS):
                rows = pl.ds(pl.multiple_of(begin + i * KEYS, KEYS), KEYS)
                grad = grad_ref[i * KEYS : (i + 1) * KEYS, :].astype(F32)
                both = grad * out_ref[rows, :].astype(F32)
                for h in range(2):
                    inner = jnp.sum(jnp.where(lane // DH == h, both, 0.0), axis=1, keepdims=True)
                    high, middle, low = split_three(-inner)
                    own = grad if h == 0 else pltpu.roll(grad, DH, 1)
                    extra = jnp.where(lane == DH + 1, middle, jnp.where(lane == DH + 2, low, 0.0))
                    extra = jnp.where(lane == DH, high, extra)
                    da_ref[h, rows, :] = jnp.where(lane < DH, own, extra).astype(BF16)

    for j in range(steps):
        pl.when(step == j)(
            functools.partial(back_block, j, k_ref, v_ref, qa_ref, cos_ref, sin_ref, pg_ref, da_ref, turned_ref)
        )

    @pl.when(step == steps - 1)
    def _():
        for i in range(steps):
            rows = slice(i * KEYS, (i + 1) * KEYS)
            both = jnp.concatenate([turned_ref[0, :, rows], turned_ref[1, :, rows]], axis=0)
            field = jnp.transpose(both) * (1.0 / math.sqrt(DH))
            pg_ref[rows, :LANES] = rotate_back(field, cos_ref[rows, :], sin_ref[rows, :]).astype(BF16)


def attend_back(pair, place, key_rows, value_rows, query_more, grads, out, cosine, sine):
    whole = pl.BlockSpec((2, SEQ, LANES), lambda i, s: (pair, 0, 0))
    grad_specs = [
        pl.BlockSpec((SEQ // 4, LANES), (lambda i, s: (0, pair)) if g.shape[1] > LANES else (lambda i, s: (0, 0)))
        for g in grads
    ]
    table = fixed((SEQ, LANES))
    return pl.pallas_call(
        back_kernel,
        grid_spec=pltpu.PrefetchScalarGridSpec(
            num_scalar_prefetch=1,
            grid=(SEQ // KEYS,),
            in_specs=[whole, whole, fixed((2, SEQ, LANES))] + grad_specs + [table, table, table],
            out_specs=fixed((SEQ, 3 * LANES)),
            scratch_shapes=[pltpu.VMEM((2, SEQ, LANES), BF16), pltpu.VMEM((2, DH, SEQ), F32)],
        ),
        out_shape=shaped((SEQ, 3 * LANES), BF16),
        compiler_params=params(),
        cost_estimate=cost(19),
        name="attend_back",
    )(place, key_rows, value_rows, query_more, *grads, out, cosine, sine)


CHUNK = 512
PARTS = 128
SCALE = math.sqrt(2.0 / math.pi)
CUBIC = 0.044715


def piece_specs(shape, axis, steps):
    def one(k):
        def index(s, *unused):
            at = jnp.clip(s - k * steps, 0, steps - 1)
            return (at, 0) if axis == 0 else (0, at)

        return pl.BlockSpec(shape, index)

    return [one(k) for k in range(4)]


def up_kernel(place_ref, *refs):
    own, more = refs[:4], refs[4:8]
    outs, x_ref, gain_ref, bias_ref, ups = refs[8:12], refs[12], refs[13], refs[14], refs[15:19]
    mid_ref, aunit_ref, munit_ref, ainv_ref, minv_ref, mn_ref, sib_ref, act_ref, gp_ref = refs[19:]
    step = pl.program_id(0)

    @pl.when(step == 0)
    def _():
        for i in range(x_ref.shape[0] // PARTS):
            rows = slice(i * PARTS, (i + 1) * PARTS)
            branch = None
            for k, w_ref in enumerate(outs):
                pair = (own + more)[2 * k : 2 * k + 2]
                left = jnp.concatenate([pair[0][rows, :], pair[1][rows, :]], axis=1)
                term = product(left, w_ref[...])
                branch = term if branch is None else branch + term
            aunit, ainv = normalize(branch)
            middle = x_ref[rows, :].astype(F32) + aunit * gain_ref[1:2, :] + bias_ref[1:2, :]
            munit, minv = normalize(middle)
            mid_ref[rows, :] = middle
            aunit_ref[rows, :] = aunit
            munit_ref[rows, :] = munit
            ainv_ref[rows, :] = jnp.broadcast_to(ainv, (PARTS, LANES))
            minv_ref[rows, :] = jnp.broadcast_to(minv, (PARTS, LANES))
            mn_ref[rows, :] = (munit * gain_ref[2:3, :] + bias_ref[2:3, :]).astype(BF16)

    for k, w_ref in enumerate(ups):

        @pl.when(step // 2 == k)
        def _(w_ref=w_ref, out_ref=(sib_ref, act_ref)[k // 2]):
            for i in range(mn_ref.shape[0] // PARTS):
                rows = slice(i * PARTS, (i + 1) * PARTS)
                value = product(mn_ref[rows, :], w_ref[...])
                square = value * value
                bent = jnp.tanh(SCALE * value * (1.0 + CUBIC * square))
                half = 0.5 + 0.5 * bent
                out_ref[rows, :] = (value * half).astype(BF16)
                slope = half + (0.5 * SCALE) * value * (1.0 - bent * bent) * (1.0 + 3.0 * CUBIC * square)
                gp_ref[rows, :] = slope.astype(BF16)


def feed_up(place, own_pairs, their_pairs, sib_own, sib_their, outs, inputs, gains, biases, ups):
    width = inputs.shape[1]
    quarter = inputs.shape[0] // 4
    in_place = lambda s, t: (t[0], 0)
    in_core = lambda s, t: (t[0] % 2, 0)
    heads = pl.BlockSpec((quarter, LANES), in_place)
    full = lambda kind: shaped((quarter, width), kind)
    hid = 2 * width
    return pl.pallas_call(
        up_kernel,
        grid_spec=pltpu.PrefetchScalarGridSpec(
            num_scalar_prefetch=1,
            grid=(2 * hid // CHUNK,),
            in_specs=[heads, heads]
            + [pl.BlockSpec((quarter, LANES), in_core)] * 2
            + [fixed((quarter, LANES))] * 4
            + [fixed(outs[0].shape)] * 4
            + [pl.BlockSpec((quarter, width), in_place), fixed((4, width)), fixed((4, width))]
            + piece_specs((width, CHUNK), 1, width // CHUNK),
            out_specs=[fixed((quarter, width))] * 3
            + [fixed((quarter, LANES))] * 2
            + [fixed((quarter, width))]
            + [
                pl.BlockSpec((quarter, CHUNK), lambda s, t: (0, jnp.minimum(s, 3))),
                pl.BlockSpec((quarter, CHUNK), lambda s, t: (0, jnp.maximum(s - 4, 0))),
                pl.BlockSpec((quarter, CHUNK), lambda s, t: (0, s)),
            ],
        ),
        out_shape=[full(F32)] * 3
        + [shaped((quarter, LANES), F32)] * 2
        + [full(BF16)]
        + [shaped((quarter, hid), BF16)] * 2
        + [shaped((quarter, 2 * hid), BF16)],
        compiler_params=params(),
        cost_estimate=cost(10),
        name="feed_up",
    )(place, *own_pairs, *their_pairs, *sib_own, *sib_their, *outs, inputs, gains, biases, *ups)


def down_kernel(place_ref, sib_ref, act_ref, d0, d1, d2, d3, mid_ref, gain_ref, bias_ref, cot_ref, weight_ref,
                out_ref, grad_ref, sum_ref, acc_ref):
    step = pl.program_id(0)
    steps = pl.num_programs(0)

    for k, w_ref in enumerate((d0, d1, d2, d3)):
        left = (sib_ref, act_ref)[k // 2]
        if k == 0:

            @pl.when(step == 0)
            def _(w_ref=w_ref, left=left):
                acc_ref[...] = product(left[...], w_ref[...])

        @pl.when((step // 2 == k) & (step > 0))
        def _(w_ref=w_ref, left=left):
            acc_ref[...] += product(left[...], w_ref[...])

    @pl.when(step == steps - 1)
    def _():
        gain_sum = bias_sum = 0.0
        for i in range(acc_ref.shape[0] // PARTS):
            rows = slice(i * PARTS, (i + 1) * PARTS)
            unit, inverse = normalize(acc_ref[rows, :])
            out_ref[rows, :] = (mid_ref[rows, :] + unit * gain_ref[3:4, :] + bias_ref[3:4, :]).astype(BF16)
            grad = cot_ref[rows, :].astype(F32) * weight_ref[rows, :1]
            gain_sum = gain_sum + column_sum(grad * unit)
            bias_sum = bias_sum + column_sum(grad)
            grad_ref[rows, :] = norm_back(grad, unit, inverse, gain_ref[3:4, :]).astype(BF16)
        sum_ref[0:1, :] = gain_sum
        sum_ref[1:2, :] = bias_sum


def feed_down(place, sib_act, own_act, downs, middle, gains, biases, cot, weight):
    quarter, width = middle.shape
    hid = sib_act.shape[1]
    return pl.pallas_call(
        down_kernel,
        grid_spec=pltpu.PrefetchScalarGridSpec(
            num_scalar_prefetch=1,
            grid=(2 * hid // CHUNK,),
            in_specs=[
                pl.BlockSpec((quarter, CHUNK), lambda s, t: (0, jnp.minimum(s, 3))),
                pl.BlockSpec((quarter, CHUNK), lambda s, t: (0, jnp.maximum(s - 4, 0))),
            ]
            + piece_specs((CHUNK, width), 0, width // CHUNK)
            + [fixed((quarter, width)), fixed((4, width)), fixed((4, width))]
            + [pl.BlockSpec((quarter, width), lambda s, t: (t[0], 0)), fixed((quarter, LANES))],
            out_specs=[fixed((quarter, width)), fixed((quarter, width)), fixed((2, width))],
            scratch_shapes=[pltpu.VMEM((quarter, width), F32)],
        ),
        out_shape=[shaped((quarter, width), BF16), shaped((quarter, width), BF16), shaped((2, width), F32)],
        compiler_params=params(),
        cost_estimate=cost(9),
        name="feed_down",
    )(place, sib_act, own_act, *downs, middle, gains, biases, cot, weight)


def feed_back_kernel(place_ref, grad_ref, gp_ref, d0, d1, d2, d3, u0, u1, u2, u3, munit_ref, minv_ref, aunit_ref,
                     ainv_ref, cot_ref, weight_ref, gain_ref, wa, wb, wc, wd,
                     sib_ref, own_ref, branch_ref, state_ref, sum_ref, ga, gb, gc, gd, acc_ref):
    step = pl.program_id(0)
    steps = pl.num_programs(0)

    @pl.when(step == 0)
    def _():
        acc_ref[...] = jnp.zeros_like(acc_ref)

    for k, (down_ref, up_ref) in enumerate(((d0, u0), (d1, u1), (d2, u2), (d3, u3))):

        @pl.when(step // 2 == k)
        def _(down_ref=down_ref, up_ref=up_ref, out_ref=(sib_ref, own_ref)[k // 2]):
            hidden = (gp_ref[...].astype(F32) * product_nt(grad_ref[...], down_ref[...])).astype(BF16)
            out_ref[...] = hidden
            acc_ref[...] += product_nt(hidden, up_ref[...])

    @pl.when(step == steps - 1)
    def _():
        sums = [0.0] * 4
        for i in range(acc_ref.shape[0] // PARTS):
            rows = slice(i * PARTS, (i + 1) * PARTS)
            mid_grad, munit, aunit = acc_ref[rows, :], munit_ref[rows, :], aunit_ref[rows, :]
            grad = cot_ref[rows, :].astype(F32) * weight_ref[rows, :1]
            state = grad + norm_back(mid_grad, munit, minv_ref[rows, :1], gain_ref[2:3, :])
            branch = norm_back(state, aunit, ainv_ref[rows, :1], gain_ref[1:2, :]).astype(BF16)
            state_ref[rows, :] = state
            branch_ref[rows, :] = branch
            terms = (state * aunit, mid_grad * munit, state, mid_grad)
            sums = [s + column_sum(t) for s, t in zip(sums, terms)]
        for k, value in enumerate(sums):
            sum_ref[k : k + 1, :] = value
        for w_ref, out_ref in ((wb, gb), (wc, gc), (wd, gd), (wa, ga)):
            out_ref[...] = product_nt(branch_ref[...], w_ref[...]).astype(BF16)


def feed_back(place, grad, slopes, downs, ups, munit, minv, aunit, ainv, cot, weight, gains, outs):
    quarter, width = grad.shape
    hid = slopes.shape[1] // 2
    local = outs[0].shape[0]
    rows = fixed((quarter, width))
    stat = fixed((quarter, LANES))
    return pl.pallas_call(
        feed_back_kernel,
        grid_spec=pltpu.PrefetchScalarGridSpec(
            num_scalar_prefetch=1,
            grid=(2 * hid // CHUNK,),
            in_specs=[rows, pl.BlockSpec((quarter, CHUNK), lambda s, t: (0, s))]
            + piece_specs((CHUNK, width), 0, width // CHUNK)
            + piece_specs((width, CHUNK), 1, width // CHUNK)
            + [rows, stat, rows, stat, pl.BlockSpec((quarter, width), lambda s, t: (t[0], 0)), stat]
            + [fixed((4, width))]
            + [fixed(outs[0].shape)] * 4,
            out_specs=[
                pl.BlockSpec((quarter, CHUNK), lambda s, t: (0, jnp.minimum(s, 3))),
                pl.BlockSpec((quarter, CHUNK), lambda s, t: (0, jnp.maximum(s - 4, 0))),
                rows,
                rows,
                fixed((4, width)),
            ]
            + [fixed((quarter, local))] * 4,
            scratch_shapes=[pltpu.VMEM((quarter, width), F32)],
        ),
        out_shape=[shaped((quarter, hid), BF16)] * 2
        + [shaped((quarter, width), BF16), shaped((quarter, width), F32), shaped((4, width), F32)]
        + [shaped((quarter, local), BF16)] * 4,
        compiler_params=params(),
        cost_estimate=cost(16),
        name="feed_back",
    )(place, grad, slopes, *downs, *ups, munit, minv, aunit, ainv, cot, weight, gains, *outs)


def turn_rows(x_refs, turned_ref):
    begin = 0
    for x_ref in x_refs:
        rows, width = x_ref.shape
        for i in range(width // 256):
            cut = slice(i * 256, (i + 1) * 256)
            turned_ref[cut, begin : begin + rows] = jnp.transpose(x_ref[:, cut])
        begin += rows


def weight_kernel(x1, x2, y1, y2, own_ref, other_ref, turned_ref):
    step = pl.program_id(0)
    rows = x1.shape[0]

    @pl.when(step == 0)
    def _():
        turn_rows((x1, x2), turned_ref)

    for k, out_ref in enumerate((other_ref, own_ref)):

        @pl.when(step // 2 == k)
        def _(out_ref=out_ref):
            field = product(turned_ref[:, :rows], y1[...]) + product(turned_ref[:, rows:], y2[...])
            out_ref[...] = field.astype(BF16)


def weight_grad(x1, x2, y1, y2, name):
    rows, width = x1.shape
    hid = y1.shape[1] // 2
    steps = hid // CHUNK
    y_spec = pl.BlockSpec((rows, CHUNK), lambda s: (0, (s + steps) % (2 * steps)))
    return pl.pallas_call(
        weight_kernel,
        grid=(2 * steps,),
        in_specs=[fixed((rows, width))] * 2 + [y_spec] * 2,
        out_specs=[
            pl.BlockSpec((width, CHUNK), lambda s: (0, jnp.maximum(s - steps, 0))),
            pl.BlockSpec((width, CHUNK), lambda s: (0, jnp.minimum(s, steps - 1))),
        ],
        out_shape=[shaped((width, hid), BF16)] * 2,
        scratch_shapes=[pltpu.VMEM((width, 2 * rows), BF16)],
        compiler_params=params(),
        cost_estimate=cost(6),
        name=name,
    )(x1, x2, y1, y2)


def out_weight_kernel(place_ref, x1, x2, a0, a1, t0, t1, b0, b1, s0, s1, own_ref, other_ref, turned_ref):
    rows = x1.shape[0]
    turn_rows((x1, x2), turned_ref)
    for out_ref, mine, sibs in ((own_ref, (a0, a1), (b0, b1)), (other_ref, (t0, t1), (s0, s1))):
        left = jnp.concatenate([mine[0][...], mine[1][...]], axis=1)
        right = jnp.concatenate([sibs[0][...], sibs[1][...]], axis=1)
        field = product(turned_ref[:, :rows], left) + product(turned_ref[:, rows:], right)
        out_ref[...] = field.astype(BF16)


def out_weight_grad(place, branch, sibling, own_pairs, their_pairs):
    rows, width = branch.shape
    block = lambda index: pl.BlockSpec((rows, LANES), index)
    mine = [block(lambda s, t: (t[0], 0))] * 2 + [block(lambda s, t: (t[0] % 2, 0))] * 2
    sibs = [block(lambda s, t: (t[0] ^ 1, 0))] * 2 + [block(lambda s, t: (1 - t[0] % 2, 0))] * 2
    return pl.pallas_call(
        out_weight_kernel,
        grid_spec=pltpu.PrefetchScalarGridSpec(
            num_scalar_prefetch=1,
            grid=(1,),
            in_specs=[fixed((rows, width))] * 2 + mine + sibs,
            out_specs=[fixed((width, 2 * LANES))] * 2,
            scratch_shapes=[pltpu.VMEM((width, 2 * rows), BF16)],
        ),
        out_shape=[shaped((width, 2 * LANES), BF16)] * 2,
        compiler_params=params(),
        cost_estimate=cost(4),
        name="out_weight_grad",
    )(place, branch, sibling, *own_pairs, *their_pairs, *own_pairs, *their_pairs)


def in_back_kernel(order_ref, p0, p1, w_ref, x_ref, send_ref, keep_ref, sum_ref):
    step = pl.program_id(0)
    field = None
    for c in range(3):
        cut = slice(c * LANES, (c + 1) * LANES)
        left = jnp.concatenate([p0[:, cut], p1[:, cut]], axis=1)
        term = product_nt(left, w_ref[c])
        field = term if field is None else field + term

    @pl.when(step < 2)
    def _():
        send_ref[...] = field.astype(BF16)

    @pl.when(step >= 2)
    def _():
        keep_ref[...] = field.astype(BF16)

    @pl.when(step == 0)
    def _():
        sum_ref[...] = jnp.zeros_like(sum_ref)

    unit, unused = normalize(x_ref[...].astype(F32))
    sum_ref[0:1, :] += column_sum(field * unit)
    sum_ref[1:2, :] += column_sum(field)


def in_back(sibling_place, own_place, parts, w_qkv, inputs):
    block = 256
    width = inputs.shape[1]
    order = jnp.stack([2 * sibling_place, 2 * sibling_place + 1, 2 * own_place, 2 * own_place + 1])
    rows = lambda s, o: (o[s], 0)
    return pl.pallas_call(
        in_back_kernel,
        grid_spec=pltpu.PrefetchScalarGridSpec(
            num_scalar_prefetch=1,
            grid=(4,),
            in_specs=[pl.BlockSpec((block, 3 * LANES), rows)] * 2
            + [fixed(w_qkv.shape), pl.BlockSpec((block, width), rows)],
            out_specs=[
                pl.BlockSpec((block, width), lambda s, o: (jnp.minimum(s, 1), 0)),
                pl.BlockSpec((block, width), lambda s, o: (jnp.maximum(s - 2, 0), 0)),
                fixed((2, width)),
            ],
        ),
        out_shape=[shaped((2 * block, width), BF16)] * 2 + [shaped((2, width), F32)],
        compiler_params=params(),
        cost_estimate=cost(4),
        name="in_back",
    )(order.astype(jnp.int32), *parts, w_qkv, inputs)


def per_device(
    inputs, w_qkv, w_out, w_up, w_down, norm_gains, norm_biases, out_cot, group_ids, group_weights
):
    tokens, width = inputs.shape
    half, quarter = tokens // 2, tokens // 4
    place = lax.axis_index("tensor")
    y_own, core_own = place // 2, place % 2
    where = place.astype(jnp.int32).reshape(1)
    dp_size = lax.axis_size("dp")
    cosine, sine = rotary_tables()

    up_y, up_first = fetch_from_y(w_up)
    down_y, unused = fetch_from_y(w_down)
    out_y = y_swap(w_out)
    out_all = [w_out, out_y, core_swap(w_out), core_swap(out_y)]
    up_all = [core_swap(w_up), core_swap(up_y), w_up, up_y]
    down_all = [core_swap(w_down), core_swap(down_y), w_down, down_y]

    own_ids = lax.dynamic_slice_in_dim(group_ids, place * quarter, quarter, 0)
    groups = jnp.arange(group_weights.shape[0], dtype=jnp.int32)
    lookup = (own_ids[:, None] == groups[None, :]).astype(F32)
    row_weight = jnp.sum(lookup * group_weights[None, :], axis=1, keepdims=True)
    row_weight = jnp.broadcast_to(row_weight, (quarter, LANES))

    normed_turned, query, key_rows, value_rows = project(
        inputs, w_qkv, norm_gains[0:1], norm_biases[0:1], cosine, sine
    )

    attended, query_more, theirs, sib_own, sib_theirs = [], [], [], [], []
    for pair in range(2):
        out, more = attend(pair, query, key_rows, value_rows)
        by_quarter = out.reshape(2, 2, quarter, LANES)
        other = y_swap(pick(out.reshape(2, half, LANES), 1 - y_own, 0))
        sib_own.append(core_swap(pick(pick(by_quarter, y_own, 0), 1 - core_own, 0)))
        sib_theirs.append(core_swap(pick(other.reshape(2, quarter, LANES), 1 - core_own, 0)))
        attended.append(out)
        query_more.append(more)
        theirs.append(other)

    middle, aunit, munit, ainv, minv, mid_normed, sib_act, own_act, slopes = feed_up(
        where, attended, theirs, sib_own, sib_theirs,
        [out_all[0], out_all[1], out_all[2], out_all[3]], inputs, norm_gains, norm_biases, up_all,
    )
    final_rows, mlp_branch, sums_three = feed_down(
        where, sib_act, own_act, down_all, middle, norm_gains, norm_biases, out_cot, row_weight
    )
    sib_hidden, own_hidden, branch_grad, state_grad, sums_mid, grad_a, grad_b, grad_c, grad_d = feed_back(
        where, mlp_branch, slopes, down_all, up_all, munit, minv, aunit, ainv, out_cot, row_weight, norm_gains,
        [out_all[0], out_all[1], out_all[2], out_all[3]],
    )

    pair_grads = []
    for pair in range(2):
        cut = slice(pair * LANES, (pair + 1) * LANES)
        from_sib = core_swap(grad_c[:, cut])
        far = core_swap(grad_d[:, cut])
        pair_grads.append([grad_a, from_sib, y_swap(grad_b[:, cut]), y_swap(far)])

    down_own, down_other = weight_grad(mlp_branch, core_swap(mlp_branch), own_act, core_swap(sib_act), "down_grad")
    up_own, up_other = weight_grad(
        mid_normed, core_swap(mid_normed), own_hidden, core_swap(sib_hidden), "up_grad"
    )
    out_own, out_other = out_weight_grad(where, branch_grad, core_swap(branch_grad), attended, theirs)

    parts = [
        attend_back(
            pair, where, key_rows, value_rows, query_more[pair], pair_grads[pair], attended[pair], cosine, sine
        )
        for pair in range(2)
    ]
    send_far, keep_far, sums_far = in_back(place ^ 3, place ^ 2, parts, w_qkv, inputs)
    send_near, keep_near, sums_near = in_back(place ^ 1, place, parts, w_qkv, inputs)
    qkv_grads = [product(normed_turned, p).astype(BF16) for p in parts]

    far = (keep_far.astype(F32) + core_swap(send_far).astype(F32)).astype(BF16)
    near = keep_near.astype(F32) + core_swap(send_near).astype(F32)
    in_rows = near + y_swap(far).astype(F32)
    first_in = lax.dynamic_slice_in_dim(inputs, place * quarter, quarter, 0).astype(F32)
    unit_in, inverse_in = normalize(first_in)
    input_grad = state_grad + norm_back(in_rows, unit_in, inverse_in, norm_gains[0])

    sums_in = sums_far + sums_near
    sums = jnp.concatenate(
        [sums_in[0:1], sums_mid[0:2], sums_three[0:1], sums_in[1:2], sums_mid[2:4], sums_three[1:2]], axis=0
    )
    for axis in ("tensor", "dp"):
        bit = 1
        while bit < lax.axis_size(axis):
            sums = sums + swap(sums, axis, bit)
            bit *= 2
    share = width // (4 * dp_size)
    sums = lax.dynamic_slice_in_dim(sums, (lax.axis_index("dp") * 4 + place) * share, share, 1)

    down_total = sum_y_first(down_own, down_other, (0, 1, 2)).T
    up_total = sum_y_second(up_own, up_other, 0, (1, 2))
    out_total = sum_y_first(out_own, out_other, (0, 1, 2)).T
    qkv_parts = [Blocks([g]).rest((0, 1, 2)) for g in qkv_grads]
    qkv_total = jnp.concatenate([jnp.moveaxis(q.reshape(-1, 3, LANES), 1, 0) for q in qkv_parts], axis=2)
    return (
        final_rows,
        input_grad,
        qkv_total,
        out_total,
        up_total,
        down_total,
        sums[:4],
        sums[4:],
    )


def solution(mesh):
    placed = (
        P("dp", None),
        P(None, None, "tensor"),
        P("tensor", None),
        P(None, "tensor"),
        P("tensor", None),
        P(),
        P(),
        P("dp", None),
        P("dp"),
        P(),
    )
    return jax.shard_map(
        per_device,
        mesh=mesh,
        in_specs=placed,
        out_specs=(
            P(("dp", "tensor"), None),
            P(("dp", "tensor"), None),
            P(None, "dp", "tensor"),
            P("tensor", "dp"),
            P("dp", "tensor"),
            P("tensor", "dp"),
            P(None, ("dp", "tensor")),
            P(None, ("dp", "tensor")),
        ),
        check_vma=False,
    )
```

```python
import functools
import math

import jax
import jax.numpy as jnp
import numpy as np
from jax import lax
from jax.experimental import pallas as pl
from jax.experimental.pallas import tpu as pltpu
from jax.sharding import PartitionSpec as P

DH = 64
SEQ = 2048
EPS = 1e-05
PART = 32
F32 = jnp.float32
BF16 = jnp.bfloat16
LANES = 128
NT = (((1,), (1,)), ((), ()))
TN = (((0,), (0,)), ((), ()))
ANY = pl.BlockSpec(memory_space=pl.ANY)


def params(mebibytes=60):
    return pltpu.CompilerParams(vmem_limit_bytes=mebibytes * 2**20)


def cost(micros):
    return pl.CostEstimate(flops=int(micros * 1.1e9), bytes_accessed=2**16, transcendentals=0)


def shaped(shape, kind):
    return jax.ShapeDtypeStruct(shape, kind)


def fixed(shape):
    return pl.BlockSpec(shape, lambda *unused: (0,) * len(shape))


def gate(field, *deps):
    return pl.pallas_call(
        lambda *refs: None,
        in_specs=[ANY] * (1 + len(deps)),
        out_specs=ANY,
        out_shape=shaped(field.shape, field.dtype),
        input_output_aliases={0: 0},
        cost_estimate=cost(0),
        name="gate",
    )(field, *deps)


def swap(field, axis, bit):
    size = lax.axis_size(axis)
    return lax.ppermute(field, axis, [(i, i ^ bit) for i in range(size)])


def core_swap(field):
    return swap(field, "tensor", 1)


def y_swap(field):
    return swap(field, "tensor", 2)


def total(addends):
    return sum(a.astype(F32) for a in addends)


def diagonal_swap(field, dp_bits, tensor_bits):
    mask = 4 * dp_bits + tensor_bits
    size = 4 * lax.axis_size("dp")
    return lax.ppermute(field, ("dp", "tensor"), [(i, i ^ mask) for i in range(size)])


def move_rows(number, sources, targets, moves, name):
    def kernel(number_ref, *refs):
        source_refs, target_refs, sems = refs[: len(sources)], refs[len(sources) : -1], refs[-1]
        copies = []
        for at, (source, begin, target, end, rows) in enumerate(moves):
            begin, end = (pl.multiple_of(f(number_ref[0]), 16) for f in (begin, end))
            copies.append(
                pltpu.make_async_copy(
                    source_refs[source].at[pl.ds(begin, rows)], target_refs[target].at[pl.ds(end, rows)], sems.at[at]
                )
            )
        for copy in copies:
            copy.start()
        for copy in copies:
            copy.wait()

    return pl.pallas_call(
        kernel,
        grid_spec=pltpu.PrefetchScalarGridSpec(
            num_scalar_prefetch=1,
            grid=(1,),
            in_specs=[ANY] * len(sources),
            out_specs=[fixed(t) for t in targets],
            scratch_shapes=[pltpu.SemaphoreType.DMA((len(moves),))],
        ),
        out_shape=[shaped(t, BF16) for t in targets],
        compiler_params=params(60),
        cost_estimate=cost(1.5),
        name=name,
    )(number, *sources)


def dp_kinds():
    return [1 << k for k in reversed(range(lax.axis_size("dp").bit_length() - 1))]


class Item:
    def __init__(self, left, *addends):
        self.left = list(left)
        self.addends = list(addends)
        self.shape = addends[0][0].shape[2:]


def block_index(kinds, bits, free, flips):
    def index(g, own_ref):
        at = 0
        for bit in bits:
            if bit in free:
                value = (g >> (len(free) - 1 - free.index(bit))) & 1
            else:
                value = own_ref[kinds.index(bit)]
                flip = flips(g, bit)
                value = value + flip - 2 * value * flip
            at = 2 * at + value
        return at

    return index


def addend_specs(items, kinds, frees, flips):
    specs, arrays = [], []
    for item, free in zip(items, frees):
        for array, which, bits in item.addends:
            at = block_index(kinds, bits, free, flips)
            specs.append(
                pl.BlockSpec((1, 1) + item.shape, lambda g, own_ref, at=at, which=which: (at(g, own_ref), which, 0, 0))
            )
            arrays.append(array)
    return specs, arrays


def sums_of(items, refs):
    refs = iter(refs)
    return [total([next(refs)[0, 0] for unused in item.addends]) for item in items]


def halve(owns, items, kind, *deps):
    kinds = ["y"] + dp_kinds()
    frees = [[b for b in item.left if b != kind] for item in items]
    steps = 2 ** len(frees[0])
    specs, arrays = addend_specs(items, kinds, frees, lambda g, bit: 1 if bit == kind else 0)
    shape = (len(items),) + items[0].shape

    def kernel(own_ref, *refs):
        for i, field in enumerate(sums_of(items, refs)):
            refs[-1][0, i] = field.astype(BF16)

    sent = pl.pallas_call(
        kernel,
        grid_spec=pltpu.PrefetchScalarGridSpec(
            num_scalar_prefetch=1,
            grid=(steps,),
            in_specs=specs + [ANY] * len(deps),
            out_specs=pl.BlockSpec((1,) + shape, lambda g, own_ref: (g, 0, 0, 0)),
        ),
        out_shape=shaped((steps,) + shape, BF16),
        compiler_params=params(60),
        cost_estimate=cost(3),
        name="halve",
    )(owns, *arrays, *deps)
    got = y_swap(sent) if kind == "y" else swap(sent, "dp", kind)
    for i, (item, free) in enumerate(zip(items, frees)):
        item.left = free
        item.addends.append((got, i, free))
    return sent


def send_three(owns, items, *deps):
    while len(items[0].left) > 2:
        deps = (halve(owns, items, items[0].left[0 if items[0].left[0] != "y" else 1], *deps),)
    kinds = ["y"] + dp_kinds()
    first, second = items[0].left
    flips = lambda g, bit: (g + 1) // 2 if bit == first else ((g + 1) % 2 if bit == second else 0)
    specs, arrays = addend_specs(items, kinds, [[] for item in items], flips)
    shape = (1, len(items)) + items[0].shape

    def kernel(own_ref, *refs):
        for i, field in enumerate(sums_of(items, refs)):
            for k in range(3):

                @pl.when(pl.program_id(0) == k)
                def _(k=k):
                    refs[k - 3][0, i] = field.astype(BF16)

    sent = pl.pallas_call(
        kernel,
        grid_spec=pltpu.PrefetchScalarGridSpec(
            num_scalar_prefetch=1,
            grid=(3,),
            in_specs=specs + [ANY] * len(deps),
            out_specs=[fixed(shape)] * 3,
        ),
        out_shape=[shaped(shape, BF16)] * 3,
        compiler_params=params(60),
        cost_estimate=cost(2),
        name="send_three",
    )(owns, *arrays, *deps)
    for g, field in enumerate(sent):
        bits = [b for b, on in ((first, (g + 1) // 2), (second, (g + 1) % 2)) if on]
        got = diagonal_swap(field, sum(b for b in bits if b != "y"), 2 if "y" in bits else 0)
        for i, item in enumerate(items):
            item.addends.append((got, i, []))
    for item in items:
        item.left = []
    return sent[-1]


def finals(owns, groups, *deps):
    kinds = ["y"] + dp_kinds()
    items = [item for group in groups for item, turned in group]
    specs, arrays = addend_specs(items, kinds, [[] for item in items], lambda g, bit: 0)
    shapes = []
    for group in groups:
        rows, columns = group[0][0].shape
        shapes.append((columns * len(group), rows) if group[0][1] else (rows, columns * len(group)))

    def kernel(own_ref, *refs):
        fields = iter(sums_of(items, refs))
        for group, out_ref in zip(groups, refs[-len(groups) :]):
            for i, (item, turned) in enumerate(group):
                cut = slice(i * item.shape[1], (i + 1) * item.shape[1])
                field = next(fields)
                if turned:
                    out_ref[cut, :] = jnp.transpose(field)
                else:
                    out_ref[:, cut] = field

    return pl.pallas_call(
        kernel,
        grid_spec=pltpu.PrefetchScalarGridSpec(
            num_scalar_prefetch=1,
            grid=(1,),
            in_specs=specs + [ANY] * len(deps),
            out_specs=[fixed(shape) for shape in shapes],
        ),
        out_shape=[shaped(shape, F32) for shape in shapes],
        compiler_params=params(60),
        cost_estimate=cost(3),
        name="finals",
    )(owns, *arrays, *deps)


def normalize(field):
    mean = jnp.mean(field, axis=-1, keepdims=True)
    centred = field - mean
    inverse = lax.rsqrt(jnp.mean(centred * centred, axis=-1, keepdims=True) + EPS)
    return centred * inverse, inverse


def norm_back(grad, unit, inverse, gain):
    scaled = grad * gain
    mean_one = jnp.mean(scaled, axis=-1, keepdims=True)
    mean_two = jnp.mean(scaled * unit, axis=-1, keepdims=True)
    return inverse * (scaled - mean_one - unit * mean_two)


def rotary_tables():
    half = DH // 2
    frequency = np.exp(np.arange(half, dtype=np.float32) * np.float32(-math.log(10000.0) / half))
    angles = np.arange(SEQ, dtype=np.float32)[:, None] * frequency.astype(np.float32)[None, :]
    cosine, sine = np.cos(angles), np.sin(angles)
    return (
        jnp.asarray(np.concatenate([cosine] * 4, axis=1).astype(np.float32)),
        jnp.asarray(np.concatenate([-sine, sine, -sine, sine], axis=1).astype(np.float32)),
    )


def lanes_of(shape):
    return lax.broadcasted_iota(jnp.int32, shape, 1)


def partner_lanes(field):
    lane = lanes_of(field.shape)
    return jnp.where(lane % DH < DH // 2, pltpu.roll(field, 96, 1), pltpu.roll(field, 32, 1))


def rotate(field, cosine, sine):
    return field * cosine + partner_lanes(field) * sine


def rotate_back(field, cosine, sine):
    return field * cosine - partner_lanes(field) * sine


def split_three(field):
    high = field.astype(BF16).astype(F32)
    rest = field - high
    middle = rest.astype(BF16).astype(F32)
    return high, middle, rest - middle


def product(left, right):
    return jnp.dot(left, right, preferred_element_type=F32)


def product_nt(left, right):
    return lax.dot_general(left, right, NT, preferred_element_type=F32)


def column_sum(field):
    return jnp.sum(field, axis=0, keepdims=True)


def project_kernel(x_ref, w_ref, gain_ref, bias_ref, cos_ref, sin_ref, *more):
    n_ref, q_ref, k_ref, v_ref, normed_ref = more[-5:]
    rows, width = x_ref.shape
    for i in range(rows // PART):
        r = slice(i * PART, (i + 1) * PART)
        unit, unused = normalize(x_ref[r, :].astype(F32))
        normed_ref[r, :] = (unit * gain_ref[0:1, :] + bias_ref[0:1, :]).astype(BF16)
    for i in range(width // 256):
        c = slice(i * 256, (i + 1) * 256)
        n_ref[c, :] = jnp.transpose(normed_ref[:, c])
    lane = lanes_of((PART, LANES))
    ones = jnp.where(lane < DH + 3, 1.0, 0.0)
    for which, out_ref in enumerate((q_ref, k_ref, v_ref)):
        both = product(normed_ref[...], w_ref[which])
        for i in range(rows // PART):
            r = slice(i * PART, (i + 1) * PART)
            for pair in range(both.shape[1] // LANES):
                field = both[r, pair * LANES : (pair + 1) * LANES]
                if which < 2:
                    field = rotate(field, cos_ref[r, :], sin_ref[r, :])
                if which == 0:
                    field = field * (1.0 / math.sqrt(DH))
                extra = jnp.zeros_like(field) if which == 0 else ones
                out_ref[2 * pair, r, :] = jnp.where(lane < DH, field, extra).astype(BF16)
                out_ref[2 * pair + 1, r, :] = jnp.where(lane < DH, pltpu.roll(field, DH, 1), extra).astype(BF16)


def project(inputs, w_qkv, gain, bias, cosine, sine, *deps):
    block = 256
    tokens, width = inputs.shape
    local = w_qkv.shape[2]
    heads = local // DH
    rows = lambda i: (i, 0)
    per_head = pl.BlockSpec((heads, block, LANES), lambda i: (0, i, 0))
    headed = shaped((heads, tokens, LANES), BF16)
    return pl.pallas_call(
        project_kernel,
        grid=(tokens // block,),
        in_specs=[
            pl.BlockSpec((block, width), rows),
            fixed((3, width, local)),
            fixed((4, width)),
            fixed((4, width)),
            pl.BlockSpec((block, LANES), rows),
            pl.BlockSpec((block, LANES), rows),
        ]
        + [ANY] * len(deps),
        out_specs=[pl.BlockSpec((width, block), lambda i: (0, i)), per_head, per_head, per_head],
        out_shape=[shaped((width, tokens), BF16), headed, headed, headed],
        scratch_shapes=[pltpu.VMEM((block, width), BF16)],
        compiler_params=params(60),
        cost_estimate=cost(10),
        name="project",
    )(inputs, w_qkv, gain, bias, cosine, sine, *deps)


ROWS = 512
KEYS = 512
STRIP = 256


def hidden_keys(shape, down, across):
    return lax.broadcasted_iota(jnp.int32, shape, 0) + down > lax.broadcasted_iota(jnp.int32, shape, 1) + across


def attend_block(n, place_ref, q_ref, k_ref, v_ref, out_refs, qa_ref, score_ref, chance_ref):
    start, end = n * ROWS, (n + 1) * ROWS
    row = lax.broadcasted_iota(jnp.int32, (LANES, ROWS), 0)
    lane = lanes_of((ROWS, LANES))
    outs = []
    for h in range(2):
        most = None
        for begin in range(0, end, STRIP):
            scores = product_nt(k_ref[h, begin : begin + STRIP, :], q_ref[h])
            if begin >= start:
                scores = jnp.where(hidden_keys((STRIP, ROWS), begin, start), -1e30, scores)
            score_ref[h, begin : begin + STRIP, :] = scores
            for i in range(0, STRIP, 8):
                most = scores[i : i + 8] if most is None else jnp.maximum(most, scores[i : i + 8])
        top = jnp.max(most, axis=0, keepdims=True)
        for begin in range(0, end, PART):
            r = slice(begin, begin + PART)
            chance_ref[h, r, :] = jnp.exp(score_ref[h, r, :] - top).astype(BF16)
        both = lax.dot_general(v_ref[h, :end, :], chance_ref[h, :end, :], TN, preferred_element_type=F32)
        summed = both[DH : DH + 1, :]
        high, middle, low = split_three(-(top + jnp.log(summed)))
        extra = jnp.where(row == DH + 1, middle, jnp.where(row == DH + 2, low, 0.0))
        extra = jnp.where(row == DH, high, extra)
        turned = jnp.transpose(jnp.where(row < DH, both * (1.0 / summed), extra))
        qa_ref[h] = jnp.where(lane < DH, q_ref[h].astype(F32), turned).astype(BF16)
        outs.append(turned)
    both = jnp.where(lane < DH, outs[0], pltpu.roll(outs[1], DH, 1)).astype(BF16)
    for which, out_ref in enumerate(out_refs):

        @pl.when((place_ref[0] ^ which) == n)
        def _(out_ref=out_ref):
            out_ref[...] = both


def attend_kernel(place_ref, q_ref, k_ref, v_ref, *more):
    block = pl.program_id(0)
    for n in range(SEQ // ROWS):
        pl.when(block == n)(
            functools.partial(attend_block, n, place_ref, q_ref, k_ref, v_ref, more[-7:-3], *more[-3:])
        )


def attend(pair, place, query, key_rows, value_rows, *deps):
    whole = pl.BlockSpec((2, SEQ, LANES), lambda i, t: (pair, 0, 0))
    return pl.pallas_call(
        attend_kernel,
        grid_spec=pltpu.PrefetchScalarGridSpec(
            num_scalar_prefetch=1,
            grid=(SEQ // ROWS,),
            in_specs=[pl.BlockSpec((2, ROWS, LANES), lambda i, t: (pair, i, 0)), whole, whole] + [ANY] * len(deps),
            out_specs=[fixed((ROWS, LANES))] * 4 + [pl.BlockSpec((2, ROWS, LANES), lambda i, t: (0, i, 0))],
            scratch_shapes=[pltpu.VMEM((2, SEQ, ROWS), F32), pltpu.VMEM((2, SEQ, ROWS), BF16)],
        ),
        out_shape=[shaped((ROWS, LANES), BF16)] * 4 + [shaped((2, SEQ, LANES), BF16)],
        compiler_params=params(60),
        cost_estimate=cost(10),
        name="attend",
    )(place, query, key_rows, value_rows, *deps)


def back_block(j, k_ref, v_ref, qa_ref, cos_ref, sin_ref, pg_ref, da_ref, dq_ref, chance_ref, score_ref):
    start, length = j * KEYS, SEQ - j * KEYS
    rows = slice(start, start + KEYS)
    lane = lanes_of((KEYS, LANES))
    key_grads, value_grads = [], []
    for h in range(2):
        keys, values = k_ref[h, rows, :], v_ref[h, rows, :]
        for begin in range(0, length, KEYS):
            cut = slice(begin, begin + KEYS)
            scores = product_nt(keys, qa_ref[h, start + begin : start + begin + KEYS, :])
            chance_grad = product_nt(values, da_ref[h, start + begin : start + begin + KEYS, :])
            for i in range(0, KEYS, 64):
                r = slice(i, i + 64)
                chance = jnp.exp(scores[r])
                if begin == 0:
                    chance = jnp.where(hidden_keys((64, KEYS), i, 0), 0.0, chance)
                chance_ref[h, r, cut] = chance.astype(BF16)
                score_ref[h, r, cut] = (chance * chance_grad[r]).astype(BF16)
        value_grads.append(product(chance_ref[h, :, :length], da_ref[h, start:, :]))
        key_grads.append(product(score_ref[h, :, :length], qa_ref[h, start:, :]))
        turned = lax.dot_general(keys[:, :DH], score_ref[h, :, :length], TN, preferred_element_type=F32)
        if j == 0:
            dq_ref[h] = turned
        else:
            dq_ref[h, :, start:] += turned
    key_grad = jnp.where(lane < DH, key_grads[0], pltpu.roll(key_grads[1], DH, 1))
    value_grad = jnp.where(lane < DH, value_grads[0], pltpu.roll(value_grads[1], DH, 1))
    pg_ref[rows, LANES : 2 * LANES] = rotate_back(key_grad, cos_ref[rows, :], sin_ref[rows, :]).astype(BF16)
    pg_ref[rows, 2 * LANES :] = value_grad.astype(BF16)


def back_kernel(place_ref, k_ref, v_ref, qa_ref, g0, g1, g2, g3, o0, o1, o2, o3, cos_ref, sin_ref, *more):
    pg_ref, da_ref, turned_ref, chance_ref, score_ref = more[-5:]
    step = pl.program_id(0)
    steps = SEQ // KEYS
    span = 64

    @pl.when(step == 0)
    def _():
        lane = lanes_of((span, LANES))
        for which, (grad_ref, out_ref) in enumerate(((g0, o0), (g1, o1), (g2, o2), (g3, o3))):
            begin = (place_ref[0] ^ which) * (SEQ // 4)
            for i in range(SEQ // 4 // span):
                rows = pl.ds(pl.multiple_of(begin + i * span, span), span)
                part = slice(i * span, (i + 1) * span)
                grad = grad_ref[part, :].astype(F32)
                both = grad * out_ref[part, :].astype(F32)
                for h in range(2):
                    inner = jnp.sum(jnp.where(lane // DH == h, both, 0.0), axis=1, keepdims=True)
                    high, middle, low = split_three(-inner)
                    own = grad if h == 0 else pltpu.roll(grad, DH, 1)
                    extra = jnp.where(lane == DH + 1, middle, jnp.where(lane == DH + 2, low, 0.0))
                    extra = jnp.where(lane == DH, high, extra)
                    da_ref[h, rows, :] = jnp.where(lane < DH, own, extra).astype(BF16)

    for j in range(steps):
        pl.when(step == j)(
            functools.partial(
                back_block, j, k_ref, v_ref, qa_ref, cos_ref, sin_ref, pg_ref, da_ref, turned_ref, chance_ref,
                score_ref,
            )
        )

    @pl.when(step == steps - 1)
    def _():
        for begin in range(0, SEQ, 256):
            rows = slice(begin, begin + 256)
            both = jnp.concatenate([turned_ref[0, :, rows], turned_ref[1, :, rows]], axis=0)
            field = jnp.transpose(both) * (1.0 / math.sqrt(DH))
            pg_ref[rows, :LANES] = rotate_back(field, cos_ref[rows, :], sin_ref[rows, :]).astype(BF16)


def attend_back(pair, place, key_rows, value_rows, query_more, grads, outs, cosine, sine, *deps):
    whole = pl.BlockSpec((2, SEQ, LANES), lambda i, s: (pair, 0, 0))
    quarters = [fixed((SEQ // 4, LANES))] * 8
    table = fixed((SEQ, LANES))
    return pl.pallas_call(
        back_kernel,
        grid_spec=pltpu.PrefetchScalarGridSpec(
            num_scalar_prefetch=1,
            grid=(SEQ // KEYS,),
            in_specs=[whole, whole, fixed((2, SEQ, LANES))] + quarters + [table, table] + [ANY] * len(deps),
            out_specs=fixed((SEQ, 3 * LANES)),
            scratch_shapes=[
                pltpu.VMEM((2, SEQ, LANES), BF16),
                pltpu.VMEM((2, DH, SEQ), F32),
                pltpu.VMEM((2, KEYS, SEQ), BF16),
                pltpu.VMEM((2, KEYS, SEQ), BF16),
            ],
        ),
        out_shape=shaped((SEQ, 3 * LANES), BF16),
        compiler_params=params(60),
        cost_estimate=cost(16),
        name="attend_back",
    )(place, key_rows, value_rows, query_more, *grads, *outs, cosine, sine, *deps)


CHUNK = 512
HALF = 256
SCALE = math.sqrt(2.0 / math.pi)
CUBIC = 0.044715


def feed_kernel(place_ref, *refs):
    pairs = [refs[2 * k : 2 * k + 2] for k in range(4)]
    x_ref, cot_ref, weight_ref, gain_ref, bias_ref = refs[8:13]
    outs, ups, downs = refs[13:17], refs[17:21], refs[21:25]
    sib_act, own_act, mn_ref, final_ref, mlp_ref, sib_hidden, own_hidden, branch_ref, state_ref, sum_ref = refs[25:35]
    features = refs[35:43]
    out_w, up_w, down_w, slope_ref, mid_ref, aunit_ref, munit_ref, ainv_ref, minv_ref, sums, sems = refs[43:]
    tokens, width = x_ref.shape

    loads = []
    for at, (sources, target) in enumerate(((outs, out_w), (ups, up_w), (downs, down_w))):
        for k, source in enumerate(sources):
            loads.append(pltpu.make_async_copy(source, target.at[k], sems.at[4 * at + k]))
    for load in loads:
        load.start()
    sums[...] = jnp.zeros_like(sums)

    def add_sum(k, field):
        part = field[0:8]
        for i in range(8, field.shape[0], 8):
            part = part + field[i : i + 8]
        sums[k] += part

    halves = [range(h, h + HALF, PART) for h in range(0, tokens, HALF)]

    for load in loads[:4]:
        load.wait()
    for parts in halves:
        rows = slice(parts.start, parts.stop)
        branch = None
        for k, (first, second) in enumerate(pairs):
            left = jnp.concatenate([first[rows, :], second[rows, :]], axis=1)
            term = product(left, out_w[k])
            branch = term if branch is None else branch + term
        for begin in parts:
            r = slice(begin, begin + PART)
            aunit, ainv = normalize(branch[begin - parts.start : begin - parts.start + PART])
            middle = x_ref[r, :].astype(F32) + aunit * gain_ref[1:2, :] + bias_ref[1:2, :]
            munit, minv = normalize(middle)
            mid_ref[r, :] = middle
            aunit_ref[r, :] = aunit
            munit_ref[r, :] = munit
            ainv_ref[r, :] = jnp.broadcast_to(ainv, (PART, LANES))
            minv_ref[r, :] = jnp.broadcast_to(minv, (PART, LANES))
            mn_ref[r, :] = (munit * gain_ref[2:3, :] + bias_ref[2:3, :]).astype(BF16)

    for k in range(4):
        loads[4 + k].wait()
        act_ref, columns = (sib_act, own_act)[k // 2], slice(k % 2 * width, (k % 2 + 1) * width)
        for parts in halves:
            value = product(mn_ref[parts.start : parts.stop, :], up_w[k])
            for i in range(0, HALF, 16):
                r = slice(parts.start + i, parts.start + i + 16)
                v = value[i : i + 16]
                square = v * v
                bent = jnp.tanh(v * (SCALE + (SCALE * CUBIC) * square))
                half = 0.5 + 0.5 * bent
                act_ref[r, columns] = (v * half).astype(BF16)
                slope = half + v * (1.0 - bent * bent) * (0.5 * SCALE + (1.5 * SCALE * CUBIC) * square)
                slope_ref[k, r, :] = slope.astype(BF16)

    for load in loads[8:]:
        load.wait()
    for parts in halves:
        rows = slice(parts.start, parts.stop)
        branch = None
        for k in range(4):
            act_ref, columns = (sib_act, own_act)[k // 2], slice(k % 2 * width, (k % 2 + 1) * width)
            term = product(act_ref[rows, columns], down_w[k])
            branch = term if branch is None else branch + term
        for begin in parts:
            r = slice(begin, begin + PART)
            unit, inverse = normalize(branch[begin - parts.start : begin - parts.start + PART])
            final_ref[r, :] = (mid_ref[r, :] + unit * gain_ref[3:4, :] + bias_ref[3:4, :]).astype(BF16)
            grad = cot_ref[r, :].astype(F32) * weight_ref[r, :1]
            add_sum(3, grad * unit)
            add_sum(7, grad)
            mlp_ref[r, :] = norm_back(grad, unit, inverse, gain_ref[3:4, :]).astype(BF16)

    mid_grads = []
    for parts in halves:
        rows = slice(parts.start, parts.stop)
        mid_grad = None
        for k in range(4):
            hid_ref, columns = (sib_hidden, own_hidden)[k // 2], slice(k % 2 * width, (k % 2 + 1) * width)
            act_grad = product_nt(mlp_ref[rows, :], down_w[k])
            hidden = (slope_ref[k, rows, :].astype(F32) * act_grad).astype(BF16)
            hid_ref[rows, columns] = hidden
            term = product_nt(hidden, up_w[k])
            mid_grad = term if mid_grad is None else mid_grad + term
        mid_grads.append(mid_grad)
    for parts, mid_all in zip(halves, mid_grads):
        rows = slice(parts.start, parts.stop)
        for begin in parts:
            r = slice(begin, begin + PART)
            mid_grad, munit, aunit = mid_all[begin - parts.start : begin - parts.start + PART], munit_ref[r, :], aunit_ref[r, :]
            grad = cot_ref[r, :].astype(F32) * weight_ref[r, :1]
            state = grad + norm_back(mid_grad, munit, minv_ref[r, :1], gain_ref[2:3, :])
            state_ref[r, :] = state
            branch_ref[r, :] = norm_back(state, aunit, ainv_ref[r, :1], gain_ref[1:2, :]).astype(BF16)
            for k, term in ((1, state * aunit), (2, mid_grad * munit), (5, state), (6, mid_grad)):
                add_sum(k, term)
        for k in (1, 2, 3, 0):
            field = product_nt(branch_ref[rows, :], out_w[k]).astype(BF16)
            for pair in range(2):
                features[2 * k + pair][rows, :] = field[:, pair * LANES : (pair + 1) * LANES]
    for k in range(8):
        sum_ref[k : k + 1, :] = column_sum(sums[k])


def feed(place, pairs, inputs, cot, weight, gains, biases, outs, ups, downs):
    width = inputs.shape[1]
    quarter = inputs.shape[0] // 4
    hid = 2 * width
    local = outs[0].shape[0]
    in_place = lambda s, t: (t[0], 0)
    stat = fixed((quarter, LANES))
    row_spec, wide = fixed((quarter, width)), fixed((quarter, hid))
    row_shape, wide_shape = shaped((quarter, width), BF16), shaped((quarter, hid), BF16)
    return pl.pallas_call(
        feed_kernel,
        grid_spec=pltpu.PrefetchScalarGridSpec(
            num_scalar_prefetch=1,
            grid=(1,),
            in_specs=[stat] * 8
            + [pl.BlockSpec((quarter, width), in_place)] * 2
            + [stat, fixed((4, width)), fixed((4, width))]
            + [ANY] * 12,
            out_specs=[wide, wide, row_spec, row_spec, row_spec, wide, wide, row_spec, row_spec, fixed((8, width))]
            + [stat] * 8,
            scratch_shapes=[
                pltpu.VMEM((4, local, width), BF16),
                pltpu.VMEM((4, width, width), BF16),
                pltpu.VMEM((4, width, width), BF16),
                pltpu.VMEM((4, quarter, width), BF16),
            ]
            + [pltpu.VMEM((quarter, width), F32)] * 3
            + [pltpu.VMEM((quarter, LANES), F32)] * 2
            + [pltpu.VMEM((8, 8, width), F32), pltpu.SemaphoreType.DMA((12,))],
        ),
        out_shape=[wide_shape, wide_shape, row_shape, row_shape, row_shape, wide_shape, wide_shape, row_shape]
        + [shaped((quarter, width), F32), shaped((8, width), F32)]
        + [shaped((quarter, LANES), BF16)] * 8,
        compiler_params=params(),
        cost_estimate=cost(34),
        name="feed",
    )(place, *[part for pair in pairs for part in pair], inputs, cot, weight, gains, biases, *outs, *ups, *downs)


def keep_and_send(own, bit, field, keep_ref, send_ref):
    blocks, rows = send_ref.shape[0], send_ref.shape[2]
    for j in range(blocks):
        low = j // bit * 2 * bit + j % bit
        for ref, value in ((keep_ref, own), (send_ref, 1 - own)):
            begin = pl.multiple_of((low + value * bit) * rows, 16)
            ref[j, 0] = field[pl.ds(begin, rows), :]


def weight_kernel(bits, own_ref, x1, x2, y1, y2, *more):
    outs, field_ref = more[-5:-1], more[-1]
    step = pl.program_id(0)
    field = lax.dot_general(x1[...], y1[...], TN, preferred_element_type=F32)
    field = field + lax.dot_general(x2[...], y2[...], TN, preferred_element_type=F32)
    field_ref[...] = field.astype(BF16)
    for half, bit in enumerate(bits):
        keep_ref, send_ref = outs[2 * half : 2 * half + 2]
        if bit == "y":
            rows = keep_ref.shape[2]
            for k, ref in enumerate((keep_ref, send_ref)):

                @pl.when(step == 2 * half + k)
                def _(ref=ref):
                    for j in range(ref.shape[0]):
                        ref[j, 0] = field_ref[j * rows : (j + 1) * rows, :]

        else:

            @pl.when(step // 2 == half)
            def _(bit=bit, keep_ref=keep_ref, send_ref=send_ref):
                keep_and_send(own_ref[half], bit, field_ref, keep_ref, send_ref)


def weight_grad(own_bits, bits, x1, x2, y1, y2, name, *deps):
    rows, width = x1.shape
    size = lax.axis_size("dp")
    y_spec = pl.BlockSpec((rows, CHUNK), lambda s, o: (0, s // 2 + 2 * (s % 2)))
    shape = (size, 1, width // size, CHUNK)
    specs = []
    for half, bit in enumerate(bits):
        if bit == "y":
            specs += [fixed(shape)] * 2
        else:
            part = (size // 2,) + shape[1:]
            specs += [pl.BlockSpec(part, lambda s, o, half=half: (jnp.clip(s - 2 * half, 0, 1), 0, 0, 0))] * 2
    return pl.pallas_call(
        functools.partial(weight_kernel, bits),
        grid_spec=pltpu.PrefetchScalarGridSpec(
            num_scalar_prefetch=1,
            grid=(4,),
            in_specs=[fixed((rows, width))] * 2 + [y_spec] * 2 + [ANY] * len(deps),
            out_specs=specs,
            scratch_shapes=[pltpu.VMEM((width, CHUNK), BF16)],
        ),
        out_shape=[shaped(shape, BF16)] * 4,
        compiler_params=params(60),
        cost_estimate=cost(7),
        name=name,
    )(own_bits, x1, x2, y1, y2, *deps)


def out_weight_kernel(x1, x2, a0, a1, t0, t1, b0, b1, s0, s1, *more):
    for out_ref, mine, sibs in ((more[-2], (a0, a1), (b0, b1)), (more[-1], (t0, t1), (s0, s1))):
        left = jnp.concatenate([mine[0][...], mine[1][...]], axis=1)
        right = jnp.concatenate([sibs[0][...], sibs[1][...]], axis=1)
        field = lax.dot_general(x1[...], left, TN, preferred_element_type=F32)
        field = field + lax.dot_general(x2[...], right, TN, preferred_element_type=F32)
        blocks, unused, rows, unused = out_ref.shape
        for j in range(blocks):
            out_ref[j, 0] = field[j * rows : (j + 1) * rows].astype(BF16)


def out_weight_grad(branch, sibling, own, theirs, own_sib, theirs_sib, *deps):
    rows, width = branch.shape
    size = lax.axis_size("dp")
    shape = (size, 1, width // size, 2 * LANES)
    return pl.pallas_call(
        out_weight_kernel,
        in_specs=[pl.BlockSpec(memory_space=pltpu.VMEM)] * 10 + [ANY] * len(deps),
        out_specs=[pl.BlockSpec(memory_space=pltpu.VMEM)] * 2,
        out_shape=[shaped(shape, BF16)] * 2,
        compiler_params=params(60),
        cost_estimate=cost(3),
        name="out_weight_grad",
    )(branch, sibling, *own, *theirs, *own_sib, *theirs_sib, *deps)


def in_back_kernel(order_ref, p0, p1, w_ref, x_ref, *more):
    send_ref, keep_ref, sum_ref, sums, field_ref = more[-5:]
    step = pl.program_id(0)

    @pl.when(step == 0)
    def _():
        sums[...] = jnp.zeros_like(sums)

    field = None
    for c in range(3):
        cut = slice(c * LANES, (c + 1) * LANES)
        left = jnp.concatenate([p0[:, cut], p1[:, cut]], axis=1)
        term = product_nt(left, w_ref[c])
        field = term if field is None else field + term
    gain_part = bias_part = 0.0
    for begin in range(0, x_ref.shape[0], PART):
        r = slice(begin, begin + PART)
        unit, unused = normalize(x_ref[r, :].astype(F32))
        field_ref[r, :] = field[r].astype(BF16)
        scaled = field[r] * unit
        for i in range(0, PART, 8):
            gain_part = gain_part + scaled[i : i + 8]
            bias_part = bias_part + field[begin + i : begin + i + 8]
    sums[0] += gain_part
    sums[1] += bias_part

    @pl.when(step < 2)
    def _():
        send_ref[...] = field_ref[...]

    @pl.when(step >= 2)
    def _():
        keep_ref[...] = field_ref[...]

    @pl.when(step == 3)
    def _():
        for k in range(2):
            sum_ref[k : k + 1, :] = column_sum(sums[k])


def in_back(sibling_place, own_place, parts, w_qkv, inputs, *deps):
    block = 256
    width = inputs.shape[1]
    order = jnp.stack([2 * sibling_place, 2 * sibling_place + 1, 2 * own_place, 2 * own_place + 1])
    rows = lambda s, o: (o[s], 0)
    return pl.pallas_call(
        in_back_kernel,
        grid_spec=pltpu.PrefetchScalarGridSpec(
            num_scalar_prefetch=1,
            grid=(4,),
            in_specs=[pl.BlockSpec((block, 3 * LANES), rows)] * 2
            + [fixed(w_qkv.shape), pl.BlockSpec((block, width), rows)]
            + [ANY] * len(deps),
            out_specs=[
                pl.BlockSpec((block, width), lambda s, o: (jnp.minimum(s, 1), 0)),
                pl.BlockSpec((block, width), lambda s, o: (jnp.maximum(s - 2, 0), 0)),
                fixed((2, width)),
            ],
            scratch_shapes=[pltpu.VMEM((2, 8, width), F32), pltpu.VMEM((block, width), BF16)],
        ),
        out_shape=[shaped((2 * block, width), BF16)] * 2 + [shaped((2, width), F32)],
        compiler_params=params(60),
        cost_estimate=cost(4),
        name="in_back",
    )(order.astype(jnp.int32), *parts, w_qkv, inputs, *deps)


def qkv_kernel(own_ref, n_ref, p_ref, *more):
    keep_ref, send_ref, field_ref = more[-3:]
    field_ref[...] = product(n_ref[...], p_ref[...]).astype(BF16)
    keep_and_send(own_ref[0], 1, field_ref, keep_ref, send_ref)


def qkv_grad(own_bits, normed_turned, part, *deps):
    width, tokens = normed_turned.shape
    columns = part.shape[1]
    size = lax.axis_size("dp")
    steps = 2
    shape = (size // 2, 1, width // size, columns)
    spec = pl.BlockSpec((size // 2 // steps,) + shape[1:], lambda i, o: (i, 0, 0, 0))
    return pl.pallas_call(
        qkv_kernel,
        grid_spec=pltpu.PrefetchScalarGridSpec(
            num_scalar_prefetch=1,
            grid=(steps,),
            in_specs=[pl.BlockSpec((width // steps, tokens), lambda i, o: (i, 0)), fixed(part.shape)] + [ANY] * len(deps),
            out_specs=[spec, spec],
            scratch_shapes=[pltpu.VMEM((width // steps, columns), BF16)],
        ),
        out_shape=[shaped(shape, BF16)] * 2,
        compiler_params=params(60),
        cost_estimate=cost(3),
        name="qkv_grad",
    )(own_bits, normed_turned, part, *deps)


def add_kernel(a_ref, b_ref, *more):
    more[-1][...] = (a_ref[...].astype(F32) + b_ref[...].astype(F32)).astype(BF16)


def add_low(a, b, *deps):
    spec = pl.BlockSpec((256, a.shape[1]), lambda i: (i, 0))
    return pl.pallas_call(
        add_kernel,
        grid=(a.shape[0] // 256,),
        in_specs=[spec, spec] + [ANY] * len(deps),
        out_specs=spec,
        out_shape=shaped(a.shape, BF16),
        compiler_params=params(60),
        cost_estimate=cost(2),
        name="add_low",
    )(a, b, *deps)


def finish_kernel(place_ref, x_ref, state_ref, keep_ref, near_ref, far_ref, gain_ref, *more):
    out_ref = more[-1]
    for begin in range(0, x_ref.shape[0], PART):
        r = slice(begin, begin + PART)
        unit, inverse = normalize(x_ref[r, :].astype(F32))
        grad = total([keep_ref[r, :], near_ref[r, :], far_ref[r, :]])
        out_ref[r, :] = state_ref[r, :] + norm_back(grad, unit, inverse, gain_ref[0:1, :])


def finish(place, inputs, state, keep, near, far, gains, *deps):
    quarter, width = state.shape
    block = 128
    steps = quarter // block
    spec = pl.BlockSpec((block, width), lambda s, t: (s, 0))
    return pl.pallas_call(
        finish_kernel,
        grid_spec=pltpu.PrefetchScalarGridSpec(
            num_scalar_prefetch=1,
            grid=(steps,),
            in_specs=[pl.BlockSpec((block, width), lambda s, t: (t[0] * steps + s, 0))]
            + [spec] * 4
            + [fixed(gains.shape)]
            + [ANY] * len(deps),
            out_specs=spec,
        ),
        out_shape=shaped((quarter, width), F32),
        compiler_params=params(60),
        cost_estimate=cost(4),
        name="finish",
    )(place, inputs, state, keep, near, far, gains, *deps)


def per_device(
    inputs, w_qkv, w_out, w_up, w_down, norm_gains, norm_biases, out_cot, group_ids, group_weights
):
    tokens, width = inputs.shape
    quarter = tokens // 4
    place = lax.axis_index("tensor")
    where = place.astype(jnp.int32).reshape(1)
    dp_size = lax.axis_size("dp")
    cosine, sine = rotary_tables()

    dp_index = lax.axis_index("dp").astype(jnp.int32)
    mine = (dp_index % 4).reshape(1)
    owns = jnp.stack([jnp.int32(0)] + [(dp_index // kind) % 2 for kind in dp_kinds()])
    bit_x, bit_z = owns[-1], owns[-2]

    own_ids = lax.dynamic_slice_in_dim(group_ids, place * quarter, quarter, 0)
    groups = jnp.arange(group_weights.shape[0], dtype=jnp.int32)
    lookup = (own_ids[:, None] == groups[None, :]).astype(F32)
    row_weight = jnp.sum(lookup * group_weights[None, :], axis=1, keepdims=True)
    row_weight = jnp.broadcast_to(row_weight, (quarter, LANES))

    up_rows, out_rows, down_rows = w_up.shape[0] // 4, w_out.shape[0] // 4, w_down.shape[0] // 4
    zero = lambda m: 0
    up_sent, down_sent = move_rows(
        mine,
        [w_up, w_out, w_down],
        [(up_rows + out_rows, width), (down_rows, width)],
        [
            (0, lambda m: m * up_rows, 0, zero, up_rows),
            (1, lambda m: m * out_rows, 0, lambda m: up_rows, out_rows),
            (2, lambda m: m * down_rows, 1, zero, down_rows),
        ],
        "take",
    )

    def halves(one, two, name):
        rows = one.shape[0] // 2
        moves = [(1, zero, 0, zero, rows), (0, lambda m: rows, 1, zero, rows)]
        low, high = move_rows(mine, [one, two], [(rows, width)] * 2, moves, name)
        return swap(low, "dp", 1), swap(high, "dp", 2)

    def whole_moves(target, rows, begin, half):
        moves = []
        for which in range(3):
            moves.append((which, lambda m: begin, target, lambda m, which=which: (m ^ which) * rows, rows))
        low = max(0, min(half - begin, rows))
        if low:
            moves.append((3, lambda m: begin, target, lambda m: (m ^ 3) * rows, low))
        if rows - low:
            start = begin + low - half
            moves.append((4, lambda m: start, target, lambda m: (m ^ 3) * rows + low, rows - low))
        return moves

    up_got = y_swap(up_sent)
    up_sib, down_sib, out_sib = core_swap(w_up), core_swap(w_down), core_swap(w_out)
    normed_turned, query, key_rows, value_rows = project(
        inputs, w_qkv, norm_gains, norm_biases, cosine, sine, up_sent
    )
    down_sent = gate(down_sent, normed_turned)
    down_got = y_swap(down_sent)

    def to_tokens(outs):
        return [outs[0], core_swap(outs[1]), y_swap(outs[2]), diagonal_swap(outs[3], 0, 3)]

    *outs_first, more_first = attend(0, where, query, key_rows, value_rows, down_sent, up_sib, down_sib, out_sib)
    rows_first = to_tokens(outs_first)
    up_got = gate(up_got, outs_first[0])
    up_one, up_two = swap(up_got, "dp", 1), swap(up_got, "dp", 2)
    *outs_second, more_second = attend(1, where, query, key_rows, value_rows, up_got)
    rows_second = to_tokens(outs_second)
    down_got = gate(down_got, outs_second[0])
    down_one, down_two = swap(down_got, "dp", 1), swap(down_got, "dp", 2)
    up_one = gate(up_one, down_got, *rows_first[1:])
    up_low, up_high = halves(up_one, up_two, "up_halves")
    down_one = gate(down_one, up_low, *rows_second[1:])
    down_low, down_high = halves(down_one, down_two, "down_halves")
    up_y, out_y = move_rows(
        mine,
        [up_got, up_one, up_two, up_low, up_high],
        [w_up.shape, w_out.shape],
        whole_moves(0, up_rows, 0, up_low.shape[0]) + whole_moves(1, out_rows, up_rows, up_low.shape[0]),
        "up_whole",
    )
    up_sib_y, out_sib_y = core_swap(up_y), core_swap(out_y)
    down_low = gate(down_low, up_y)
    (down_y,) = move_rows(
        mine,
        [down_got, down_one, down_two, down_low, down_high],
        [w_down.shape],
        whole_moves(0, down_rows, 0, down_low.shape[0]),
        "down_whole",
    )
    down_sib_y = core_swap(down_y)
    rows = [(rows_first[k], rows_second[k]) for k in range(4)]

    (
        sib_act, own_act, mid_normed, final_rows, mlp_branch, sib_hidden, own_hidden, branch_grad, state_grad, sums_feed,
        *features,
    ) = feed(
        where, [rows[0], rows[2], rows[1], rows[3]],
        inputs, out_cot, row_weight, norm_gains, norm_biases,
        [w_out, out_y, out_sib, out_sib_y], [up_sib, up_sib_y, w_up, up_y], [down_sib, down_sib_y, w_down, down_y],
    )

    pair_grads = []
    for pair in range(2):
        own, for_y, for_core, for_far = features[pair::2]
        pair_grads.append([own, core_swap(for_core), y_swap(for_y), diagonal_swap(for_far, 0, 3)])

    kinds = dp_kinds()
    both = ["y"] + kinds
    without = lambda bits, *gone: [b for b in bits if b not in gone]
    d0_keep, d0_send, d1_keep, d1_send = weight_grad(
        jnp.stack([bit_x, bit_x]), ("y", 1), mlp_branch, core_swap(mlp_branch), own_act, core_swap(sib_act), "down_grad",
        pair_grads[0][1],
    )
    d0 = Item(kinds, (d0_keep, 0, kinds), (y_swap(d0_send), 0, kinds))
    x_bits = without(both, 1)
    d1 = Item(x_bits, (d1_keep, 0, x_bits), (swap(d1_send, "dp", 1), 0, x_bits))
    u0_keep, u0_send, u1_keep, u1_send = weight_grad(
        jnp.stack([bit_x, bit_z]), (1, 2), mid_normed, core_swap(mid_normed), own_hidden, core_swap(sib_hidden), "up_grad",
        d0_send, d1_send, pair_grads[0][2], pair_grads[0][3],
    )
    z_bits = without(both, 2)
    u0 = Item(x_bits, (u0_keep, 0, x_bits), (swap(u0_send, "dp", 1), 0, x_bits))
    u1 = Item(z_bits, (u1_keep, 0, z_bits), (swap(u1_send, "dp", 2), 0, z_bits))
    part_first = attend_back(
        0, where, key_rows, value_rows, more_first, pair_grads[0], outs_first, cosine, sine, u0_send,
        *pair_grads[1][1:],
    )
    out_keep, out_send = out_weight_grad(
        branch_grad, core_swap(branch_grad), rows[0], rows[2], (outs_first[1], outs_second[1]),
        (core_swap(rows_first[3]), core_swap(rows_second[3])), part_first,
    )
    out_item = Item(kinds, (out_keep, 0, kinds), (y_swap(out_send), 0, kinds))
    no_x = without(kinds, 1)

    def qkv_item(part, *deps):
        keep, send = qkv_grad(bit_x.reshape(1), normed_turned, part, *deps)
        return Item(no_x, (keep, 0, no_x), (swap(send, "dp", 1), 0, no_x)), send

    q0, q0_send = qkv_item(part_first, out_send)
    part_second = attend_back(
        1, where, key_rows, value_rows, more_second, pair_grads[1], outs_second, cosine, sine, q0_send
    )
    parts = [part_first, part_second]

    deps = (d0.addends[-1][0], d1.addends[-1][0])
    send_far, keep_far, sums_far = in_back(place ^ 3, place ^ 2, parts, w_qkv, inputs, *deps)
    last = halve(owns, [d0, u1], 1, send_far, u0.addends[-1][0])
    far = add_low(keep_far, core_swap(send_far), last)
    far_got = y_swap(far)
    last = halve(owns, [d1, u0], 2, far)
    send_near, keep_near, sums_near = in_back(place ^ 1, place, parts, w_qkv, inputs, last)
    near_got = core_swap(send_near)
    q1, q1_send = qkv_item(part_second, send_near)
    sums_in = sums_far + sums_near
    sums = jnp.concatenate([sums_in[0:1], sums_feed[1:4], sums_in[1:2], sums_feed[5:8]], axis=0)
    sum_steps = [("tensor", 1), ("tensor", 2)] + [("dp", kind) for kind in kinds[::-1]]

    def add_sums(sums, *after):
        return sums + gate(swap(sums, *sum_steps.pop(0)), *after)

    sums = add_sums(sums, q1_send)
    last = halve(owns, [out_item], 1, q1_send)
    sums = add_sums(sums, last)
    last = send_three(owns, [d0], last, far_got, sums)
    sums = add_sums(sums, last)
    last = send_three(owns, [d1, u0, u1], last, sums)
    last = send_three(owns, [q0, q1], last, near_got)
    sums = add_sums(sums, last)
    last = send_three(owns, [out_item], last, sums)
    while sum_steps:
        sums = add_sums(sums, last)
    share = width // (4 * dp_size)
    sums = lax.dynamic_slice_in_dim(sums, (lax.axis_index("dp") * 4 + place) * share, share, 1)

    input_grad = finish(where, inputs, state_grad, keep_near, near_got, far_got, norm_gains, last)
    (down_total, up_total) = finals(owns, [[(d0, True), (d1, True)], [(u0, False), (u1, False)]], input_grad)
    (qkv_total, out_total) = finals(owns, [[(q0, False), (q1, False)], [(out_item, True)]], up_total)
    qkv_total = qkv_total.reshape(-1, 2, 3, LANES).transpose(2, 0, 1, 3).reshape(3, -1, 2 * LANES)
    return (
        final_rows,
        input_grad,
        qkv_total,
        out_total,
        up_total,
        down_total,
        sums[:4],
        sums[4:],
    )


def solution(mesh):
    placed = (
        P("dp", None),
        P(None, None, "tensor"),
        P("tensor", None),
        P(None, "tensor"),
        P("tensor", None),
        P(),
        P(),
        P("dp", None),
        P("dp"),
        P(),
    )
    return jax.shard_map(
        per_device,
        mesh=mesh,
        in_specs=placed,
        out_specs=(
            P(("dp", "tensor"), None),
            P(("dp", "tensor"), None),
            P(None, "dp", "tensor"),
            P("tensor", "dp"),
            P("dp", "tensor"),
            P("tensor", "dp"),
            P(None, ("dp", "tensor")),
            P(None, ("dp", "tensor")),
        ),
        check_vma=False,
    )
```

```python
import functools
import math

import jax
import jax.numpy as jnp
import numpy as np
from jax import lax
from jax.experimental import pallas as pl
from jax.experimental.pallas import tpu as pltpu
from jax.sharding import PartitionSpec as P

DH = 64
SEQ = 2048
EPS = 1e-05
PART = 32
F32 = jnp.float32
BF16 = jnp.bfloat16
LANES = 128
NT = (((1,), (1,)), ((), ()))
TN = (((0,), (0,)), ((), ()))
ANY = pl.BlockSpec(memory_space=pl.ANY)


def params(mebibytes=60):
    return pltpu.CompilerParams(vmem_limit_bytes=mebibytes * 2**20)


def cost(micros):
    return pl.CostEstimate(flops=int(micros * 1.1e9), bytes_accessed=2**16, transcendentals=0)


def shaped(shape, kind):
    return jax.ShapeDtypeStruct(shape, kind)


def fixed(shape):
    return pl.BlockSpec(shape, lambda *unused: (0,) * len(shape))


def gate(field, *deps, micros=0):
    return pl.pallas_call(
        lambda *refs: None,
        in_specs=[ANY] * (1 + len(deps)),
        out_specs=ANY,
        out_shape=shaped(field.shape, field.dtype),
        input_output_aliases={0: 0},
        cost_estimate=cost(micros),
        name="gate",
    )(field, *deps)


def swap(field, axis, bit):
    size = lax.axis_size(axis)
    return lax.ppermute(field, axis, [(i, i ^ bit) for i in range(size)])


def core_swap(field):
    return swap(field, "tensor", 1)


def y_swap(field):
    return swap(field, "tensor", 2)


def total(addends):
    return sum(a.astype(F32) for a in addends)


def diagonal_swap(field, dp_bits, tensor_bits):
    mask = 4 * dp_bits + tensor_bits
    size = 4 * lax.axis_size("dp")
    return lax.ppermute(field, ("dp", "tensor"), [(i, i ^ mask) for i in range(size)])


def move_rows(number, sources, targets, moves, name):
    def kernel(number_ref, *refs):
        source_refs, target_refs, sems = refs[: len(sources)], refs[len(sources) : -1], refs[-1]
        copies = []
        for at, (source, begin, target, end, rows) in enumerate(moves):
            begin, end = (pl.multiple_of(f(number_ref[0]), 16) for f in (begin, end))
            copies.append(
                pltpu.make_async_copy(
                    source_refs[source].at[pl.ds(begin, rows)], target_refs[target].at[pl.ds(end, rows)], sems.at[at]
                )
            )
        for copy in copies:
            copy.start()
        for copy in copies:
            copy.wait()

    return pl.pallas_call(
        kernel,
        grid_spec=pltpu.PrefetchScalarGridSpec(
            num_scalar_prefetch=1,
            grid=(1,),
            in_specs=[ANY] * len(sources),
            out_specs=[fixed(t) for t in targets],
            scratch_shapes=[pltpu.SemaphoreType.DMA((len(moves),))],
        ),
        out_shape=[shaped(t, BF16) for t in targets],
        compiler_params=params(60),
        cost_estimate=cost(1.5),
        name=name,
    )(number, *sources)


def dp_kinds():
    return [1 << k for k in reversed(range(lax.axis_size("dp").bit_length() - 1))]


class Item:
    def __init__(self, left, *arrays):
        self.left = list(left)
        self.addends = [(array, 0, list(left)) for array in arrays]
        self.shape = arrays[0].shape[2:]


def block_index(kinds, bits, free, flips):
    def index(g, own_ref):
        at = 0
        for bit in bits:
            if bit in free:
                value = (g >> (len(free) - 1 - free.index(bit))) & 1
            else:
                value = own_ref[kinds.index(bit)]
                flip = flips(g, bit)
                value = value + flip - 2 * value * flip
            at = 2 * at + value
        return at

    return index


def addend_specs(items, kinds, frees, flips):
    specs, arrays = [], []
    for item, free in zip(items, frees):
        rows, columns = item.shape
        for array, first, bits in item.addends:
            at = block_index(kinds, bits, free, flips)
            fits = array.shape[3] % columns == 0 and first % columns == 0
            block, column = (columns, first // columns) if fits else (array.shape[3], 0)
            specs.append(
                pl.BlockSpec((1, 1, rows, block), lambda g, own_ref, at=at, column=column: (at(g, own_ref), 0, 0, column))
            )
            arrays.append(array)
    return specs, arrays


def sums_of(items, refs):
    refs = iter(refs)
    fields = []
    for item in items:
        terms = []
        for array, first, bits in item.addends:
            ref = next(refs)
            begin = first if ref.shape[3] > item.shape[1] else 0
            terms.append(ref[0, 0, :, begin : begin + item.shape[1]])
        fields.append(total(terms))
    return fields


def put_beside(out_ref, fields):
    begin = 0
    for field in fields:
        out_ref[0, 0, :, begin : begin + field.shape[1]] = field.astype(BF16)
        begin += field.shape[1]


def received(items, got, lefts):
    begin = 0
    for item, left in zip(items, lefts):
        item.addends.append((got, begin, list(left)))
        begin += item.shape[1]


def packed(items):
    return (1, items[0].shape[0], sum(item.shape[1] for item in items))


def halve(owns, items, kind, *deps):
    kinds = ["y"] + dp_kinds()
    frees = [[b for b in item.left if b != kind] for item in items]
    steps = 2 ** len(frees[0])
    specs, arrays = addend_specs(items, kinds, frees, lambda g, bit: 1 if bit == kind else 0)
    shape = packed(items)

    def kernel(own_ref, *refs):
        put_beside(refs[-1], sums_of(items, refs))

    sent = pl.pallas_call(
        kernel,
        grid_spec=pltpu.PrefetchScalarGridSpec(
            num_scalar_prefetch=1,
            grid=(steps,),
            in_specs=specs + [ANY] * len(deps),
            out_specs=pl.BlockSpec((1,) + shape, lambda g, own_ref: (g, 0, 0, 0)),
        ),
        out_shape=shaped((steps,) + shape, BF16),
        compiler_params=params(60),
        cost_estimate=cost(3),
        name="halve",
    )(owns, *arrays, *deps)
    got = y_swap(sent) if kind == "y" else swap(sent, "dp", kind)
    received(items, got, frees)
    for item, free in zip(items, frees):
        item.left = free
    return sent


def send_last(owns, items, *deps):
    pair = max((item.left for item in items), key=len)[-2:] if "y" not in items[0].left else ["y", 4]
    for item in items:
        while [b for b in item.left if b not in pair]:
            deps = (halve(owns, [item], [b for b in item.left if b not in pair][0], *deps),)
    kinds = ["y"] + dp_kinds()
    first, second = pair
    flips = lambda g, bit: (g + 1) // 2 if bit == first else ((g + 1) % 2 if bit == second else 0)
    specs, arrays = addend_specs(items, kinds, [[] for item in items], flips)
    masks = [[second], [first], [first, second]]
    takers = [[i for i, item in enumerate(items) if all(b in item.left for b in mask)] for mask in masks]
    shapes = [(1,) + packed([items[i] for i in taker]) for taker in takers]

    def kernel(own_ref, *refs):
        fields = sums_of(items, refs)
        for k, taker in enumerate(takers):

            @pl.when(pl.program_id(0) == k)
            def _(k=k, taker=taker):
                put_beside(refs[k - 3], [fields[i] for i in taker])

    sent = pl.pallas_call(
        kernel,
        grid_spec=pltpu.PrefetchScalarGridSpec(
            num_scalar_prefetch=1,
            grid=(3,),
            in_specs=specs + [ANY] * len(deps),
            out_specs=[fixed(shape) for shape in shapes],
        ),
        out_shape=[shaped(shape, BF16) for shape in shapes],
        compiler_params=params(60),
        cost_estimate=cost(2),
        name="send_last",
    )(owns, *arrays, *deps)
    for field, mask, taker in zip(sent, masks, takers):
        got = diagonal_swap(field, sum(b for b in mask if b != "y"), 2 if "y" in mask else 0)
        received([items[i] for i in taker], got, [[]] * len(taker))
    for item in items:
        item.left = []
    return sent[-1]


def finals(owns, groups, *deps):
    kinds = ["y"] + dp_kinds()
    items = [item for group in groups for item, turned in group]
    specs, arrays = addend_specs(items, kinds, [[] for item in items], lambda g, bit: 0)
    shapes = []
    for group in groups:
        rows, columns = group[0][0].shape
        shapes.append((columns * len(group), rows) if group[0][1] else (rows, columns * len(group)))

    def kernel(own_ref, *refs):
        fields = iter(sums_of(items, refs))
        for group, out_ref in zip(groups, refs[-len(groups) :]):
            for i, (item, turned) in enumerate(group):
                cut = slice(i * item.shape[1], (i + 1) * item.shape[1])
                field = next(fields)
                if turned:
                    out_ref[cut, :] = jnp.transpose(field)
                else:
                    out_ref[:, cut] = field

    return pl.pallas_call(
        kernel,
        grid_spec=pltpu.PrefetchScalarGridSpec(
            num_scalar_prefetch=1,
            grid=(1,),
            in_specs=specs + [ANY] * len(deps),
            out_specs=[fixed(shape) for shape in shapes],
        ),
        out_shape=[shaped(shape, F32) for shape in shapes],
        compiler_params=params(60),
        cost_estimate=cost(3),
        name="finals",
    )(owns, *arrays, *deps)


def normalize(field):
    mean = jnp.mean(field, axis=-1, keepdims=True)
    centred = field - mean
    inverse = lax.rsqrt(jnp.mean(centred * centred, axis=-1, keepdims=True) + EPS)
    return centred * inverse, inverse


def norm_back(grad, unit, inverse, gain):
    scaled = grad * gain
    mean_one = jnp.mean(scaled, axis=-1, keepdims=True)
    mean_two = jnp.mean(scaled * unit, axis=-1, keepdims=True)
    return inverse * (scaled - mean_one - unit * mean_two)


def rotary_tables():
    half = DH // 2
    frequency = np.exp(np.arange(half, dtype=np.float32) * np.float32(-math.log(10000.0) / half))
    angles = np.arange(SEQ, dtype=np.float32)[:, None] * frequency.astype(np.float32)[None, :]
    cosine, sine = np.cos(angles), np.sin(angles)
    return (
        jnp.asarray(np.concatenate([cosine] * 4, axis=1).astype(np.float32)),
        jnp.asarray(np.concatenate([-sine, sine, -sine, sine], axis=1).astype(np.float32)),
    )


def lanes_of(shape):
    return lax.broadcasted_iota(jnp.int32, shape, 1)


def partner_lanes(field):
    lane = lanes_of(field.shape)
    return jnp.where(lane % DH < DH // 2, pltpu.roll(field, 96, 1), pltpu.roll(field, 32, 1))


def rotate(field, cosine, sine):
    return field * cosine + partner_lanes(field) * sine


def rotate_back(field, cosine, sine):
    return field * cosine - partner_lanes(field) * sine


def split_three(field):
    high = field.astype(BF16).astype(F32)
    rest = field - high
    middle = rest.astype(BF16).astype(F32)
    return high, middle, rest - middle


def product(left, right):
    return jnp.dot(left, right, preferred_element_type=F32)


def product_nt(left, right):
    return lax.dot_general(left, right, NT, preferred_element_type=F32)


def column_sum(field):
    return jnp.sum(field, axis=0, keepdims=True)


def project_kernel(x_ref, w_ref, gain_ref, bias_ref, cos_ref, sin_ref, *more):
    n_ref, q_ref, k_ref, v_ref, normed_ref = more[-5:]
    rows, width = x_ref.shape
    for i in range(rows // PART):
        r = slice(i * PART, (i + 1) * PART)
        unit, unused = normalize(x_ref[r, :].astype(F32))
        normed_ref[r, :] = (unit * gain_ref[0:1, :] + bias_ref[0:1, :]).astype(BF16)
    for i in range(width // 256):
        c = slice(i * 256, (i + 1) * 256)
        n_ref[c, :] = jnp.transpose(normed_ref[:, c])
    lane = lanes_of((PART, LANES))
    ones = jnp.where(lane < DH + 3, 1.0, 0.0)
    for which, out_ref in enumerate((q_ref, k_ref, v_ref)):
        both = product(normed_ref[...], w_ref[which])
        for i in range(rows // PART):
            r = slice(i * PART, (i + 1) * PART)
            for pair in range(both.shape[1] // LANES):
                field = both[r, pair * LANES : (pair + 1) * LANES]
                if which < 2:
                    field = rotate(field, cos_ref[r, :], sin_ref[r, :])
                if which == 0:
                    field = field * (1.0 / math.sqrt(DH))
                extra = jnp.zeros_like(field) if which == 0 else ones
                out_ref[2 * pair, r, :] = jnp.where(lane < DH, field, extra).astype(BF16)
                out_ref[2 * pair + 1, r, :] = jnp.where(lane < DH, pltpu.roll(field, DH, 1), extra).astype(BF16)


def project(inputs, w_qkv, gain, bias, cosine, sine, *deps):
    block = 256
    tokens, width = inputs.shape
    local = w_qkv.shape[2]
    heads = local // DH
    rows = lambda i: (i, 0)
    per_head = pl.BlockSpec((heads, block, LANES), lambda i: (0, i, 0))
    headed = shaped((heads, tokens, LANES), BF16)
    return pl.pallas_call(
        project_kernel,
        grid=(tokens // block,),
        in_specs=[
            pl.BlockSpec((block, width), rows),
            fixed((3, width, local)),
            fixed((4, width)),
            fixed((4, width)),
            pl.BlockSpec((block, LANES), rows),
            pl.BlockSpec((block, LANES), rows),
        ]
        + [ANY] * len(deps),
        out_specs=[pl.BlockSpec((width, block), lambda i: (0, i)), per_head, per_head, per_head],
        out_shape=[shaped((width, tokens), BF16), headed, headed, headed],
        scratch_shapes=[pltpu.VMEM((block, width), BF16)],
        compiler_params=params(60),
        cost_estimate=cost(10),
        name="project",
    )(inputs, w_qkv, gain, bias, cosine, sine, *deps)


ROWS = 512
KEYS = 512
STRIP = 256


def hidden_keys(shape, down, across):
    return lax.broadcasted_iota(jnp.int32, shape, 0) + down > lax.broadcasted_iota(jnp.int32, shape, 1) + across


def attend_block(n, place_ref, q_ref, k_ref, v_ref, out_refs, qa_ref, score_ref, chance_ref):
    start, end = n * ROWS, (n + 1) * ROWS
    row = lax.broadcasted_iota(jnp.int32, (LANES, ROWS), 0)
    lane = lanes_of((ROWS, LANES))
    outs = []
    for h in range(2):
        most = None
        for begin in range(0, end, STRIP):
            scores = product_nt(k_ref[h, begin : begin + STRIP, :], q_ref[h])
            if begin >= start:
                scores = jnp.where(hidden_keys((STRIP, ROWS), begin, start), -1e30, scores)
            score_ref[h, begin : begin + STRIP, :] = scores
            for i in range(0, STRIP, 8):
                most = scores[i : i + 8] if most is None else jnp.maximum(most, scores[i : i + 8])
        top = jnp.max(most, axis=0, keepdims=True)
        for begin in range(0, end, PART):
            r = slice(begin, begin + PART)
            chance_ref[h, r, :] = jnp.exp(score_ref[h, r, :] - top).astype(BF16)
        both = lax.dot_general(v_ref[h, :end, :], chance_ref[h, :end, :], TN, preferred_element_type=F32)
        summed = both[DH : DH + 1, :]
        high, middle, low = split_three(-(top + jnp.log(summed)))
        extra = jnp.where(row == DH + 1, middle, jnp.where(row == DH + 2, low, 0.0))
        extra = jnp.where(row == DH, high, extra)
        turned = jnp.transpose(jnp.where(row < DH, both * (1.0 / summed), extra))
        qa_ref[h] = jnp.where(lane < DH, q_ref[h].astype(F32), turned).astype(BF16)
        outs.append(turned)
    both = jnp.where(lane < DH, outs[0], pltpu.roll(outs[1], DH, 1)).astype(BF16)
    for which, out_ref in enumerate(out_refs):

        @pl.when((place_ref[0] ^ which) == n)
        def _(out_ref=out_ref):
            out_ref[...] = both


def attend_kernel(place_ref, q_ref, k_ref, v_ref, *more):
    block = pl.program_id(0)
    keys_ref, values_ref = more[-2:]
    for n in range(SEQ // ROWS):

        @pl.when(block == n)
        def _(n=n):
            keys_ref[:, n * ROWS : (n + 1) * ROWS, :] = k_ref[...]
            values_ref[:, n * ROWS : (n + 1) * ROWS, :] = v_ref[...]
            attend_block(n, place_ref, q_ref, keys_ref, values_ref, more[-9:-5], *more[-5:-2])


def attend(pair, place, query, key_rows, value_rows, before, *deps):
    part = pl.BlockSpec((2, ROWS, LANES), lambda i, t: (pair, i, 0))
    return pl.pallas_call(
        attend_kernel,
        grid_spec=pltpu.PrefetchScalarGridSpec(
            num_scalar_prefetch=1,
            grid=(SEQ // ROWS,),
            in_specs=[part, part, part]
            + [ANY] * (len(before) + len(deps)),
            out_specs=[pl.BlockSpec((ROWS, LANES), lambda i, t: (0, pair))] * 4
            + [pl.BlockSpec((2, ROWS, LANES), lambda i, t: (0, i, 0))],
            scratch_shapes=[pltpu.VMEM((2, SEQ, ROWS), F32), pltpu.VMEM((2, SEQ, ROWS), BF16)]
            + [pltpu.VMEM((2, SEQ, LANES), BF16)] * 2,
        ),
        out_shape=[shaped((ROWS, 2 * LANES), BF16)] * 4 + [shaped((2, SEQ, LANES), BF16)],
        input_output_aliases={4 + k: k for k in range(len(before))},
        compiler_params=params(60),
        cost_estimate=cost(10),
        name="attend",
    )(place, query, key_rows, value_rows, *before, *deps)


def back_block(j, k_ref, v_ref, qa_ref, cos_ref, sin_ref, pg_ref, da_ref, dq_ref, chance_ref, score_ref):
    start, length = j * KEYS, SEQ - j * KEYS
    rows = slice(start, start + KEYS)
    lane = lanes_of((KEYS, LANES))
    key_grads, value_grads = [], []
    for h in range(2):
        keys, values = k_ref[h], v_ref[h]
        for begin in range(0, length, KEYS):
            cut = slice(begin, begin + KEYS)
            scores = product_nt(keys, qa_ref[h, start + begin : start + begin + KEYS, :])
            chance_grad = product_nt(values, da_ref[h, start + begin : start + begin + KEYS, :])
            for i in range(0, KEYS, 64):
                r = slice(i, i + 64)
                chance = jnp.exp(scores[r])
                if begin == 0:
                    chance = jnp.where(hidden_keys((64, KEYS), i, 0), 0.0, chance)
                chance_ref[h, r, cut] = chance.astype(BF16)
                score_ref[h, r, cut] = (chance * chance_grad[r]).astype(BF16)
        value_grads.append(product(chance_ref[h, :, :length], da_ref[h, start:, :]))
        key_grads.append(product(score_ref[h, :, :length], qa_ref[h, start:, :]))
        turned = lax.dot_general(keys[:, :DH], score_ref[h, :, :length], TN, preferred_element_type=F32)
        if j == 0:
            dq_ref[h] = turned
        else:
            dq_ref[h, :, start:] += turned
    key_grad = jnp.where(lane < DH, key_grads[0], pltpu.roll(key_grads[1], DH, 1))
    value_grad = jnp.where(lane < DH, value_grads[0], pltpu.roll(value_grads[1], DH, 1))
    pg_ref[:, LANES : 2 * LANES] = rotate_back(key_grad, cos_ref[...], sin_ref[...]).astype(BF16)
    pg_ref[:, 2 * LANES :] = value_grad.astype(BF16)
    for begin in range(0, KEYS, 256):
        cut = slice(begin, begin + 256)
        turned = [dq_ref[h, :, start + begin : start + begin + 256] for h in range(2)]
        field = jnp.transpose(jnp.concatenate(turned, axis=0)) * (1.0 / math.sqrt(DH))
        pg_ref[cut, :LANES] = rotate_back(field, cos_ref[cut, :], sin_ref[cut, :]).astype(BF16)


def back_kernel(place_ref, k_ref, v_ref, qa_ref, g0, g1, g2, g3, o0, o1, o2, o3, cos_ref, sin_ref, *more):
    pg_ref, da_ref, turned_ref, chance_ref, score_ref = more[-5:]
    step = pl.program_id(0)
    steps = SEQ // KEYS
    span = 64

    @pl.when(step == 0)
    def _():
        lane = lanes_of((span, LANES))
        for which, (grad_ref, out_ref) in enumerate(((g0, o0), (g1, o1), (g2, o2), (g3, o3))):
            begin = (place_ref[0] ^ which) * (SEQ // 4)
            for i in range(SEQ // 4 // span):
                rows = pl.ds(pl.multiple_of(begin + i * span, span), span)
                part = slice(i * span, (i + 1) * span)
                grad = grad_ref[part, :].astype(F32)
                both = grad * out_ref[part, :].astype(F32)
                for h in range(2):
                    inner = jnp.sum(jnp.where(lane // DH == h, both, 0.0), axis=1, keepdims=True)
                    high, middle, low = split_three(-inner)
                    own = grad if h == 0 else pltpu.roll(grad, DH, 1)
                    extra = jnp.where(lane == DH + 1, middle, jnp.where(lane == DH + 2, low, 0.0))
                    extra = jnp.where(lane == DH, high, extra)
                    da_ref[h, rows, :] = jnp.where(lane < DH, own, extra).astype(BF16)

    for j in range(steps):
        pl.when(step == j)(
            functools.partial(
                back_block, j, k_ref, v_ref, qa_ref, cos_ref, sin_ref, pg_ref, da_ref, turned_ref, chance_ref,
                score_ref,
            )
        )


def attend_back(pair, place, key_rows, value_rows, query_more, grads, outs, cosine, sine, *deps):
    keyed = pl.BlockSpec((2, KEYS, LANES), lambda i, s: (pair, i, 0))
    last = lambda g: g.shape[1] // LANES - 2
    quarters = [pl.BlockSpec((SEQ // 4, LANES), lambda i, s, at=last(g): (0, at + pair)) for g in (*grads, *outs)]
    table = pl.BlockSpec((KEYS, LANES), lambda i, s: (i, 0))
    return pl.pallas_call(
        back_kernel,
        grid_spec=pltpu.PrefetchScalarGridSpec(
            num_scalar_prefetch=1,
            grid=(SEQ // KEYS,),
            in_specs=[keyed, keyed, fixed((2, SEQ, LANES))] + quarters + [table, table] + [ANY] * len(deps),
            out_specs=pl.BlockSpec((KEYS, 3 * LANES), lambda i, s: (i, 0)),
            scratch_shapes=[
                pltpu.VMEM((2, SEQ, LANES), BF16),
                pltpu.VMEM((2, DH, SEQ), F32),
                pltpu.VMEM((2, KEYS, SEQ), BF16),
                pltpu.VMEM((2, KEYS, SEQ), BF16),
            ],
        ),
        out_shape=shaped((SEQ, 3 * LANES), BF16),
        compiler_params=params(60),
        cost_estimate=cost(0.5),
        name="attend_back",
    )(place, key_rows, value_rows, query_more, *grads, *outs, cosine, sine, *deps)


CHUNK = 512
HALF = 256
SCALE = math.sqrt(2.0 / math.pi)
CUBIC = 0.044715


def feed_kernel(place_ref, *refs):
    parts_in = refs[:4]
    x_ref, cot_ref, weight_ref, gain_ref, bias_ref = refs[4:9]
    (w_out, out_sib), (up_sib, w_up), (both_sib_y, both_y), downs = refs[9:11], refs[11:13], refs[13:15], refs[15:19]
    down_ref, up_ref, out_ref, own_act, own_hidden, final_ref, state_ref, sum_ref = refs[19:27]
    out_w, up_w, down_w, slope_ref, mid_ref, aunit_ref, munit_ref, ainv_ref, minv_ref, sums, sems = refs[30:]
    tokens, width = x_ref.shape
    local = out_w.shape[1]
    outs = [w_out, both_y.at[pl.ds(width, local)], out_sib, both_sib_y.at[pl.ds(width, local)]]
    ups = [up_sib, both_sib_y.at[pl.ds(0, width)], w_up, both_y.at[pl.ds(0, width)]]
    features = [refs[27], refs[28], down_ref.at[:, 3 * width :], refs[29]]
    mlp_ref, sib_act = down_ref.at[:, 0:width], down_ref.at[:, width : 3 * width]
    mn_ref, sib_hidden = up_ref.at[:, 0:width], up_ref.at[:, width : 3 * width]
    branch_ref = out_ref.at[:, 0:width]
    out_ref[:, width:] = parts_in[3][...]

    loads = []
    for at, (sources, target) in enumerate(((outs, out_w), (ups, up_w), (downs, down_w))):
        for k, source in enumerate(sources):
            loads.append(pltpu.make_async_copy(source, target.at[k], sems.at[4 * at + k]))
    for load in loads:
        load.start()
    sums[...] = jnp.zeros_like(sums)

    def add_sum(k, field):
        part = field[0:8]
        for i in range(8, field.shape[0], 8):
            part = part + field[i : i + 8]
        sums[k] += part

    halves = [range(h, h + HALF, PART) for h in range(0, tokens, HALF)]

    for load in loads[:4]:
        load.wait()
    for parts in halves:
        rows = slice(parts.start, parts.stop)
        branch = None
        for k, part_ref in enumerate(parts_in):
            term = product(part_ref[rows, :], out_w[k])
            branch = term if branch is None else branch + term
        for begin in parts:
            r = slice(begin, begin + PART)
            aunit, ainv = normalize(branch[begin - parts.start : begin - parts.start + PART])
            middle = x_ref[r, :].astype(F32) + aunit * gain_ref[1:2, :] + bias_ref[1:2, :]
            munit, minv = normalize(middle)
            mid_ref[r, :] = middle
            aunit_ref[r, :] = aunit
            munit_ref[r, :] = munit
            ainv_ref[r, :] = jnp.broadcast_to(ainv, (PART, LANES))
            minv_ref[r, :] = jnp.broadcast_to(minv, (PART, LANES))
            mn_ref[r, :] = (munit * gain_ref[2:3, :] + bias_ref[2:3, :]).astype(BF16)

    for k in range(4):
        loads[4 + k].wait()
        act_ref, columns = (sib_act, own_act)[k // 2], slice(k % 2 * width, (k % 2 + 1) * width)
        for parts in halves:
            value = product(mn_ref[parts.start : parts.stop, :], up_w[k])
            for i in range(0, HALF, 16):
                r = slice(parts.start + i, parts.start + i + 16)
                v = value[i : i + 16]
                square = v * v
                bent = jnp.tanh(v * (SCALE + (SCALE * CUBIC) * square))
                half = 0.5 + 0.5 * bent
                act_ref[r, columns] = (v * half).astype(BF16)
                slope = half + v * (1.0 - bent * bent) * (0.5 * SCALE + (1.5 * SCALE * CUBIC) * square)
                slope_ref[k, r, :] = slope.astype(BF16)

    for load in loads[8:]:
        load.wait()
    for parts in halves:
        rows = slice(parts.start, parts.stop)
        branch = None
        for k in range(4):
            act_ref, columns = (sib_act, own_act)[k // 2], slice(k % 2 * width, (k % 2 + 1) * width)
            term = product(act_ref[rows, columns], down_w[k])
            branch = term if branch is None else branch + term
        for begin in parts:
            r = slice(begin, begin + PART)
            unit, inverse = normalize(branch[begin - parts.start : begin - parts.start + PART])
            final_ref[r, :] = (mid_ref[r, :] + unit * gain_ref[3:4, :] + bias_ref[3:4, :]).astype(BF16)
            grad = cot_ref[r, :].astype(F32) * weight_ref[r, :1]
            add_sum(3, grad * unit)
            add_sum(7, grad)
            mlp_ref[r, :] = norm_back(grad, unit, inverse, gain_ref[3:4, :]).astype(BF16)

    mid_grads = []
    for parts in halves:
        rows = slice(parts.start, parts.stop)
        mid_grad = None
        for k in range(4):
            hid_ref, columns = (sib_hidden, own_hidden)[k // 2], slice(k % 2 * width, (k % 2 + 1) * width)
            act_grad = product_nt(mlp_ref[rows, :], down_w[k])
            hidden = (slope_ref[k, rows, :].astype(F32) * act_grad).astype(BF16)
            hid_ref[rows, columns] = hidden
            term = product_nt(hidden, up_w[k])
            mid_grad = term if mid_grad is None else mid_grad + term
        mid_grads.append(mid_grad)
    for parts, mid_all in zip(halves, mid_grads):
        rows = slice(parts.start, parts.stop)
        for begin in parts:
            r = slice(begin, begin + PART)
            mid_grad, munit, aunit = mid_all[begin - parts.start : begin - parts.start + PART], munit_ref[r, :], aunit_ref[r, :]
            grad = cot_ref[r, :].astype(F32) * weight_ref[r, :1]
            state = grad + norm_back(mid_grad, munit, minv_ref[r, :1], gain_ref[2:3, :])
            state_ref[r, :] = state
            branch_ref[r, :] = norm_back(state, aunit, ainv_ref[r, :1], gain_ref[1:2, :]).astype(BF16)
            for k, term in ((1, state * aunit), (2, mid_grad * munit), (5, state), (6, mid_grad)):
                add_sum(k, term)
        for k in (1, 2, 3, 0):
            features[k][rows, :] = product_nt(branch_ref[rows, :], out_w[k]).astype(BF16)
    for k in range(8):
        sum_ref[k : k + 1, :] = column_sum(sums[k])


def feed(place, parts, inputs, cot, weight, gains, biases, outs, ups, both, downs):
    width = inputs.shape[1]
    quarter = inputs.shape[0] // 4
    hid = 2 * width
    local = outs[0].shape[0]
    in_place = lambda s, t: (t[0], 0)
    stat = fixed((quarter, LANES))
    part = (quarter, local)
    shapes = [(quarter, 3 * width + local), (quarter, 3 * width), (quarter, width + local)] + [(quarter, hid)] * 2 + [(quarter, width)] * 2
    kinds = [BF16] * 6 + [F32]
    shapes, kinds = shapes + [(8, width)] + [part] * 3, kinds + [F32] + [BF16] * 3
    return pl.pallas_call(
        feed_kernel,
        grid_spec=pltpu.PrefetchScalarGridSpec(
            num_scalar_prefetch=1,
            grid=(1,),
            in_specs=[fixed(part)] * 4
            + [pl.BlockSpec((quarter, width), in_place)] * 2
            + [stat, fixed((4, width)), fixed((4, width))]
            + [ANY] * 10,
            out_specs=[fixed(shape) for shape in shapes],
            scratch_shapes=[
                pltpu.VMEM((4, local, width), BF16),
                pltpu.VMEM((4, width, width), BF16),
                pltpu.VMEM((4, width, width), BF16),
                pltpu.VMEM((4, quarter, width), BF16),
            ]
            + [pltpu.VMEM((quarter, width), F32)] * 3
            + [pltpu.VMEM((quarter, LANES), F32)] * 2
            + [pltpu.VMEM((8, 8, width), F32), pltpu.SemaphoreType.DMA((12,))],
        ),
        out_shape=[shaped(shape, kind) for shape, kind in zip(shapes, kinds)],
        compiler_params=params(60),
        cost_estimate=cost(34),
        name="feed",
    )(place, *parts, inputs, cot, weight, gains, biases, *outs, *ups, *both, *downs)


def keep_and_send(own, bit, field, keep_ref, send_ref):
    blocks, rows = send_ref.shape[0], send_ref.shape[2]
    for j in range(blocks):
        low = j // bit * 2 * bit + j % bit
        for ref, value in ((keep_ref, own), (send_ref, 1 - own)):
            begin = pl.multiple_of((low + value * bit) * rows, 16)
            ref[j, 0] = field[pl.ds(begin, rows), :]


def weight_kernel(bits, own_ref, x1, x2, y1, y2, *more):
    outs, field_ref = more[-5:-1], more[-1]
    step = pl.program_id(0)
    field = lax.dot_general(x1[...], y1[...], TN, preferred_element_type=F32)
    field = field + lax.dot_general(x2[...], y2[...], TN, preferred_element_type=F32)
    field_ref[...] = field.astype(BF16)
    for half, bit in enumerate(bits):
        keep_ref, send_ref = outs[2 * half : 2 * half + 2]
        if bit == "y":
            rows = keep_ref.shape[2]
            for k, ref in enumerate((keep_ref, send_ref)):

                @pl.when(step == 2 * half + k)
                def _(ref=ref):
                    for j in range(ref.shape[0]):
                        ref[j, 0] = field_ref[j * rows : (j + 1) * rows, :]

        else:

            @pl.when(step // 2 == half)
            def _(bit=bit, keep_ref=keep_ref, send_ref=send_ref):
                keep_and_send(own_ref[own_ref.shape[0] - bit], bit, field_ref, keep_ref, send_ref)


def weight_grad(own_bits, bits, mine, got, y1, name, *deps):
    rows, width = mine.shape[0], y1.shape[1] // 2
    size = lax.axis_size("dp")
    y_spec = lambda first: pl.BlockSpec((rows, CHUNK), lambda s, o: (0, first + s // 2 + 2 * (s % 2)))
    shape = (size, 1, width // size, CHUNK)
    specs = []
    for half, bit in enumerate(bits):
        if bit == "y":
            specs += [fixed(shape)] * 2
        else:
            part = (size // 2,) + shape[1:]
            specs += [pl.BlockSpec(part, lambda s, o, half=half: (jnp.clip(s - 2 * half, 0, 1), 0, 0, 0))] * 2
    return pl.pallas_call(
        functools.partial(weight_kernel, bits),
        grid_spec=pltpu.PrefetchScalarGridSpec(
            num_scalar_prefetch=1,
            grid=(4,),
            in_specs=[fixed((rows, width))] * 2 + [y_spec(0), y_spec(width // CHUNK)] + [ANY] * len(deps),
            out_specs=specs,
            scratch_shapes=[pltpu.VMEM((width, CHUNK), BF16)],
        ),
        out_shape=[shaped(shape, BF16)] * 4,
        compiler_params=params(60),
        cost_estimate=cost(0),
        name=name,
    )(own_bits, mine, got, y1, got, *deps)


def out_weight_kernel(mine_ref, got_ref, own_ref, theirs_ref, own_sib_ref, *more):
    width = more[-1].shape[0] * more[-1].shape[2]
    x1, x2 = mine_ref[:, :width], got_ref[:, :width]
    for out_ref, left, right in ((more[-2], own_ref, own_sib_ref), (more[-1], theirs_ref, got_ref.at[:, width:])):
        field = lax.dot_general(x1, left[...], TN, preferred_element_type=F32)
        field = field + lax.dot_general(x2, right[...], TN, preferred_element_type=F32)
        blocks, unused, rows, unused = out_ref.shape
        for j in range(blocks):
            out_ref[j, 0] = field[j * rows : (j + 1) * rows].astype(BF16)


def out_weight_grad(mine, got, own, theirs, own_sib, *deps):
    rows, local = own.shape
    width = mine.shape[1] - local
    size = lax.axis_size("dp")
    shape = (size, 1, width // size, local)
    arrays = [mine, got, own, theirs, own_sib]
    return pl.pallas_call(
        out_weight_kernel,
        grid=(1,),
        in_specs=[fixed(a.shape) for a in arrays] + [ANY] * len(deps),
        out_specs=[fixed(shape)] * 2,
        out_shape=[shaped(shape, BF16)] * 2,
        compiler_params=params(60),
        cost_estimate=cost(0),
        name="out_weight_grad",
    )(*arrays, *deps)


def in_back_kernel(order_ref, p0, p1, w_ref, x_ref, feed_ref, *more):
    send_ref, keep_ref, sum_ref, sums, field_ref = more[-5:]
    step = pl.program_id(0)
    block = x_ref.shape[0]

    @pl.when(step == 0)
    def _():
        sums[...] = jnp.zeros_like(sums)

    field = None
    for c in range(3):
        cut = slice(c * LANES, (c + 1) * LANES)
        left = jnp.concatenate([p0[:, cut], p1[:, cut]], axis=1)
        term = product_nt(left, w_ref[c])
        field = term if field is None else field + term
    gain_part = bias_part = 0.0
    for begin in range(0, block, PART):
        r = slice(begin, begin + PART)
        unit, unused = normalize(x_ref[r, :].astype(F32))
        field_ref[r, :] = field[r].astype(BF16)
        scaled = field[r] * unit
        for i in range(0, PART, 8):
            gain_part = gain_part + scaled[i : i + 8]
            bias_part = bias_part + field[begin + i : begin + i + 8]
    sums[0] += gain_part
    sums[1] += bias_part

    @pl.when(step // 2 % 2 == 0)
    def _():
        send_ref[...] = field_ref[...]

    @pl.when(step // 2 % 2 == 1)
    def _():
        keep_ref[...] = field_ref[...]

    @pl.when(step == 7)
    def _():
        sum_ref[...] = feed_ref[...]
        for k in range(2):
            sum_ref[4 * k : 4 * k + 1, :] = column_sum(sums[k])


def in_back(place, parts, w_qkv, inputs, feed_sums, *deps):
    block = 256
    tokens, width = inputs.shape
    rows = lambda s, o: (2 * (o[0] ^ (3 - s // 2)) + s % 2, 0)
    shapes = [(tokens // 2, width), (tokens // 2, width), (8, width)]
    return pl.pallas_call(
        in_back_kernel,
        grid_spec=pltpu.PrefetchScalarGridSpec(
            num_scalar_prefetch=1,
            grid=(8,),
            in_specs=[pl.BlockSpec((block, 3 * LANES), rows)] * 2
            + [fixed(w_qkv.shape), pl.BlockSpec((block, width), rows), fixed((8, width))]
            + [ANY] * len(deps),
            out_specs=[
                pl.BlockSpec((block, width), lambda s, o: (s // 4 * 2 + jnp.minimum(s % 4, 1), 0)),
                pl.BlockSpec((block, width), lambda s, o: (s // 4 * 2 + jnp.maximum(s % 4 - 2, 0), 0)),
                fixed(shapes[2]),
            ],
            scratch_shapes=[pltpu.VMEM((2, 8, width), F32), pltpu.VMEM((block, width), BF16)],
        ),
        out_shape=[shaped(shapes[0], BF16), shaped(shapes[1], BF16), shaped(shapes[2], F32)],
        compiler_params=params(60),
        cost_estimate=cost(1),
        name="in_back",
    )(place, *parts, w_qkv, inputs, feed_sums, *deps)


def qkv_kernel(own_ref, n_ref, p_ref, *more):
    keep_ref, send_ref, field_ref = more[-3:]
    rows = n_ref.shape[0]
    for k in range(field_ref.shape[0] // rows):

        @pl.when(pl.program_id(0) == k)
        def _(k=k):
            field_ref[k * rows : (k + 1) * rows, :] = product(n_ref[...], p_ref[...]).astype(BF16)

    @pl.when(pl.program_id(0) == pl.num_programs(0) - 1)
    def _():
        keep_and_send(own_ref[own_ref.shape[0] - 3], 4, field_ref, keep_ref, send_ref)


def qkv_grad(own_bits, normed_turned, part, *deps):
    width, tokens = normed_turned.shape
    columns = part.shape[1]
    size = lax.axis_size("dp")
    steps = 2
    shape = (size // 2, 1, width // size, columns)
    return pl.pallas_call(
        qkv_kernel,
        grid_spec=pltpu.PrefetchScalarGridSpec(
            num_scalar_prefetch=1,
            grid=(steps,),
            in_specs=[pl.BlockSpec((width // steps, tokens), lambda i, o: (i, 0)), fixed(part.shape)] + [ANY] * len(deps),
            out_specs=[fixed(shape)] * 2,
            scratch_shapes=[pltpu.VMEM((width, columns), BF16)],
        ),
        out_shape=[shaped(shape, BF16)] * 2,
        compiler_params=params(60),
        cost_estimate=cost(0),
        name="qkv_grad",
    )(own_bits, normed_turned, part, *deps)


def add_kernel(keep_ref, got_ref, *more):
    for begin in range(0, keep_ref.shape[0], PART):
        r = slice(begin, begin + PART)
        more[-1][r, :] = total([keep_ref[r, :], got_ref[r, :]]).astype(BF16)


def add_core(keep, got, *deps):
    rows, width = keep.shape[0] // 2, keep.shape[1]
    block = rows // 2
    spec = pl.BlockSpec((block, width), lambda i: (i, 0))
    return pl.pallas_call(
        add_kernel,
        grid=(2,),
        in_specs=[spec, spec] + [ANY] * len(deps),
        out_specs=spec,
        out_shape=shaped((rows, width), BF16),
        compiler_params=params(60),
        cost_estimate=cost(3),
        name="add_core",
    )(keep, got, *deps)


def finish_kernel(place_ref, x_ref, state_ref, keep_ref, near_ref, far_ref, gain_ref, *more):
    out_ref = more[-1]
    for begin in range(0, x_ref.shape[0], PART):
        r = slice(begin, begin + PART)
        unit, inverse = normalize(x_ref[r, :].astype(F32))
        grad = total([keep_ref[r, :], near_ref[r, :], far_ref[r, :]])
        out_ref[r, :] = state_ref[r, :] + norm_back(grad, unit, inverse, gain_ref[0:1, :])


def finish(place, inputs, state, keep, near, far, gains, *deps):
    quarter, width = state.shape
    block = 128
    steps = quarter // block
    spec = pl.BlockSpec((block, width), lambda s, t: (s, 0))
    return pl.pallas_call(
        finish_kernel,
        grid_spec=pltpu.PrefetchScalarGridSpec(
            num_scalar_prefetch=1,
            grid=(steps,),
            in_specs=[pl.BlockSpec((block, width), lambda s, t: (t[0] * steps + s, 0)), spec]
            + [pl.BlockSpec((block, width), lambda s, t: (steps + s, 0))] * 2
            + [spec]
            + [fixed(gains.shape)]
            + [ANY] * len(deps),
            out_specs=spec,
        ),
        out_shape=shaped((quarter, width), F32),
        compiler_params=params(60),
        cost_estimate=cost(0),
        name="finish",
    )(place, inputs, state, keep, near, far, gains, *deps)


def per_device(
    inputs, w_qkv, w_out, w_up, w_down, norm_gains, norm_biases, out_cot, group_ids, group_weights
):
    tokens, width = inputs.shape
    quarter = tokens // 4
    place = lax.axis_index("tensor")
    where = place.astype(jnp.int32).reshape(1)
    dp_size = lax.axis_size("dp")
    cosine, sine = rotary_tables()

    dp_index = lax.axis_index("dp").astype(jnp.int32)
    mine = (dp_index % 4).reshape(1)
    owns = jnp.stack([jnp.int32(0)] + [(dp_index // kind) % 2 for kind in dp_kinds()])

    own_ids = lax.dynamic_slice_in_dim(group_ids, place * quarter, quarter, 0)
    groups = jnp.arange(group_weights.shape[0], dtype=jnp.int32)
    lookup = (own_ids[:, None] == groups[None, :]).astype(F32)
    row_weight = jnp.sum(lookup * group_weights[None, :], axis=1, keepdims=True)
    row_weight = jnp.broadcast_to(row_weight, (quarter, LANES))

    up_rows, out_rows, down_rows = w_up.shape[0] // 4, w_out.shape[0] // 4, w_down.shape[0] // 4
    zero = lambda m: 0
    up_sent, down_sent = move_rows(
        mine,
        [w_up, w_out, w_down],
        [(up_rows + out_rows, width), (down_rows, width)],
        [
            (0, lambda m: m * up_rows, 0, zero, up_rows),
            (1, lambda m: m * out_rows, 0, lambda m: up_rows, out_rows),
            (2, lambda m: m * down_rows, 1, zero, down_rows),
        ],
        "take",
    )

    def halves(one, two, name):
        rows = one.shape[0] // 2
        moves = [(1, zero, 0, zero, rows), (0, lambda m: rows, 1, zero, rows)]
        low, high = move_rows(mine, [one, two], [(rows, width)] * 2, moves, name)
        return swap(low, "dp", 1), swap(high, "dp", 2), low

    def quarter_moves(target, first, rows, begin, count):
        return [
            (which, lambda m: begin, target, lambda m, which=which: first + (m ^ which) * rows, rows)
            for which in range(count)
        ]

    up_got = y_swap(up_sent)
    up_sib, down_sib, out_sib = core_swap(w_up), core_swap(w_down), core_swap(w_out)
    normed_turned, query, key_rows, value_rows = project(
        inputs, w_qkv, norm_gains, norm_biases, cosine, sine, up_sent
    )
    down_sent = gate(down_sent, normed_turned)
    down_got = y_swap(down_sent)
    up_got = gate(up_got, down_sent)
    up_one, up_two = swap(up_got, "dp", 1), swap(up_got, "dp", 2)

    *outs, more_first = attend(0, where, query, key_rows, value_rows, [], up_got, up_sib, down_sib, out_sib)
    down_got = gate(down_got, outs[0])
    down_one, down_two = swap(down_got, "dp", 1), swap(down_got, "dp", 2)
    up_one = gate(up_one, down_got)
    up_low, up_high, last = halves(up_one, up_two, "up_halves")
    *outs, more_second = attend(1, where, query, key_rows, value_rows, outs, last, down_got)
    rows = [outs[0], core_swap(outs[1]), y_swap(outs[2]), diagonal_swap(outs[3], 0, 3)]
    up_one = gate(up_one, outs[1], outs[2], outs[3])

    def last_moves(target, first, rows, begin, half):
        low = max(0, min(half - begin, rows))
        moves = [(3, lambda m: begin, target, lambda m: first + (m ^ 3) * rows, low)] if low else []
        start = begin + low - half
        return moves + [(4, lambda m: start, target, lambda m: first + (m ^ 3) * rows + low, rows - low)]

    half = (up_rows + out_rows) // 2
    (upout_y,) = move_rows(
        mine,
        [up_got, up_one, up_two, up_low, up_high],
        [(w_up.shape[0] + w_out.shape[0], width)],
        quarter_moves(0, 0, up_rows, 0, 3)
        + quarter_moves(0, w_up.shape[0], out_rows, up_rows, 3)
        + last_moves(0, 0, up_rows, 0, half)
        + last_moves(0, w_up.shape[0], out_rows, up_rows, half),
        "up_whole",
    )
    upout_sib_y = core_swap(upout_y)
    down_one = gate(down_one, upout_y, rows[1])
    down_low, down_high, last = halves(down_one, down_two, "down_halves")
    down_low = gate(down_low, rows[2], rows[3])
    (down_y,) = move_rows(
        mine,
        [down_got, down_one, down_two, down_low, down_high],
        [w_down.shape],
        quarter_moves(0, 0, down_rows, 0, 3) + last_moves(0, 0, down_rows, 0, down_rows // 2),
        "down_whole",
    )
    down_sib_y = core_swap(down_y)

    for_down, for_up, for_out, own_act, own_hidden, final_rows, state_grad, sums_feed, own, for_y, for_far = feed(
        where, [rows[0], rows[2], rows[1], rows[3]], inputs, out_cot, row_weight, norm_gains, norm_biases,
        [w_out, out_sib], [up_sib, w_up], [upout_sib_y, upout_y], [down_sib, down_sib_y, w_down, down_y],
    )

    down_got = core_swap(for_down)
    grads = [own, down_got, y_swap(for_y), diagonal_swap(for_far, 0, 3)]
    for_up = gate(for_up, down_got)
    up_got = core_swap(for_up)
    kinds = dp_kinds()
    both = ["y"] + kinds
    without = lambda bits, *gone: [b for b in bits if b not in gone]
    newest = lambda *items: [item.addends[-1][0] for item in items]
    d0_keep, d0_send, d1_keep, d1_send = weight_grad(
        owns, ("y", 1), for_down, down_got, own_act, "down_grad", for_up
    )
    d0 = Item(kinds, d0_keep, y_swap(d0_send))
    d1 = Item(without(both, 1), d1_keep, swap(d1_send, "dp", 1))
    u0_keep, u0_send, u1_keep, u1_send = weight_grad(
        owns, (1, 2), for_up, up_got, own_hidden, "up_grad", d0_send, d1_send, *grads[2:]
    )
    u1 = Item(without(both, 2), u1_keep, swap(u1_send, "dp", 2))
    for_out = gate(for_out, u1_send)
    out_got = core_swap(for_out)
    part_first = attend_back(
        0, where, key_rows, value_rows, more_first, grads, outs, cosine, sine, u1_send, for_out
    )
    u0_send = gate(u0_send, part_first)
    u0 = Item(without(both, 1), u0_keep, swap(u0_send, "dp", 1))
    out_keep, out_send = out_weight_grad(for_out, out_got, rows[0], rows[2], outs[1], u0_send)
    out_item = Item(kinds, out_keep, y_swap(out_send))

    def qkv_item(part, *deps):
        keep, send = qkv_grad(owns, normed_turned, part, *deps)
        return Item(without(kinds, 4), keep, swap(send, "dp", 4)), send

    q0, last = qkv_item(part_first, out_send)
    last = halve(owns, [d1], 2, last)
    part_second = attend_back(
        1, where, key_rows, value_rows, more_second, grads, outs, cosine, sine, last, *newest(d0, u1)
    )
    part_second = gate(part_second, *newest(u0), micros=3)
    parts = [part_first, part_second]

    send, keep, sums = in_back(where, parts, w_qkv, inputs, sums_feed, *newest(d1, q0, out_item))
    core_got = core_swap(send)
    last = halve(owns, [u1, d0], 1, send)
    last = halve(owns, [u0, out_item], 2, last)
    far = add_core(keep, core_got, last)
    far_got = y_swap(far)
    q1, last = qkv_item(part_second, far)
    last = gate(last, *newest(u1), micros=3)
    last = gate(last, *newest(u0), micros=3)
    last = send_last(owns, [d1, u0, u1], last, far_got)
    last = halve(owns, [q0, q1, out_item], 1, last)
    input_grad = finish(where, inputs, state_grad, keep, core_got, far_got, norm_gains, last)
    share = width // (4 * dp_size)
    sums = gate(sums, input_grad)
    sums = sums.reshape(8, 4 * dp_size, share).transpose(1, 0, 2)
    sums = jnp.sum(lax.all_to_all(sums, ("dp", "tensor"), 0, 0, tiled=True), axis=0)
    last = gate(last, input_grad, sums, *[a[0] for a in u0.addends[-3:]], micros=3)
    last = gate(last, *newest(q0), micros=3)
    last = send_last(owns, [d0, q0, q1, out_item], last)
    up_total, down_total, qkv_total, out_total = finals(
        owns, [[(u0, False), (u1, False)], [(d0, True), (d1, True)], [(q0, False), (q1, False)], [(out_item, True)]], last
    )
    qkv_total = qkv_total.reshape(-1, 2, 3, LANES).transpose(2, 0, 1, 3).reshape(3, -1, 2 * LANES)
    return (
        final_rows,
        input_grad,
        qkv_total,
        out_total,
        up_total,
        down_total,
        sums[:4],
        sums[4:],
    )


def solution(mesh):
    placed = (
        P("dp", None),
        P(None, None, "tensor"),
        P("tensor", None),
        P(None, "tensor"),
        P("tensor", None),
        P(),
        P(),
        P("dp", None),
        P("dp"),
        P(),
    )
    return jax.shard_map(
        per_device,
        mesh=mesh,
        in_specs=placed,
        out_specs=(
            P(("dp", "tensor"), None),
            P(("dp", "tensor"), None),
            P(None, "dp", "tensor"),
            P("tensor", "dp"),
            P("dp", "tensor"),
            P("tensor", "dp"),
            P(None, ("dp", "tensor")),
            P(None, ("dp", "tensor")),
        ),
        check_vma=False,
    )
```

```python
import functools
import math

import jax
import jax.numpy as jnp
import numpy as np
from jax import lax
from jax.experimental import pallas as pl
from jax.experimental.pallas import tpu as pltpu
from jax.sharding import PartitionSpec as P

DH = 64
SEQ = 2048
EPS = 1e-05
PART = 32
F32 = jnp.float32
BF16 = jnp.bfloat16
LANES = 128
NT = (((1,), (1,)), ((), ()))
TN = (((0,), (0,)), ((), ()))
ANY = pl.BlockSpec(memory_space=pl.ANY)


def params(mebibytes=60):
    return pltpu.CompilerParams(vmem_limit_bytes=mebibytes * 2**20)


def cost(micros):
    return pl.CostEstimate(flops=int(micros * 1.1e9), bytes_accessed=2**16, transcendentals=0)


def shaped(shape, kind):
    return jax.ShapeDtypeStruct(shape, kind)


def fixed(shape):
    return pl.BlockSpec(shape, lambda *unused: (0,) * len(shape))


def gate(field, *deps, micros=0):
    return pl.pallas_call(
        lambda *refs: None,
        in_specs=[ANY] * (1 + len(deps)),
        out_specs=ANY,
        out_shape=shaped(field.shape, field.dtype),
        input_output_aliases={0: 0},
        cost_estimate=cost(micros),
        name="gate",
    )(field, *deps)


def swap(field, axis, bit):
    size = lax.axis_size(axis)
    return lax.ppermute(field, axis, [(i, i ^ bit) for i in range(size)])


def core_swap(field):
    return swap(field, "tensor", 1)


def y_swap(field):
    return swap(field, "tensor", 2)


def total(addends):
    return sum(a.astype(F32) for a in addends)


def diagonal_swap(field, dp_bits, tensor_bits):
    mask = 4 * dp_bits + tensor_bits
    size = 4 * lax.axis_size("dp")
    return lax.ppermute(field, ("dp", "tensor"), [(i, i ^ mask) for i in range(size)])


def move_rows(number, sources, targets, moves, name):
    def kernel(number_ref, *refs):
        source_refs, target_refs, sems = refs[: len(sources)], refs[len(sources) : -1], refs[-1]
        copies = []
        for at, (source, begin, target, end, rows) in enumerate(moves):
            begin, end = (pl.multiple_of(f(number_ref[0]), 16) for f in (begin, end))
            copies.append(
                pltpu.make_async_copy(
                    source_refs[source].at[pl.ds(begin, rows)], target_refs[target].at[pl.ds(end, rows)], sems.at[at]
                )
            )
        for copy in copies:
            copy.start()
        for copy in copies:
            copy.wait()

    return pl.pallas_call(
        kernel,
        grid_spec=pltpu.PrefetchScalarGridSpec(
            num_scalar_prefetch=1,
            grid=(1,),
            in_specs=[ANY] * len(sources),
            out_specs=[fixed(t) for t in targets],
            scratch_shapes=[pltpu.SemaphoreType.DMA((len(moves),))],
        ),
        out_shape=[shaped(t, BF16) for t in targets],
        compiler_params=params(60),
        cost_estimate=cost(1.5),
        name=name,
    )(number, *sources)


def dp_kinds():
    return [1 << k for k in reversed(range(lax.axis_size("dp").bit_length() - 1))]


class Item:
    def __init__(self, left, *arrays):
        self.left = list(left)
        self.addends = [(array, 0, list(left)) for array in arrays]
        self.shape = arrays[0].shape[2:]


def block_index(kinds, bits, free, flips):
    def index(g, own_ref):
        at = 0
        for bit in bits:
            if bit in free:
                value = (g >> (len(free) - 1 - free.index(bit))) & 1
            else:
                value = own_ref[kinds.index(bit)]
                flip = flips(g, bit)
                value = value + flip - 2 * value * flip
            at = 2 * at + value
        return at

    return index


def addend_specs(items, kinds, frees, flips):
    specs, arrays = [], []
    for item, free in zip(items, frees):
        rows, columns = item.shape
        for array, first, bits in item.addends:
            at = block_index(kinds, bits, free, flips)
            fits = array.shape[3] % columns == 0 and first % columns == 0
            block, column = (columns, first // columns) if fits else (array.shape[3], 0)
            specs.append(
                pl.BlockSpec((1, 1, rows, block), lambda g, own_ref, at=at, column=column: (at(g, own_ref), 0, 0, column))
            )
            arrays.append(array)
    return specs, arrays


def sums_of(items, refs):
    refs = iter(refs)
    fields = []
    for item in items:
        terms = []
        for array, first, bits in item.addends:
            ref = next(refs)
            begin = first if ref.shape[3] > item.shape[1] else 0
            terms.append(ref[0, 0, :, begin : begin + item.shape[1]])
        fields.append(total(terms))
    return fields


def put_beside(out_ref, fields):
    begin = 0
    for field in fields:
        out_ref[0, 0, :, begin : begin + field.shape[1]] = field.astype(BF16)
        begin += field.shape[1]


def received(items, got, lefts):
    begin = 0
    for item, left in zip(items, lefts):
        item.addends.append((got, begin, list(left)))
        begin += item.shape[1]


def packed(items):
    return (1, items[0].shape[0], sum(item.shape[1] for item in items))


def halve(owns, items, kind, *deps):
    kinds = ["y"] + dp_kinds()
    frees = [[b for b in item.left if b != kind] for item in items]
    steps = 2 ** len(frees[0])
    specs, arrays = addend_specs(items, kinds, frees, lambda g, bit: 1 if bit == kind else 0)
    shape = packed(items)

    def kernel(own_ref, *refs):
        put_beside(refs[-1], sums_of(items, refs))

    sent = pl.pallas_call(
        kernel,
        grid_spec=pltpu.PrefetchScalarGridSpec(
            num_scalar_prefetch=1,
            grid=(steps,),
            in_specs=specs + [ANY] * len(deps),
            out_specs=pl.BlockSpec((1,) + shape, lambda g, own_ref: (g, 0, 0, 0)),
        ),
        out_shape=shaped((steps,) + shape, BF16),
        compiler_params=params(60),
        cost_estimate=cost(3),
        name="halve",
    )(owns, *arrays, *deps)
    got = y_swap(sent) if kind == "y" else swap(sent, "dp", kind)
    received(items, got, frees)
    for item, free in zip(items, frees):
        item.left = free
    return sent


def send_last(owns, items, *deps):
    pair = ["y", 4] if "y" in items[0].left else [4, 2]
    for item in items:
        while [b for b in item.left if b not in pair]:
            deps = (halve(owns, [item], [b for b in item.left if b not in pair][0], *deps),)
    kinds = ["y"] + dp_kinds()
    masks = [[pair[1]], [pair[0]], pair]
    takers = [[i for i, item in enumerate(items) if all(b in item.left for b in mask)] for mask in masks]
    masks, takers = [m for m, t in zip(masks, takers) if t], [t for t in takers if t]

    def flips(g, bit):
        value = 0
        for k, mask in enumerate(masks):
            if bit in mask:
                value = jnp.where(g == k, 1, value)
        return value

    specs, arrays = addend_specs(items, kinds, [[] for item in items], flips)
    shapes = [(1,) + packed([items[i] for i in taker]) for taker in takers]

    def kernel(own_ref, *refs):
        fields = sums_of(items, refs)
        for k, taker in enumerate(takers):

            @pl.when(pl.program_id(0) == k)
            def _(k=k, taker=taker):
                put_beside(refs[k - len(masks)], [fields[i] for i in taker])

    sent = pl.pallas_call(
        kernel,
        grid_spec=pltpu.PrefetchScalarGridSpec(
            num_scalar_prefetch=1,
            grid=(len(masks),),
            in_specs=specs + [ANY] * len(deps),
            out_specs=[fixed(shape) for shape in shapes],
        ),
        out_shape=[shaped(shape, BF16) for shape in shapes],
        compiler_params=params(60),
        cost_estimate=cost(2),
        name="send_last",
    )(owns, *arrays, *deps)
    for field, mask, taker in zip(sent, masks, takers):
        got = diagonal_swap(field, sum(b for b in mask if b != "y"), 2 if "y" in mask else 0)
        received([items[i] for i in taker], got, [[]] * len(taker))
    for item in items:
        item.left = []
    return sent[-1]


def finals(owns, groups, heads, *deps):
    kinds = ["y"] + dp_kinds()
    items = [item for group in groups for item, turned in group] + heads
    specs, arrays = addend_specs(items, kinds, [[] for item in items], lambda g, bit: 0)
    shapes = []
    for group in groups:
        rows, columns = group[0][0].shape
        shapes.append((columns * len(group), rows) if group[0][1] else (rows, columns * len(group)))

    shapes.append((3, heads[0].shape[0], LANES * len(heads)))

    def kernel(own_ref, *refs):
        fields = sums_of(items, refs)
        for at, field in enumerate(fields[-len(heads) :]):
            for c in range(3):
                refs[-1][c, :, at * LANES : (at + 1) * LANES] = field[:, c * LANES : (c + 1) * LANES]
        fields = iter(fields)
        for group, out_ref in zip(groups, refs[-len(groups) - 1 :]):
            for i, (item, turned) in enumerate(group):
                cut = slice(i * item.shape[1], (i + 1) * item.shape[1])
                field = next(fields)
                if turned:
                    out_ref[cut, :] = jnp.transpose(field)
                else:
                    out_ref[:, cut] = field

    return pl.pallas_call(
        kernel,
        grid_spec=pltpu.PrefetchScalarGridSpec(
            num_scalar_prefetch=1,
            grid=(1,),
            in_specs=specs + [ANY] * len(deps),
            out_specs=[fixed(shape) for shape in shapes],
        ),
        out_shape=[shaped(shape, F32) for shape in shapes],
        compiler_params=params(60),
        cost_estimate=cost(3),
        name="finals",
    )(owns, *arrays, *deps)


def normalize(field):
    mean = jnp.mean(field, axis=-1, keepdims=True)
    centred = field - mean
    inverse = lax.rsqrt(jnp.mean(centred * centred, axis=-1, keepdims=True) + EPS)
    return centred * inverse, inverse


def norm_back(grad, unit, inverse, gain):
    scaled = grad * gain
    mean_one = jnp.mean(scaled, axis=-1, keepdims=True)
    mean_two = jnp.mean(scaled * unit, axis=-1, keepdims=True)
    return inverse * (scaled - mean_one - unit * mean_two)


def rotary_tables():
    half = DH // 2
    frequency = np.exp(np.arange(half, dtype=np.float32) * np.float32(-math.log(10000.0) / half))
    angles = np.arange(SEQ, dtype=np.float32)[:, None] * frequency.astype(np.float32)[None, :]
    cosine, sine = np.cos(angles), np.sin(angles)
    return (
        jnp.asarray(np.concatenate([cosine] * 4, axis=1).astype(np.float32)),
        jnp.asarray(np.concatenate([-sine, sine, -sine, sine], axis=1).astype(np.float32)),
    )


def lanes_of(shape):
    return lax.broadcasted_iota(jnp.int32, shape, 1)


def partner_lanes(field):
    lane = lanes_of(field.shape)
    return jnp.where(lane % DH < DH // 2, pltpu.roll(field, 96, 1), pltpu.roll(field, 32, 1))


def rotate(field, cosine, sine):
    return field * cosine + partner_lanes(field) * sine


def rotate_back(field, cosine, sine):
    return field * cosine - partner_lanes(field) * sine


def split_three(field):
    high = field.astype(BF16).astype(F32)
    rest = field - high
    middle = rest.astype(BF16).astype(F32)
    return high, middle, rest - middle


def product(left, right):
    return jnp.dot(left, right, preferred_element_type=F32)


def product_nt(left, right):
    return lax.dot_general(left, right, NT, preferred_element_type=F32)


def column_sum(field):
    return jnp.sum(field, axis=0, keepdims=True)


def project_kernel(x_ref, w_ref, gain_ref, bias_ref, cos_ref, sin_ref, *more):
    n_ref, q_ref, k_ref, v_ref, normed_ref = more[-5:]
    rows, width = x_ref.shape
    for i in range(rows // PART):
        r = slice(i * PART, (i + 1) * PART)
        unit, unused = normalize(x_ref[r, :].astype(F32))
        normed_ref[r, :] = (unit * gain_ref[0:1, :] + bias_ref[0:1, :]).astype(BF16)
    for i in range(width // 256):
        c = slice(i * 256, (i + 1) * 256)
        n_ref[c, :] = jnp.transpose(normed_ref[:, c])
    lane = lanes_of((PART, LANES))
    ones = jnp.where(lane < DH + 3, 1.0, 0.0)
    for which, out_ref in enumerate((q_ref, k_ref, v_ref)):
        both = product(normed_ref[...], w_ref[which])
        for i in range(rows // PART):
            r = slice(i * PART, (i + 1) * PART)
            for pair in range(both.shape[1] // LANES):
                field = both[r, pair * LANES : (pair + 1) * LANES]
                if which < 2:
                    field = rotate(field, cos_ref[r, :], sin_ref[r, :])
                if which == 0:
                    field = field * (1.0 / math.sqrt(DH))
                extra = jnp.zeros_like(field) if which == 0 else ones
                out_ref[2 * pair, r, :] = jnp.where(lane < DH, field, extra).astype(BF16)
                out_ref[2 * pair + 1, r, :] = jnp.where(lane < DH, pltpu.roll(field, DH, 1), extra).astype(BF16)


def project(inputs, w_qkv, gain, bias, cosine, sine, *deps):
    block = 256
    tokens, width = inputs.shape
    local = w_qkv.shape[2]
    heads = local // DH
    rows = lambda i: (i, 0)
    per_head = pl.BlockSpec((heads, block, LANES), lambda i: (0, i, 0))
    headed = shaped((heads, tokens, LANES), BF16)
    return pl.pallas_call(
        project_kernel,
        grid=(tokens // block,),
        in_specs=[
            pl.BlockSpec((block, width), rows),
            fixed((3, width, local)),
            fixed((4, width)),
            fixed((4, width)),
            pl.BlockSpec((block, LANES), rows),
            pl.BlockSpec((block, LANES), rows),
        ]
        + [ANY] * len(deps),
        out_specs=[pl.BlockSpec((width, block), lambda i: (0, i)), per_head, per_head, per_head],
        out_shape=[shaped((width, tokens), BF16), headed, headed, headed],
        scratch_shapes=[pltpu.VMEM((block, width), BF16)],
        compiler_params=params(60),
        cost_estimate=cost(10),
        name="project",
    )(inputs, w_qkv, gain, bias, cosine, sine, *deps)


ROWS = 512
KEYS = 512
STRIP = 256


def hidden_keys(shape, down, across):
    return lax.broadcasted_iota(jnp.int32, shape, 0) + down > lax.broadcasted_iota(jnp.int32, shape, 1) + across


def attend_block(n, place_ref, q_ref, k_ref, v_ref, out_refs, qa_ref, score_ref, chance_ref):
    start, end = n * ROWS, (n + 1) * ROWS
    row = lax.broadcasted_iota(jnp.int32, (LANES, ROWS), 0)
    lane = lanes_of((ROWS, LANES))
    outs = []
    for h in range(2):
        most = None
        for begin in range(0, end, STRIP):
            scores = product_nt(k_ref[h, begin : begin + STRIP, :], q_ref[h])
            if begin >= start:
                scores = jnp.where(hidden_keys((STRIP, ROWS), begin, start), -1e30, scores)
            score_ref[h, begin : begin + STRIP, :] = scores
            for i in range(0, STRIP, 8):
                most = scores[i : i + 8] if most is None else jnp.maximum(most, scores[i : i + 8])
        top = jnp.max(most, axis=0, keepdims=True)
        for begin in range(0, end, PART):
            r = slice(begin, begin + PART)
            chance_ref[h, r, :] = jnp.exp(score_ref[h, r, :] - top).astype(BF16)
        both = lax.dot_general(v_ref[h, :end, :], chance_ref[h, :end, :], TN, preferred_element_type=F32)
        summed = both[DH : DH + 1, :]
        high, middle, low = split_three(-(top + jnp.log(summed)))
        extra = jnp.where(row == DH + 1, middle, jnp.where(row == DH + 2, low, 0.0))
        extra = jnp.where(row == DH, high, extra)
        turned = jnp.transpose(jnp.where(row < DH, both * (1.0 / summed), extra))
        qa_ref[h] = jnp.where(lane < DH, q_ref[h].astype(F32), turned).astype(BF16)
        outs.append(turned)
    both = jnp.where(lane < DH, outs[0], pltpu.roll(outs[1], DH, 1)).astype(BF16)
    for which, out_ref in enumerate(out_refs):

        @pl.when((place_ref[0] ^ which) == n)
        def _(out_ref=out_ref):
            out_ref[...] = both


def attend_kernel(place_ref, q_ref, k_ref, v_ref, *more):
    block = pl.program_id(0)
    keys_ref, values_ref = more[-2:]
    for n in range(SEQ // ROWS):

        @pl.when(block == n)
        def _(n=n):
            keys_ref[:, n * ROWS : (n + 1) * ROWS, :] = k_ref[...]
            values_ref[:, n * ROWS : (n + 1) * ROWS, :] = v_ref[...]
            attend_block(n, place_ref, q_ref, keys_ref, values_ref, more[-9:-5], *more[-5:-2])


def attend(pair, place, query, key_rows, value_rows, before, *deps):
    part = pl.BlockSpec((2, ROWS, LANES), lambda i, t: (pair, i, 0))
    return pl.pallas_call(
        attend_kernel,
        grid_spec=pltpu.PrefetchScalarGridSpec(
            num_scalar_prefetch=1,
            grid=(SEQ // ROWS,),
            in_specs=[part, part, part]
            + [ANY] * (len(before) + len(deps)),
            out_specs=[pl.BlockSpec((ROWS, LANES), lambda i, t: (0, pair))] * 4
            + [pl.BlockSpec((2, ROWS, LANES), lambda i, t: (0, i, 0))],
            scratch_shapes=[pltpu.VMEM((2, SEQ, ROWS), F32), pltpu.VMEM((2, SEQ, ROWS), BF16)]
            + [pltpu.VMEM((2, SEQ, LANES), BF16)] * 2,
        ),
        out_shape=[shaped((ROWS, 2 * LANES), BF16)] * 4 + [shaped((2, SEQ, LANES), BF16)],
        input_output_aliases={4 + k: k for k in range(len(before))},
        compiler_params=params(60),
        cost_estimate=cost(10),
        name="attend",
    )(place, query, key_rows, value_rows, *before, *deps)


def back_block(j, k_ref, v_ref, qa_ref, cos_ref, sin_ref, pg_ref, da_ref, dq_ref, chance_ref, score_ref):
    start, length = j * KEYS, SEQ - j * KEYS
    rows = slice(start, start + KEYS)
    lane = lanes_of((KEYS, LANES))
    key_grads, value_grads = [], []
    for h in range(2):
        keys, values = k_ref[h], v_ref[h]
        for begin in range(0, length, KEYS):
            cut = slice(begin, begin + KEYS)
            scores = product_nt(keys, qa_ref[h, start + begin : start + begin + KEYS, :])
            chance_grad = product_nt(values, da_ref[h, start + begin : start + begin + KEYS, :])
            for i in range(0, KEYS, 64):
                r = slice(i, i + 64)
                chance = jnp.exp(scores[r])
                if begin == 0:
                    chance = jnp.where(hidden_keys((64, KEYS), i, 0), 0.0, chance)
                chance_ref[h, r, cut] = chance.astype(BF16)
                score_ref[h, r, cut] = (chance * chance_grad[r]).astype(BF16)
        value_grads.append(product(chance_ref[h, :, :length], da_ref[h, start:, :]))
        key_grads.append(product(score_ref[h, :, :length], qa_ref[h, start:, :]))
        turned = lax.dot_general(keys[:, :DH], score_ref[h, :, :length], TN, preferred_element_type=F32)
        if j == 0:
            dq_ref[h] = turned
        else:
            dq_ref[h, :, start:] += turned
    key_grad = jnp.where(lane < DH, key_grads[0], pltpu.roll(key_grads[1], DH, 1))
    value_grad = jnp.where(lane < DH, value_grads[0], pltpu.roll(value_grads[1], DH, 1))
    pg_ref[:, LANES : 2 * LANES] = rotate_back(key_grad, cos_ref[...], sin_ref[...]).astype(BF16)
    pg_ref[:, 2 * LANES :] = value_grad.astype(BF16)
    for begin in range(0, KEYS, 256):
        cut = slice(begin, begin + 256)
        turned = [dq_ref[h, :, start + begin : start + begin + 256] for h in range(2)]
        field = jnp.transpose(jnp.concatenate(turned, axis=0)) * (1.0 / math.sqrt(DH))
        pg_ref[cut, :LANES] = rotate_back(field, cos_ref[cut, :], sin_ref[cut, :]).astype(BF16)


def back_kernel(place_ref, k_ref, v_ref, qa_ref, g0, g1, g2, g3, o0, o1, o2, o3, cos_ref, sin_ref, *more):
    pg_ref, da_ref, turned_ref, chance_ref, score_ref = more[-5:]
    step = pl.program_id(0)
    steps = SEQ // KEYS
    span = 64

    @pl.when(step == 0)
    def _():
        lane = lanes_of((span, LANES))
        for which, (grad_ref, out_ref) in enumerate(((g0, o0), (g1, o1), (g2, o2), (g3, o3))):
            begin = (place_ref[0] ^ which) * (SEQ // 4)
            for i in range(SEQ // 4 // span):
                rows = pl.ds(pl.multiple_of(begin + i * span, span), span)
                part = slice(i * span, (i + 1) * span)
                grad = grad_ref[part, :].astype(F32)
                both = grad * out_ref[part, :].astype(F32)
                for h in range(2):
                    inner = jnp.sum(jnp.where(lane // DH == h, both, 0.0), axis=1, keepdims=True)
                    high, middle, low = split_three(-inner)
                    own = grad if h == 0 else pltpu.roll(grad, DH, 1)
                    extra = jnp.where(lane == DH + 1, middle, jnp.where(lane == DH + 2, low, 0.0))
                    extra = jnp.where(lane == DH, high, extra)
                    da_ref[h, rows, :] = jnp.where(lane < DH, own, extra).astype(BF16)

    for j in range(steps):
        pl.when(step == j)(
            functools.partial(
                back_block, j, k_ref, v_ref, qa_ref, cos_ref, sin_ref, pg_ref, da_ref, turned_ref, chance_ref,
                score_ref,
            )
        )


def attend_back(pair, place, key_rows, value_rows, query_more, grads, outs, cosine, sine, *deps):
    keyed = pl.BlockSpec((2, KEYS, LANES), lambda i, s: (pair, i, 0))
    last = lambda g: g.shape[1] // LANES - 2
    quarters = [pl.BlockSpec((SEQ // 4, LANES), lambda i, s, at=last(g): (0, at + pair)) for g in (*grads, *outs)]
    table = pl.BlockSpec((KEYS, LANES), lambda i, s: (i, 0))
    return pl.pallas_call(
        back_kernel,
        grid_spec=pltpu.PrefetchScalarGridSpec(
            num_scalar_prefetch=1,
            grid=(SEQ // KEYS,),
            in_specs=[keyed, keyed, fixed((2, SEQ, LANES))] + quarters + [table, table] + [ANY] * len(deps),
            out_specs=pl.BlockSpec((KEYS, 3 * LANES), lambda i, s: (i, 0)),
            scratch_shapes=[
                pltpu.VMEM((2, SEQ, LANES), BF16),
                pltpu.VMEM((2, DH, SEQ), F32),
                pltpu.VMEM((2, KEYS, SEQ), BF16),
                pltpu.VMEM((2, KEYS, SEQ), BF16),
            ],
        ),
        out_shape=shaped((SEQ, 3 * LANES), BF16),
        compiler_params=params(60),
        cost_estimate=cost(0.5),
        name="attend_back",
    )(place, key_rows, value_rows, query_more, *grads, *outs, cosine, sine, *deps)


CHUNK = 512
HALF = 256
SCALE = math.sqrt(2.0 / math.pi)
CUBIC = 0.044715


def feed_kernel(place_ref, *refs):
    parts_in = refs[:4]
    x_ref, cot_ref, weight_ref, gain_ref, bias_ref = refs[4:9]
    (w_out, out_sib), (up_sib, w_up), (both_sib_y, both_y), downs = refs[9:11], refs[11:13], refs[13:15], refs[15:19]
    down_ref, up_ref, out_ref, own_act, own_hidden, final_ref, state_ref, sum_ref = refs[19:27]
    out_w, up_w, down_w, slope_ref, mid_ref, aunit_ref, munit_ref, ainv_ref, minv_ref, sums, sems = refs[30:]
    tokens, width = x_ref.shape
    local = out_w.shape[1]
    outs = [w_out, both_y.at[pl.ds(width, local)], out_sib, both_sib_y.at[pl.ds(width, local)]]
    ups = [up_sib, both_sib_y.at[pl.ds(0, width)], w_up, both_y.at[pl.ds(0, width)]]
    features = [refs[27], refs[28], down_ref.at[:, 3 * width :], refs[29]]
    mlp_ref, sib_act = down_ref.at[:, 0:width], down_ref.at[:, width : 3 * width]
    mn_ref, sib_hidden = up_ref.at[:, 0:width], up_ref.at[:, width : 3 * width]
    branch_ref = out_ref.at[:, 0:width]
    out_ref[:, width:] = parts_in[3][...]

    loads = []
    for at, (sources, target) in enumerate(((outs, out_w), (ups, up_w), (downs, down_w))):
        for k, source in enumerate(sources):
            loads.append(pltpu.make_async_copy(source, target.at[k], sems.at[4 * at + k]))
    for load in loads:
        load.start()
    sums[...] = jnp.zeros_like(sums)

    def add_sum(k, field):
        part = field[0:8]
        for i in range(8, field.shape[0], 8):
            part = part + field[i : i + 8]
        sums[k] += part

    halves = [range(h, h + HALF, PART) for h in range(0, tokens, HALF)]

    for load in loads[:4]:
        load.wait()
    for parts in halves:
        rows = slice(parts.start, parts.stop)
        branch = None
        for k, part_ref in enumerate(parts_in):
            term = product(part_ref[rows, :], out_w[k])
            branch = term if branch is None else branch + term
        for begin in parts:
            r = slice(begin, begin + PART)
            aunit, ainv = normalize(branch[begin - parts.start : begin - parts.start + PART])
            middle = x_ref[r, :].astype(F32) + aunit * gain_ref[1:2, :] + bias_ref[1:2, :]
            munit, minv = normalize(middle)
            mid_ref[r, :] = middle
            aunit_ref[r, :] = aunit
            munit_ref[r, :] = munit
            ainv_ref[r, :] = jnp.broadcast_to(ainv, (PART, LANES))
            minv_ref[r, :] = jnp.broadcast_to(minv, (PART, LANES))
            mn_ref[r, :] = (munit * gain_ref[2:3, :] + bias_ref[2:3, :]).astype(BF16)

    for k in range(4):
        loads[4 + k].wait()
        act_ref, columns = (sib_act, own_act)[k // 2], slice(k % 2 * width, (k % 2 + 1) * width)
        for parts in halves:
            value = product(mn_ref[parts.start : parts.stop, :], up_w[k])
            for i in range(0, HALF, 16):
                r = slice(parts.start + i, parts.start + i + 16)
                v = value[i : i + 16]
                square = v * v
                bent = jnp.tanh(v * (SCALE + (SCALE * CUBIC) * square))
                half = 0.5 + 0.5 * bent
                act_ref[r, columns] = (v * half).astype(BF16)
                slope = half + v * (1.0 - bent * bent) * (0.5 * SCALE + (1.5 * SCALE * CUBIC) * square)
                slope_ref[k, r, :] = slope.astype(BF16)

    for load in loads[8:]:
        load.wait()
    for parts in halves:
        rows = slice(parts.start, parts.stop)
        branch = None
        for k in range(4):
            act_ref, columns = (sib_act, own_act)[k // 2], slice(k % 2 * width, (k % 2 + 1) * width)
            term = product(act_ref[rows, columns], down_w[k])
            branch = term if branch is None else branch + term
        for begin in parts:
            r = slice(begin, begin + PART)
            unit, inverse = normalize(branch[begin - parts.start : begin - parts.start + PART])
            final_ref[r, :] = (mid_ref[r, :] + unit * gain_ref[3:4, :] + bias_ref[3:4, :]).astype(BF16)
            grad = cot_ref[r, :].astype(F32) * weight_ref[r, :1]
            add_sum(3, grad * unit)
            add_sum(7, grad)
            mlp_ref[r, :] = norm_back(grad, unit, inverse, gain_ref[3:4, :]).astype(BF16)

    mid_grads = []
    for parts in halves:
        rows = slice(parts.start, parts.stop)
        mid_grad = None
        for k in range(4):
            hid_ref, columns = (sib_hidden, own_hidden)[k // 2], slice(k % 2 * width, (k % 2 + 1) * width)
            act_grad = product_nt(mlp_ref[rows, :], down_w[k])
            hidden = (slope_ref[k, rows, :].astype(F32) * act_grad).astype(BF16)
            hid_ref[rows, columns] = hidden
            term = product_nt(hidden, up_w[k])
            mid_grad = term if mid_grad is None else mid_grad + term
        mid_grads.append(mid_grad)
    for parts, mid_all in zip(halves, mid_grads):
        rows = slice(parts.start, parts.stop)
        for begin in parts:
            r = slice(begin, begin + PART)
            mid_grad, munit, aunit = mid_all[begin - parts.start : begin - parts.start + PART], munit_ref[r, :], aunit_ref[r, :]
            grad = cot_ref[r, :].astype(F32) * weight_ref[r, :1]
            state = grad + norm_back(mid_grad, munit, minv_ref[r, :1], gain_ref[2:3, :])
            state_ref[r, :] = state
            branch_ref[r, :] = norm_back(state, aunit, ainv_ref[r, :1], gain_ref[1:2, :]).astype(BF16)
            for k, term in ((1, state * aunit), (2, mid_grad * munit), (5, state), (6, mid_grad)):
                add_sum(k, term)
        for k in (1, 2, 3, 0):
            features[k][rows, :] = product_nt(branch_ref[rows, :], out_w[k]).astype(BF16)
    for k in range(8):
        sum_ref[k : k + 1, :] = column_sum(sums[k])


def feed(place, parts, inputs, cot, weight, gains, biases, outs, ups, both, downs):
    width = inputs.shape[1]
    quarter = inputs.shape[0] // 4
    hid = 2 * width
    local = outs[0].shape[0]
    in_place = lambda s, t: (t[0], 0)
    stat = fixed((quarter, LANES))
    part = (quarter, local)
    shapes = [(quarter, 3 * width + local), (quarter, 3 * width), (quarter, width + local)] + [(quarter, hid)] * 2 + [(quarter, width)] * 2
    kinds = [BF16] * 6 + [F32]
    shapes, kinds = shapes + [(8, width)] + [part] * 3, kinds + [F32] + [BF16] * 3
    return pl.pallas_call(
        feed_kernel,
        grid_spec=pltpu.PrefetchScalarGridSpec(
            num_scalar_prefetch=1,
            grid=(1,),
            in_specs=[fixed(part)] * 4
            + [pl.BlockSpec((quarter, width), in_place)] * 2
            + [stat, fixed((4, width)), fixed((4, width))]
            + [ANY] * 10,
            out_specs=[fixed(shape) for shape in shapes],
            scratch_shapes=[
                pltpu.VMEM((4, local, width), BF16),
                pltpu.VMEM((4, width, width), BF16),
                pltpu.VMEM((4, width, width), BF16),
                pltpu.VMEM((4, quarter, width), BF16),
            ]
            + [pltpu.VMEM((quarter, width), F32)] * 3
            + [pltpu.VMEM((quarter, LANES), F32)] * 2
            + [pltpu.VMEM((8, 8, width), F32), pltpu.SemaphoreType.DMA((12,))],
        ),
        out_shape=[shaped(shape, kind) for shape, kind in zip(shapes, kinds)],
        compiler_params=params(60),
        cost_estimate=cost(34),
        name="feed",
    )(place, *parts, inputs, cot, weight, gains, biases, *outs, *ups, *both, *downs)


def keep_and_send(own, bit, field, keep_ref, send_ref):
    blocks, rows = send_ref.shape[0], send_ref.shape[2]
    for j in range(blocks):
        low = j // bit * 2 * bit + j % bit
        for ref, value in ((keep_ref, own), (send_ref, 1 - own)):
            begin = pl.multiple_of((low + value * bit) * rows, 16)
            ref[j, 0] = field[pl.ds(begin, rows), :]


def weight_kernel(bits, own_ref, x1, x2, y1, y2, *more):
    outs, field_ref = more[-5:-1], more[-1]
    step = pl.program_id(0)
    field = lax.dot_general(x1[...], y1[...], TN, preferred_element_type=F32)
    field = field + lax.dot_general(x2[...], y2[...], TN, preferred_element_type=F32)
    field_ref[...] = field.astype(BF16)
    for half, bit in enumerate(bits):
        keep_ref, send_ref = outs[2 * half : 2 * half + 2]
        if bit == "y":
            rows = keep_ref.shape[2]
            for k, ref in enumerate((keep_ref, send_ref)):

                @pl.when(step == 2 * half + k)
                def _(ref=ref):
                    for j in range(ref.shape[0]):
                        ref[j, 0] = field_ref[j * rows : (j + 1) * rows, :]

        else:

            @pl.when(step // 2 == half)
            def _(bit=bit, keep_ref=keep_ref, send_ref=send_ref):
                keep_and_send(own_ref[own_ref.shape[0] - bit], bit, field_ref, keep_ref, send_ref)


def weight_grad(own_bits, bits, mine, got, y1, name, *deps):
    rows, width = mine.shape[0], y1.shape[1] // 2
    size = lax.axis_size("dp")
    y_spec = lambda first: pl.BlockSpec((rows, CHUNK), lambda s, o: (0, first + s // 2 + 2 * (s % 2)))
    shape = (size, 1, width // size, CHUNK)
    specs = []
    for half, bit in enumerate(bits):
        if bit == "y":
            specs += [fixed(shape)] * 2
        else:
            part = (size // 2,) + shape[1:]
            specs += [pl.BlockSpec(part, lambda s, o, half=half: (jnp.clip(s - 2 * half, 0, 1), 0, 0, 0))] * 2
    return pl.pallas_call(
        functools.partial(weight_kernel, bits),
        grid_spec=pltpu.PrefetchScalarGridSpec(
            num_scalar_prefetch=1,
            grid=(4,),
            in_specs=[fixed((rows, width))] * 2 + [y_spec(0), y_spec(width // CHUNK)] + [ANY] * len(deps),
            out_specs=specs,
            scratch_shapes=[pltpu.VMEM((width, CHUNK), BF16)],
        ),
        out_shape=[shaped(shape, BF16)] * 4,
        compiler_params=params(60),
        cost_estimate=cost(0),
        name=name,
    )(own_bits, mine, got, y1, got, *deps)


def out_weight_kernel(mine_ref, got_ref, own_ref, theirs_ref, own_sib_ref, *more):
    width = more[-1].shape[0] * more[-1].shape[2]
    x1, x2 = mine_ref[:, :width], got_ref[:, :width]
    for out_ref, left, right in ((more[-2], own_ref, own_sib_ref), (more[-1], theirs_ref, got_ref.at[:, width:])):
        field = lax.dot_general(x1, left[...], TN, preferred_element_type=F32)
        field = field + lax.dot_general(x2, right[...], TN, preferred_element_type=F32)
        blocks, unused, rows, unused = out_ref.shape
        for j in range(blocks):
            out_ref[j, 0] = field[j * rows : (j + 1) * rows].astype(BF16)


def out_weight_grad(mine, got, own, theirs, own_sib, *deps):
    rows, local = own.shape
    width = mine.shape[1] - local
    size = lax.axis_size("dp")
    shape = (size, 1, width // size, local)
    arrays = [mine, got, own, theirs, own_sib]
    return pl.pallas_call(
        out_weight_kernel,
        grid=(1,),
        in_specs=[fixed(a.shape) for a in arrays] + [ANY] * len(deps),
        out_specs=[fixed(shape)] * 2,
        out_shape=[shaped(shape, BF16)] * 2,
        compiler_params=params(60),
        cost_estimate=cost(0),
        name="out_weight_grad",
    )(*arrays, *deps)


def in_back_kernel(order_ref, p0, p1, w_ref, x_ref, feed_ref, *more):
    send_ref, keep_ref, sum_ref, sums, field_ref = more[-5:]
    step = pl.program_id(0)
    block = x_ref.shape[0]

    @pl.when(step == 0)
    def _():
        sums[...] = jnp.zeros_like(sums)

    field = None
    for c in range(3):
        cut = slice(c * LANES, (c + 1) * LANES)
        left = jnp.concatenate([p0[:, cut], p1[:, cut]], axis=1)
        term = product_nt(left, w_ref[c])
        field = term if field is None else field + term
    gain_part = bias_part = 0.0
    for begin in range(0, block, PART):
        r = slice(begin, begin + PART)
        unit, unused = normalize(x_ref[r, :].astype(F32))
        field_ref[r, :] = field[r].astype(BF16)
        scaled = field[r] * unit
        for i in range(0, PART, 8):
            gain_part = gain_part + scaled[i : i + 8]
            bias_part = bias_part + field[begin + i : begin + i + 8]
    sums[0] += gain_part
    sums[1] += bias_part

    @pl.when(step // 2 % 2 == 0)
    def _():
        send_ref[...] = field_ref[...]

    @pl.when(step // 2 % 2 == 1)
    def _():
        keep_ref[...] = field_ref[...]

    @pl.when(step == 7)
    def _():
        sum_ref[...] = feed_ref[...]
        for k in range(2):
            sum_ref[4 * k : 4 * k + 1, :] = column_sum(sums[k])


def in_back(place, parts, w_qkv, inputs, feed_sums, *deps):
    block = 256
    tokens, width = inputs.shape
    rows = lambda s, o: (2 * (o[0] ^ (3 - s // 2)) + s % 2, 0)
    shapes = [(tokens // 2, width), (tokens // 2, width), (8, width)]
    return pl.pallas_call(
        in_back_kernel,
        grid_spec=pltpu.PrefetchScalarGridSpec(
            num_scalar_prefetch=1,
            grid=(8,),
            in_specs=[pl.BlockSpec((block, 3 * LANES), rows)] * 2
            + [fixed(w_qkv.shape), pl.BlockSpec((block, width), rows), fixed((8, width))]
            + [ANY] * len(deps),
            out_specs=[
                pl.BlockSpec((block, width), lambda s, o: (s // 4 * 2 + jnp.minimum(s % 4, 1), 0)),
                pl.BlockSpec((block, width), lambda s, o: (s // 4 * 2 + jnp.maximum(s % 4 - 2, 0), 0)),
                fixed(shapes[2]),
            ],
            scratch_shapes=[pltpu.VMEM((2, 8, width), F32), pltpu.VMEM((block, width), BF16)],
        ),
        out_shape=[shaped(shapes[0], BF16), shaped(shapes[1], BF16), shaped(shapes[2], F32)],
        compiler_params=params(60),
        cost_estimate=cost(1),
        name="in_back",
    )(place, *parts, w_qkv, inputs, feed_sums, *deps)


def qkv_kernel(own_ref, n_ref, p_ref, *more):
    keep_ref, send_ref, field_ref = more[-3:]
    rows = n_ref.shape[0]
    for k in range(field_ref.shape[0] // rows):

        @pl.when(pl.program_id(0) == k)
        def _(k=k):
            field_ref[k * rows : (k + 1) * rows, :] = product(n_ref[...], p_ref[...]).astype(BF16)

    @pl.when(pl.program_id(0) == pl.num_programs(0) - 1)
    def _():
        keep_and_send(own_ref[own_ref.shape[0] - 3], 4, field_ref, keep_ref, send_ref)


def qkv_grad(own_bits, normed_turned, part, *deps):
    width, tokens = normed_turned.shape
    columns = part.shape[1]
    size = lax.axis_size("dp")
    steps = 2
    shape = (size // 2, 1, width // size, columns)
    return pl.pallas_call(
        qkv_kernel,
        grid_spec=pltpu.PrefetchScalarGridSpec(
            num_scalar_prefetch=1,
            grid=(steps,),
            in_specs=[pl.BlockSpec((width // steps, tokens), lambda i, o: (i, 0)), fixed(part.shape)] + [ANY] * len(deps),
            out_specs=[fixed(shape)] * 2,
            scratch_shapes=[pltpu.VMEM((width, columns), BF16)],
        ),
        out_shape=[shaped(shape, BF16)] * 2,
        compiler_params=params(60),
        cost_estimate=cost(0),
        name="qkv_grad",
    )(own_bits, normed_turned, part, *deps)


def add_kernel(keep_ref, got_ref, *more):
    for begin in range(0, keep_ref.shape[0], PART):
        r = slice(begin, begin + PART)
        more[-1][r, :] = total([keep_ref[r, :], got_ref[r, :]]).astype(BF16)


def add_core(keep, got, *deps):
    rows, width = keep.shape[0] // 2, keep.shape[1]
    block = rows // 2
    spec = pl.BlockSpec((block, width), lambda i: (i, 0))
    return pl.pallas_call(
        add_kernel,
        grid=(2,),
        in_specs=[spec, spec] + [ANY] * len(deps),
        out_specs=spec,
        out_shape=shaped((rows, width), BF16),
        compiler_params=params(60),
        cost_estimate=cost(3),
        name="add_core",
    )(keep, got, *deps)


def finish_kernel(place_ref, x_ref, state_ref, keep_ref, near_ref, far_ref, gain_ref, *more):
    out_ref = more[-1]
    for begin in range(0, x_ref.shape[0], PART):
        r = slice(begin, begin + PART)
        unit, inverse = normalize(x_ref[r, :].astype(F32))
        grad = total([keep_ref[r, :], near_ref[r, :], far_ref[r, :]])
        out_ref[r, :] = state_ref[r, :] + norm_back(grad, unit, inverse, gain_ref[0:1, :])


def finish(place, inputs, state, keep, near, far, gains, *deps):
    quarter, width = state.shape
    block = 128
    steps = quarter // block
    spec = pl.BlockSpec((block, width), lambda s, t: (s, 0))
    return pl.pallas_call(
        finish_kernel,
        grid_spec=pltpu.PrefetchScalarGridSpec(
            num_scalar_prefetch=1,
            grid=(steps,),
            in_specs=[pl.BlockSpec((block, width), lambda s, t: (t[0] * steps + s, 0)), spec]
            + [pl.BlockSpec((block, width), lambda s, t: (steps + s, 0))] * 2
            + [spec]
            + [fixed(gains.shape)]
            + [ANY] * len(deps),
            out_specs=spec,
        ),
        out_shape=shaped((quarter, width), F32),
        compiler_params=params(60),
        cost_estimate=cost(0),
        name="finish",
    )(place, inputs, state, keep, near, far, gains, *deps)


def per_device(
    inputs, w_qkv, w_out, w_up, w_down, norm_gains, norm_biases, out_cot, group_ids, group_weights
):
    tokens, width = inputs.shape
    quarter = tokens // 4
    place = lax.axis_index("tensor")
    where = place.astype(jnp.int32).reshape(1)
    dp_size = lax.axis_size("dp")
    cosine, sine = rotary_tables()

    dp_index = lax.axis_index("dp").astype(jnp.int32)
    mine = (dp_index % 4).reshape(1)
    owns = jnp.stack([jnp.int32(0)] + [(dp_index // kind) % 2 for kind in dp_kinds()])

    own_ids = lax.dynamic_slice_in_dim(group_ids, place * quarter, quarter, 0)
    groups = jnp.arange(group_weights.shape[0], dtype=jnp.int32)
    lookup = (own_ids[:, None] == groups[None, :]).astype(F32)
    row_weight = jnp.sum(lookup * group_weights[None, :], axis=1, keepdims=True)
    row_weight = jnp.broadcast_to(row_weight, (quarter, LANES))

    up_rows, out_rows, down_rows = w_up.shape[0] // 4, w_out.shape[0] // 4, w_down.shape[0] // 4
    zero = lambda m: 0
    up_sent, down_sent = move_rows(
        mine,
        [w_up, w_out, w_down],
        [(up_rows + out_rows, width), (down_rows, width)],
        [
            (0, lambda m: m * up_rows, 0, zero, up_rows),
            (1, lambda m: m * out_rows, 0, lambda m: up_rows, out_rows),
            (2, lambda m: m * down_rows, 1, zero, down_rows),
        ],
        "take",
    )

    def halves(one, two, name):
        rows = one.shape[0] // 2
        moves = [(1, zero, 0, zero, rows), (0, lambda m: rows, 1, zero, rows)]
        low, high = move_rows(mine, [one, two], [(rows, width)] * 2, moves, name)
        return swap(low, "dp", 1), swap(high, "dp", 2), low

    def quarter_moves(target, first, rows, begin, count):
        return [
            (which, lambda m: begin, target, lambda m, which=which: first + (m ^ which) * rows, rows)
            for which in range(count)
        ]

    up_got = y_swap(up_sent)
    up_sib, down_sib, out_sib = core_swap(w_up), core_swap(w_down), core_swap(w_out)
    normed_turned, query, key_rows, value_rows = project(
        inputs, w_qkv, norm_gains, norm_biases, cosine, sine, up_sent
    )
    down_sent = gate(down_sent, normed_turned)
    down_got = y_swap(down_sent)
    up_got = gate(up_got, down_sent)
    up_one, up_two = swap(up_got, "dp", 1), swap(up_got, "dp", 2)

    *outs, more_first = attend(0, where, query, key_rows, value_rows, [], up_got, up_sib, down_sib, out_sib)
    down_got = gate(down_got, outs[0])
    down_one, down_two = swap(down_got, "dp", 1), swap(down_got, "dp", 2)
    up_one = gate(up_one, down_got)
    up_low, up_high, last = halves(up_one, up_two, "up_halves")
    *outs, more_second = attend(1, where, query, key_rows, value_rows, outs, last, down_got)
    rows = [outs[0], core_swap(outs[1]), y_swap(outs[2]), diagonal_swap(outs[3], 0, 3)]
    up_one = gate(up_one, outs[1], outs[2], outs[3])

    def last_moves(target, first, rows, begin, half):
        low = max(0, min(half - begin, rows))
        moves = [(3, lambda m: begin, target, lambda m: first + (m ^ 3) * rows, low)] if low else []
        start = begin + low - half
        return moves + [(4, lambda m: start, target, lambda m: first + (m ^ 3) * rows + low, rows - low)]

    half = (up_rows + out_rows) // 2
    (upout_y,) = move_rows(
        mine,
        [up_got, up_one, up_two, up_low, up_high],
        [(w_up.shape[0] + w_out.shape[0], width)],
        quarter_moves(0, 0, up_rows, 0, 3)
        + quarter_moves(0, w_up.shape[0], out_rows, up_rows, 3)
        + last_moves(0, 0, up_rows, 0, half)
        + last_moves(0, w_up.shape[0], out_rows, up_rows, half),
        "up_whole",
    )
    upout_sib_y = core_swap(upout_y)
    down_one = gate(down_one, upout_y, rows[1])
    down_low, down_high, last = halves(down_one, down_two, "down_halves")
    down_low = gate(down_low, rows[2], rows[3])
    (down_y,) = move_rows(
        mine,
        [down_got, down_one, down_two, down_low, down_high],
        [w_down.shape],
        quarter_moves(0, 0, down_rows, 0, 3) + last_moves(0, 0, down_rows, 0, down_rows // 2),
        "down_whole",
    )
    down_sib_y = core_swap(down_y)

    for_down, for_up, for_out, own_act, own_hidden, final_rows, state_grad, sums_feed, own, for_y, for_far = feed(
        where, [rows[0], rows[2], rows[1], rows[3]], inputs, out_cot, row_weight, norm_gains, norm_biases,
        [w_out, out_sib], [up_sib, w_up], [upout_sib_y, upout_y], [down_sib, down_sib_y, w_down, down_y],
    )

    down_got = core_swap(for_down)
    grads = [own, down_got, y_swap(for_y), diagonal_swap(for_far, 0, 3)]
    for_up = gate(for_up, down_got)
    up_got = core_swap(for_up)
    kinds = dp_kinds()
    both = ["y"] + kinds
    without = lambda bits, *gone: [b for b in bits if b not in gone]
    newest = lambda *items: [item.addends[-1][0] for item in items]
    d0_keep, d0_send, d1_keep, d1_send = weight_grad(
        owns, ("y", 1), for_down, down_got, own_act, "down_grad", for_up
    )
    d0 = Item(kinds, d0_keep, y_swap(d0_send))
    d1 = Item(without(both, 1), d1_keep, swap(d1_send, "dp", 1))
    u0_keep, u0_send, u1_keep, u1_send = weight_grad(
        owns, (1, 2), for_up, up_got, own_hidden, "up_grad", d0_send, d1_send, *grads[2:]
    )
    u1 = Item(without(both, 2), u1_keep, swap(u1_send, "dp", 2))
    for_out = gate(for_out, u1_send)
    out_got = core_swap(for_out)
    part_first = attend_back(
        0, where, key_rows, value_rows, more_first, grads, outs, cosine, sine, u1_send, for_out
    )
    u0_send = gate(u0_send, part_first)
    u0 = Item(without(both, 1), u0_keep, swap(u0_send, "dp", 1))
    out_keep, out_send = out_weight_grad(for_out, out_got, rows[0], rows[2], outs[1], u0_send)
    out_item = Item(kinds, out_keep, y_swap(out_send))

    def qkv_item(part, *deps):
        keep, send = qkv_grad(owns, normed_turned, part, *deps)
        return Item(without(kinds, 4), keep, swap(send, "dp", 4)), send

    q0, last = qkv_item(part_first, out_send)
    last = halve(owns, [d1], 2, last)
    part_second = attend_back(
        1, where, key_rows, value_rows, more_second, grads, outs, cosine, sine, last, *newest(d0, u1)
    )
    part_second = gate(part_second, *newest(u0), micros=3)
    parts = [part_first, part_second]

    send, keep, sums = in_back(where, parts, w_qkv, inputs, sums_feed, *newest(d1, q0, out_item))
    core_got = core_swap(send)
    last = halve(owns, [u1, d0], 1, send)
    last = halve(owns, [u0, out_item], 2, last)
    far = add_core(keep, core_got, last)
    far_got = y_swap(far)
    q1, last = qkv_item(part_second, far)
    last = gate(last, *newest(u1), micros=3)
    last = gate(last, *newest(u0), micros=3)
    last = send_last(owns, [d1, u0, u1], last, far_got)
    last = halve(owns, [q0, q1, out_item], 1, last)
    last = halve(owns, [d0], 2, last)
    input_grad = finish(where, inputs, state_grad, keep, core_got, far_got, norm_gains, last)
    last = send_last(owns, [q0, q1, d0, out_item], input_grad)
    share = width // (4 * dp_size)
    sums = gate(sums, last)
    sums = sums.reshape(8, 4 * dp_size, share).transpose(1, 0, 2)
    sums = jnp.sum(lax.all_to_all(sums, ("dp", "tensor"), 0, 0, tiled=True), axis=0)
    last = gate(last, *[a[0] for a in u0.addends[-3:]], micros=6)
    up_total, down_total, out_total, qkv_total = finals(
        owns, [[(u0, False), (u1, False)], [(d0, True), (d1, True)], [(out_item, True)]], [q0, q1], last
    )
    return (
        final_rows,
        input_grad,
        qkv_total,
        out_total,
        up_total,
        down_total,
        sums[:4],
        sums[4:],
    )


def solution(mesh):
    placed = (
        P("dp", None),
        P(None, None, "tensor"),
        P("tensor", None),
        P(None, "tensor"),
        P("tensor", None),
        P(),
        P(),
        P("dp", None),
        P("dp"),
        P(),
    )
    return jax.shard_map(
        per_device,
        mesh=mesh,
        in_specs=placed,
        out_specs=(
            P(("dp", "tensor"), None),
            P(("dp", "tensor"), None),
            P(None, "dp", "tensor"),
            P("tensor", "dp"),
            P("dp", "tensor"),
            P("tensor", "dp"),
            P(None, ("dp", "tensor")),
            P(None, ("dp", "tensor")),
        ),
        check_vma=False,
    )
```

```python
import functools
import math

import jax
import jax.numpy as jnp
import numpy as np
from jax import lax
from jax.experimental import pallas as pl
from jax.experimental.pallas import tpu as pltpu
from jax.sharding import PartitionSpec as P

DH = 64
SEQ = 2048
EPS = 1e-05
PART = 32
F32 = jnp.float32
BF16 = jnp.bfloat16
LANES = 128
NT = (((1,), (1,)), ((), ()))
TN = (((0,), (0,)), ((), ()))
ANY = pl.BlockSpec(memory_space=pl.ANY)


def params(mebibytes=60):
    return pltpu.CompilerParams(vmem_limit_bytes=mebibytes * 2**20)


def cost(micros):
    return pl.CostEstimate(flops=int(micros * 1.1e9), bytes_accessed=2**16, transcendentals=0)


def shaped(shape, kind):
    return jax.ShapeDtypeStruct(shape, kind)


def fixed(shape):
    return pl.BlockSpec(shape, lambda *unused: (0,) * len(shape))


def gate(field, *deps, micros=0):
    return pl.pallas_call(
        lambda *refs: None,
        in_specs=[ANY] * (1 + len(deps)),
        out_specs=ANY,
        out_shape=shaped(field.shape, field.dtype),
        input_output_aliases={0: 0},
        cost_estimate=cost(micros),
        name="gate",
    )(field, *deps)


def swap(field, axis, bit):
    size = lax.axis_size(axis)
    return lax.ppermute(field, axis, [(i, i ^ bit) for i in range(size)])


def core_swap(field):
    return swap(field, "tensor", 1)


def y_swap(field):
    return swap(field, "tensor", 2)


def total(addends):
    return sum(a.astype(F32) for a in addends)


def diagonal_swap(field, dp_bits, tensor_bits):
    mask = 4 * dp_bits + tensor_bits
    size = 4 * lax.axis_size("dp")
    return lax.ppermute(field, ("dp", "tensor"), [(i, i ^ mask) for i in range(size)])


def move_rows(number, sources, targets, moves, name):
    def kernel(number_ref, *refs):
        source_refs, target_refs, sems = refs[: len(sources)], refs[len(sources) : -1], refs[-1]
        copies = []
        for at, (source, begin, target, end, rows) in enumerate(moves):
            begin, end = (pl.multiple_of(f(number_ref[0]), 16) for f in (begin, end))
            copies.append(
                pltpu.make_async_copy(
                    source_refs[source].at[pl.ds(begin, rows)], target_refs[target].at[pl.ds(end, rows)], sems.at[at]
                )
            )
        for copy in copies:
            copy.start()
        for copy in copies:
            copy.wait()

    return pl.pallas_call(
        kernel,
        grid_spec=pltpu.PrefetchScalarGridSpec(
            num_scalar_prefetch=1,
            grid=(1,),
            in_specs=[ANY] * len(sources),
            out_specs=[fixed(t) for t in targets],
            scratch_shapes=[pltpu.SemaphoreType.DMA((len(moves),))],
        ),
        out_shape=[shaped(t, BF16) for t in targets],
        compiler_params=params(60),
        cost_estimate=cost(1.5),
        name=name,
    )(number, *sources)


def dp_kinds():
    return [1 << k for k in reversed(range(lax.axis_size("dp").bit_length() - 1))]


class Item:
    def __init__(self, left, *arrays):
        self.left = list(left)
        self.addends = [(array, 0, list(left)) for array in arrays]
        self.shape = arrays[0].shape[2:]


def block_index(kinds, bits, free, flips):
    def index(g, own_ref):
        at = 0
        for bit in bits:
            if bit in free:
                value = (g >> (len(free) - 1 - free.index(bit))) & 1
            else:
                value = own_ref[kinds.index(bit)]
                flip = flips(g, bit)
                value = value + flip - 2 * value * flip
            at = 2 * at + value
        return at

    return index


def addend_specs(items, kinds, frees, flips):
    specs, arrays = [], []
    for item, free in zip(items, frees):
        rows, columns = item.shape
        for array, first, bits in item.addends:
            at = block_index(kinds, bits, free, flips)
            fits = array.shape[3] % columns == 0 and first % columns == 0
            block, column = (columns, first // columns) if fits else (array.shape[3], 0)
            specs.append(
                pl.BlockSpec((1, 1, rows, block), lambda g, own_ref, at=at, column=column: (at(g, own_ref), 0, 0, column))
            )
            arrays.append(array)
    return specs, arrays


def sums_of(items, refs):
    refs = iter(refs)
    fields = []
    for item in items:
        terms = []
        for array, first, bits in item.addends:
            ref = next(refs)
            begin = first if ref.shape[3] > item.shape[1] else 0
            terms.append(ref[0, 0, :, begin : begin + item.shape[1]])
        fields.append(total(terms))
    return fields


def put_beside(out_ref, fields):
    begin = 0
    for field in fields:
        out_ref[0, 0, :, begin : begin + field.shape[1]] = field.astype(BF16)
        begin += field.shape[1]


def received(items, got, lefts):
    begin = 0
    for item, left in zip(items, lefts):
        item.addends.append((got, begin, list(left)))
        begin += item.shape[1]


def packed(items):
    return (1, items[0].shape[0], sum(item.shape[1] for item in items))


def halve(owns, items, kind, *deps):
    kinds = ["y"] + dp_kinds()
    frees = [[b for b in item.left if b != kind] for item in items]
    steps = 2 ** len(frees[0])
    specs, arrays = addend_specs(items, kinds, frees, lambda g, bit: 1 if bit == kind else 0)
    shape = packed(items)

    def kernel(own_ref, *refs):
        put_beside(refs[-1], sums_of(items, refs))

    sent = pl.pallas_call(
        kernel,
        grid_spec=pltpu.PrefetchScalarGridSpec(
            num_scalar_prefetch=1,
            grid=(steps,),
            in_specs=specs + [ANY] * len(deps),
            out_specs=pl.BlockSpec((1,) + shape, lambda g, own_ref: (g, 0, 0, 0)),
        ),
        out_shape=shaped((steps,) + shape, BF16),
        compiler_params=params(60),
        cost_estimate=cost(3),
        name="halve",
    )(owns, *arrays, *deps)
    got = y_swap(sent) if kind == "y" else swap(sent, "dp", kind)
    received(items, got, frees)
    for item, free in zip(items, frees):
        item.left = free
    return sent


def send_last(owns, items, *deps):
    pair = ["y", 4] if "y" in items[0].left else [4, 2]
    for item in items:
        while [b for b in item.left if b not in pair]:
            deps = (halve(owns, [item], [b for b in item.left if b not in pair][0], *deps),)
    kinds = ["y"] + dp_kinds()
    masks = [[pair[1]], [pair[0]], pair]
    takers = [[i for i, item in enumerate(items) if all(b in item.left for b in mask)] for mask in masks]
    masks, takers = [m for m, t in zip(masks, takers) if t], [t for t in takers if t]

    def flips(g, bit):
        value = 0
        for k, mask in enumerate(masks):
            if bit in mask:
                value = jnp.where(g == k, 1, value)
        return value

    specs, arrays = addend_specs(items, kinds, [[] for item in items], flips)
    shapes = [(1,) + packed([items[i] for i in taker]) for taker in takers]

    def kernel(own_ref, *refs):
        fields = sums_of(items, refs)
        for k, taker in enumerate(takers):

            @pl.when(pl.program_id(0) == k)
            def _(k=k, taker=taker):
                put_beside(refs[k - len(masks)], [fields[i] for i in taker])

    sent = pl.pallas_call(
        kernel,
        grid_spec=pltpu.PrefetchScalarGridSpec(
            num_scalar_prefetch=1,
            grid=(len(masks),),
            in_specs=specs + [ANY] * len(deps),
            out_specs=[fixed(shape) for shape in shapes],
        ),
        out_shape=[shaped(shape, BF16) for shape in shapes],
        compiler_params=params(60),
        cost_estimate=cost(2),
        name="send_last",
    )(owns, *arrays, *deps)
    for field, mask, taker in zip(sent, masks, takers):
        got = diagonal_swap(field, sum(b for b in mask if b != "y"), 2 if "y" in mask else 0)
        received([items[i] for i in taker], got, [[]] * len(taker))
    for item in items:
        item.left = []
    return sent[-1]


def finals(owns, groups, heads, *deps):
    kinds = ["y"] + dp_kinds()
    items = [item for group in groups for item, turned in group] + heads
    specs, arrays = addend_specs(items, kinds, [[] for item in items], lambda g, bit: 0)
    shapes = []
    for group in groups:
        rows, columns = group[0][0].shape
        shapes.append((columns * len(group), rows) if group[0][1] else (rows, columns * len(group)))

    shapes.append((3, heads[0].shape[0], LANES * len(heads)))

    def kernel(own_ref, *refs):
        fields = sums_of(items, refs)
        for at, field in enumerate(fields[-len(heads) :]):
            for c in range(3):
                refs[-1][c, :, at * LANES : (at + 1) * LANES] = field[:, c * LANES : (c + 1) * LANES]
        fields = iter(fields)
        for group, out_ref in zip(groups, refs[-len(groups) - 1 :]):
            for i, (item, turned) in enumerate(group):
                cut = slice(i * item.shape[1], (i + 1) * item.shape[1])
                field = next(fields)
                if turned:
                    out_ref[cut, :] = jnp.transpose(field)
                else:
                    out_ref[:, cut] = field

    return pl.pallas_call(
        kernel,
        grid_spec=pltpu.PrefetchScalarGridSpec(
            num_scalar_prefetch=1,
            grid=(1,),
            in_specs=specs + [ANY] * len(deps),
            out_specs=[fixed(shape) for shape in shapes],
        ),
        out_shape=[shaped(shape, F32) for shape in shapes],
        compiler_params=params(60),
        cost_estimate=cost(3),
        name="finals",
    )(owns, *arrays, *deps)


def normalize(field):
    mean = jnp.mean(field, axis=-1, keepdims=True)
    centred = field - mean
    inverse = lax.rsqrt(jnp.mean(centred * centred, axis=-1, keepdims=True) + EPS)
    return centred * inverse, inverse


def norm_back(grad, unit, inverse, gain):
    scaled = grad * gain
    mean_one = jnp.mean(scaled, axis=-1, keepdims=True)
    mean_two = jnp.mean(scaled * unit, axis=-1, keepdims=True)
    return inverse * (scaled - mean_one - unit * mean_two)


def rotary_tables():
    half = DH // 2
    frequency = np.exp(np.arange(half, dtype=np.float32) * np.float32(-math.log(10000.0) / half))
    angles = np.arange(SEQ, dtype=np.float32)[:, None] * frequency.astype(np.float32)[None, :]
    cosine, sine = np.cos(angles), np.sin(angles)
    return (
        jnp.asarray(np.concatenate([cosine] * 4, axis=1).astype(np.float32)),
        jnp.asarray(np.concatenate([-sine, sine, -sine, sine], axis=1).astype(np.float32)),
    )


def lanes_of(shape):
    return lax.broadcasted_iota(jnp.int32, shape, 1)


def partner_lanes(field):
    lane = lanes_of(field.shape)
    return jnp.where(lane % DH < DH // 2, pltpu.roll(field, 96, 1), pltpu.roll(field, 32, 1))


def rotate(field, cosine, sine):
    return field * cosine + partner_lanes(field) * sine


def rotate_back(field, cosine, sine):
    return field * cosine - partner_lanes(field) * sine


def split_three(field):
    high = field.astype(BF16).astype(F32)
    rest = field - high
    middle = rest.astype(BF16).astype(F32)
    return high, middle, rest - middle


def product(left, right):
    return jnp.dot(left, right, preferred_element_type=F32)


def product_nt(left, right):
    return lax.dot_general(left, right, NT, preferred_element_type=F32)


def column_sum(field):
    return jnp.sum(field, axis=0, keepdims=True)


def project_kernel(x_ref, w_ref, gain_ref, bias_ref, cos_ref, sin_ref, *more):
    n_ref, q_ref, k_ref, v_ref, normed_ref = more[-5:]
    rows, width = x_ref.shape
    for i in range(rows // PART):
        r = slice(i * PART, (i + 1) * PART)
        unit, unused = normalize(x_ref[r, :].astype(F32))
        normed_ref[r, :] = (unit * gain_ref[0:1, :] + bias_ref[0:1, :]).astype(BF16)
    for i in range(width // 256):
        c = slice(i * 256, (i + 1) * 256)
        n_ref[c, :] = jnp.transpose(normed_ref[:, c])
    lane = lanes_of((PART, LANES))
    ones = jnp.where(lane < DH + 3, 1.0, 0.0)
    for which, out_ref in enumerate((q_ref, k_ref, v_ref)):
        both = product(normed_ref[...], w_ref[which])
        for i in range(rows // PART):
            r = slice(i * PART, (i + 1) * PART)
            for pair in range(both.shape[1] // LANES):
                field = both[r, pair * LANES : (pair + 1) * LANES]
                if which < 2:
                    field = rotate(field, cos_ref[r, :], sin_ref[r, :])
                if which == 0:
                    field = field * (1.0 / math.sqrt(DH))
                extra = jnp.zeros_like(field) if which == 0 else ones
                out_ref[2 * pair, r, :] = jnp.where(lane < DH, field, extra).astype(BF16)
                out_ref[2 * pair + 1, r, :] = jnp.where(lane < DH, pltpu.roll(field, DH, 1), extra).astype(BF16)


def project(inputs, w_qkv, gain, bias, cosine, sine, *deps):
    block = 256
    tokens, width = inputs.shape
    local = w_qkv.shape[2]
    heads = local // DH
    rows = lambda i: (i, 0)
    per_head = pl.BlockSpec((heads, block, LANES), lambda i: (0, i, 0))
    headed = shaped((heads, tokens, LANES), BF16)
    return pl.pallas_call(
        project_kernel,
        grid=(tokens // block,),
        in_specs=[
            pl.BlockSpec((block, width), rows),
            fixed((3, width, local)),
            fixed((4, width)),
            fixed((4, width)),
            pl.BlockSpec((block, LANES), rows),
            pl.BlockSpec((block, LANES), rows),
        ]
        + [ANY] * len(deps),
        out_specs=[pl.BlockSpec((width, block), lambda i: (0, i)), per_head, per_head, per_head],
        out_shape=[shaped((width, tokens), BF16), headed, headed, headed],
        scratch_shapes=[pltpu.VMEM((block, width), BF16)],
        compiler_params=params(60),
        cost_estimate=cost(10),
        name="project",
    )(inputs, w_qkv, gain, bias, cosine, sine, *deps)


ROWS = 512
KEYS = 512
STRIP = 256


def hidden_keys(shape, down, across):
    return lax.broadcasted_iota(jnp.int32, shape, 0) + down > lax.broadcasted_iota(jnp.int32, shape, 1) + across


def attend_block(n, place_ref, q_ref, k_ref, v_ref, out_refs, qa_ref, score_ref, chance_ref):
    start, end = n * ROWS, (n + 1) * ROWS
    row = lax.broadcasted_iota(jnp.int32, (LANES, ROWS), 0)
    lane = lanes_of((ROWS, LANES))
    outs = []
    for h in range(2):
        most = None
        for begin in range(0, end, STRIP):
            scores = product_nt(k_ref[h, begin : begin + STRIP, :], q_ref[h])
            if begin >= start:
                scores = jnp.where(hidden_keys((STRIP, ROWS), begin, start), -1e30, scores)
            score_ref[h, begin : begin + STRIP, :] = scores
            for i in range(0, STRIP, 8):
                most = scores[i : i + 8] if most is None else jnp.maximum(most, scores[i : i + 8])
        top = jnp.max(most, axis=0, keepdims=True)
        for begin in range(0, end, PART):
            r = slice(begin, begin + PART)
            chance_ref[h, r, :] = jnp.exp(score_ref[h, r, :] - top).astype(BF16)
        both = lax.dot_general(v_ref[h, :end, :], chance_ref[h, :end, :], TN, preferred_element_type=F32)
        summed = both[DH : DH + 1, :]
        high, middle, low = split_three(-(top + jnp.log(summed)))
        extra = jnp.where(row == DH + 1, middle, jnp.where(row == DH + 2, low, 0.0))
        extra = jnp.where(row == DH, high, extra)
        turned = jnp.transpose(jnp.where(row < DH, both * (1.0 / summed), extra))
        qa_ref[h] = jnp.where(lane < DH, q_ref[h].astype(F32), turned).astype(BF16)
        outs.append(turned)
    both = jnp.where(lane < DH, outs[0], pltpu.roll(outs[1], DH, 1)).astype(BF16)
    for which, out_ref in enumerate(out_refs):

        @pl.when((place_ref[0] ^ which) == n)
        def _(out_ref=out_ref):
            out_ref[...] = both


def attend_kernel(place_ref, q_ref, k_ref, v_ref, *more):
    block = pl.program_id(0)
    keys_ref, values_ref = more[-2:]
    for n in range(SEQ // ROWS):

        @pl.when(block == n)
        def _(n=n):
            keys_ref[:, n * ROWS : (n + 1) * ROWS, :] = k_ref[...]
            values_ref[:, n * ROWS : (n + 1) * ROWS, :] = v_ref[...]
            attend_block(n, place_ref, q_ref, keys_ref, values_ref, more[-9:-5], *more[-5:-2])


def attend(pair, place, query, key_rows, value_rows, before, *deps):
    part = pl.BlockSpec((2, ROWS, LANES), lambda i, t: (pair, i, 0))
    return pl.pallas_call(
        attend_kernel,
        grid_spec=pltpu.PrefetchScalarGridSpec(
            num_scalar_prefetch=1,
            grid=(SEQ // ROWS,),
            in_specs=[part, part, part]
            + [ANY] * (len(before) + len(deps)),
            out_specs=[pl.BlockSpec((ROWS, LANES), lambda i, t: (0, pair))] * 4
            + [pl.BlockSpec((2, ROWS, LANES), lambda i, t: (0, i, 0))],
            scratch_shapes=[pltpu.VMEM((2, SEQ, ROWS), F32), pltpu.VMEM((2, SEQ, ROWS), BF16)]
            + [pltpu.VMEM((2, SEQ, LANES), BF16)] * 2,
        ),
        out_shape=[shaped((ROWS, 2 * LANES), BF16)] * 4 + [shaped((2, SEQ, LANES), BF16)],
        input_output_aliases={4 + k: k for k in range(len(before))},
        compiler_params=params(60),
        cost_estimate=cost(10),
        name="attend",
    )(place, query, key_rows, value_rows, *before, *deps)


def back_block(j, k_ref, v_ref, qa_ref, cos_ref, sin_ref, pg_ref, da_ref, dq_ref, chance_ref, score_ref):
    start, length = j * KEYS, SEQ - j * KEYS
    rows = slice(start, start + KEYS)
    lane = lanes_of((KEYS, LANES))
    key_grads, value_grads = [], []
    for h in range(2):
        keys, values = k_ref[h], v_ref[h]
        for begin in range(0, length, KEYS):
            cut = slice(begin, begin + KEYS)
            scores = product_nt(keys, qa_ref[h, start + begin : start + begin + KEYS, :])
            chance_grad = product_nt(values, da_ref[h, start + begin : start + begin + KEYS, :])
            for i in range(0, KEYS, 64):
                r = slice(i, i + 64)
                chance = jnp.exp(scores[r])
                if begin == 0:
                    chance = jnp.where(hidden_keys((64, KEYS), i, 0), 0.0, chance)
                chance_ref[h, r, cut] = chance.astype(BF16)
                score_ref[h, r, cut] = (chance * chance_grad[r]).astype(BF16)
        value_grads.append(product(chance_ref[h, :, :length], da_ref[h, start:, :]))
        key_grads.append(product(score_ref[h, :, :length], qa_ref[h, start:, :]))
        turned = lax.dot_general(keys[:, :DH], score_ref[h, :, :length], TN, preferred_element_type=F32)
        if j == 0:
            dq_ref[h] = turned
        else:
            dq_ref[h, :, start:] += turned
    key_grad = jnp.where(lane < DH, key_grads[0], pltpu.roll(key_grads[1], DH, 1))
    value_grad = jnp.where(lane < DH, value_grads[0], pltpu.roll(value_grads[1], DH, 1))
    pg_ref[:, LANES : 2 * LANES] = rotate_back(key_grad, cos_ref[...], sin_ref[...]).astype(BF16)
    pg_ref[:, 2 * LANES :] = value_grad.astype(BF16)
    for begin in range(0, KEYS, 256):
        cut = slice(begin, begin + 256)
        turned = [dq_ref[h, :, start + begin : start + begin + 256] for h in range(2)]
        field = jnp.transpose(jnp.concatenate(turned, axis=0)) * (1.0 / math.sqrt(DH))
        pg_ref[cut, :LANES] = rotate_back(field, cos_ref[cut, :], sin_ref[cut, :]).astype(BF16)


def back_kernel(place_ref, k_ref, v_ref, qa_ref, g0, g1, g2, g3, o0, o1, o2, o3, cos_ref, sin_ref, *more):
    pg_ref, da_ref, turned_ref, chance_ref, score_ref = more[-5:]
    step = pl.program_id(0)
    steps = SEQ // KEYS
    span = 64

    @pl.when(step == 0)
    def _():
        lane = lanes_of((span, LANES))
        for which, (grad_ref, out_ref) in enumerate(((g0, o0), (g1, o1), (g2, o2), (g3, o3))):
            begin = (place_ref[0] ^ which) * (SEQ // 4)
            for i in range(SEQ // 4 // span):
                rows = pl.ds(pl.multiple_of(begin + i * span, span), span)
                part = slice(i * span, (i + 1) * span)
                grad = grad_ref[part, :].astype(F32)
                both = grad * out_ref[part, :].astype(F32)
                for h in range(2):
                    inner = jnp.sum(jnp.where(lane // DH == h, both, 0.0), axis=1, keepdims=True)
                    high, middle, low = split_three(-inner)
                    own = grad if h == 0 else pltpu.roll(grad, DH, 1)
                    extra = jnp.where(lane == DH + 1, middle, jnp.where(lane == DH + 2, low, 0.0))
                    extra = jnp.where(lane == DH, high, extra)
                    da_ref[h, rows, :] = jnp.where(lane < DH, own, extra).astype(BF16)

    for j in range(steps):
        pl.when(step == j)(
            functools.partial(
                back_block, j, k_ref, v_ref, qa_ref, cos_ref, sin_ref, pg_ref, da_ref, turned_ref, chance_ref,
                score_ref,
            )
        )


def attend_back(pair, place, key_rows, value_rows, query_more, grads, outs, cosine, sine, *deps):
    keyed = pl.BlockSpec((2, KEYS, LANES), lambda i, s: (pair, i, 0))
    last = lambda g: g.shape[1] // LANES - 2
    quarters = [pl.BlockSpec((SEQ // 4, LANES), lambda i, s, at=last(g): (0, at + pair)) for g in (*grads, *outs)]
    table = pl.BlockSpec((KEYS, LANES), lambda i, s: (i, 0))
    return pl.pallas_call(
        back_kernel,
        grid_spec=pltpu.PrefetchScalarGridSpec(
            num_scalar_prefetch=1,
            grid=(SEQ // KEYS,),
            in_specs=[keyed, keyed, fixed((2, SEQ, LANES))] + quarters + [table, table] + [ANY] * len(deps),
            out_specs=pl.BlockSpec((KEYS, 3 * LANES), lambda i, s: (i, 0)),
            scratch_shapes=[
                pltpu.VMEM((2, SEQ, LANES), BF16),
                pltpu.VMEM((2, DH, SEQ), F32),
                pltpu.VMEM((2, KEYS, SEQ), BF16),
                pltpu.VMEM((2, KEYS, SEQ), BF16),
            ],
        ),
        out_shape=shaped((SEQ, 3 * LANES), BF16),
        compiler_params=params(60),
        cost_estimate=cost(0.5),
        name="attend_back",
    )(place, key_rows, value_rows, query_more, *grads, *outs, cosine, sine, *deps)


CHUNK = 512
HALF = 256
SCALE = math.sqrt(2.0 / math.pi)
CUBIC = 0.044715


def feed_kernel(place_ref, *refs):
    parts_in = refs[:4]
    x_ref, cot_ref, weight_ref, gain_ref, bias_ref = refs[4:9]
    (w_out, out_sib), (up_sib, w_up), (both_sib_y, both_y), downs = refs[9:11], refs[11:13], refs[13:15], refs[15:19]
    down_ref, up_ref, out_ref, own_act, own_hidden, final_ref, state_ref, sum_ref = refs[19:27]
    out_w, up_w, down_w, slope_ref, mid_ref, aunit_ref, munit_ref, ainv_ref, minv_ref, sums, sems = refs[30:]
    tokens, width = x_ref.shape
    local = out_w.shape[1]
    outs = [w_out, both_y.at[pl.ds(width, local)], out_sib, both_sib_y.at[pl.ds(width, local)]]
    ups = [up_sib, both_sib_y.at[pl.ds(0, width)], w_up, both_y.at[pl.ds(0, width)]]
    features = [refs[27], refs[28], down_ref.at[:, 3 * width :], refs[29]]
    mlp_ref, sib_act = down_ref.at[:, 0:width], down_ref.at[:, width : 3 * width]
    mn_ref, sib_hidden = up_ref.at[:, 0:width], up_ref.at[:, width : 3 * width]
    branch_ref = out_ref.at[:, 0:width]
    out_ref[:, width:] = parts_in[3][...]

    loads = []
    for at, (sources, target) in enumerate(((outs, out_w), (ups, up_w), (downs, down_w))):
        for k, source in enumerate(sources):
            loads.append(pltpu.make_async_copy(source, target.at[k], sems.at[4 * at + k]))
    for load in loads:
        load.start()
    sums[...] = jnp.zeros_like(sums)

    def add_sum(k, field):
        part = field[0:8]
        for i in range(8, field.shape[0], 8):
            part = part + field[i : i + 8]
        sums[k] += part

    halves = [range(h, h + HALF, PART) for h in range(0, tokens, HALF)]

    for load in loads[:4]:
        load.wait()
    for parts in halves:
        rows = slice(parts.start, parts.stop)
        branch = None
        for k, part_ref in enumerate(parts_in):
            term = product(part_ref[rows, :], out_w[k])
            branch = term if branch is None else branch + term
        for begin in parts:
            r = slice(begin, begin + PART)
            aunit, ainv = normalize(branch[begin - parts.start : begin - parts.start + PART])
            middle = x_ref[r, :].astype(F32) + aunit * gain_ref[1:2, :] + bias_ref[1:2, :]
            munit, minv = normalize(middle)
            mid_ref[r, :] = middle
            aunit_ref[r, :] = aunit
            munit_ref[r, :] = munit
            ainv_ref[r, :] = jnp.broadcast_to(ainv, (PART, LANES))
            minv_ref[r, :] = jnp.broadcast_to(minv, (PART, LANES))
            mn_ref[r, :] = (munit * gain_ref[2:3, :] + bias_ref[2:3, :]).astype(BF16)

    for k in range(4):
        loads[4 + k].wait()
        act_ref, columns = (sib_act, own_act)[k // 2], slice(k % 2 * width, (k % 2 + 1) * width)
        for parts in halves:
            value = product(mn_ref[parts.start : parts.stop, :], up_w[k])
            for i in range(0, HALF, 16):
                r = slice(parts.start + i, parts.start + i + 16)
                v = value[i : i + 16]
                square = v * v
                bent = jnp.tanh(v * (SCALE + (SCALE * CUBIC) * square))
                half = 0.5 + 0.5 * bent
                act_ref[r, columns] = (v * half).astype(BF16)
                slope = half + v * (1.0 - bent * bent) * (0.5 * SCALE + (1.5 * SCALE * CUBIC) * square)
                slope_ref[k, r, :] = slope.astype(BF16)

    for load in loads[8:]:
        load.wait()
    for parts in halves:
        rows = slice(parts.start, parts.stop)
        branch = None
        for k in range(4):
            act_ref, columns = (sib_act, own_act)[k // 2], slice(k % 2 * width, (k % 2 + 1) * width)
            term = product(act_ref[rows, columns], down_w[k])
            branch = term if branch is None else branch + term
        for begin in parts:
            r = slice(begin, begin + PART)
            unit, inverse = normalize(branch[begin - parts.start : begin - parts.start + PART])
            final_ref[r, :] = (mid_ref[r, :] + unit * gain_ref[3:4, :] + bias_ref[3:4, :]).astype(BF16)
            grad = cot_ref[r, :].astype(F32) * weight_ref[r, :1]
            add_sum(3, grad * unit)
            add_sum(7, grad)
            mlp_ref[r, :] = norm_back(grad, unit, inverse, gain_ref[3:4, :]).astype(BF16)

    mid_grads = []
    for parts in halves:
        rows = slice(parts.start, parts.stop)
        mid_grad = None
        for k in range(4):
            hid_ref, columns = (sib_hidden, own_hidden)[k // 2], slice(k % 2 * width, (k % 2 + 1) * width)
            act_grad = product_nt(mlp_ref[rows, :], down_w[k])
            hidden = (slope_ref[k, rows, :].astype(F32) * act_grad).astype(BF16)
            hid_ref[rows, columns] = hidden
            term = product_nt(hidden, up_w[k])
            mid_grad = term if mid_grad is None else mid_grad + term
        mid_grads.append(mid_grad)
    for parts, mid_all in zip(halves, mid_grads):
        rows = slice(parts.start, parts.stop)
        for begin in parts:
            r = slice(begin, begin + PART)
            mid_grad, munit, aunit = mid_all[begin - parts.start : begin - parts.start + PART], munit_ref[r, :], aunit_ref[r, :]
            grad = cot_ref[r, :].astype(F32) * weight_ref[r, :1]
            state = grad + norm_back(mid_grad, munit, minv_ref[r, :1], gain_ref[2:3, :])
            state_ref[r, :] = state
            branch_ref[r, :] = norm_back(state, aunit, ainv_ref[r, :1], gain_ref[1:2, :]).astype(BF16)
            for k, term in ((1, state * aunit), (2, mid_grad * munit), (5, state), (6, mid_grad)):
                add_sum(k, term)
        for k in (1, 2, 3, 0):
            features[k][rows, :] = product_nt(branch_ref[rows, :], out_w[k]).astype(BF16)
    for k in range(8):
        sum_ref[k : k + 1, :] = column_sum(sums[k])


def feed(place, parts, inputs, cot, weight, gains, biases, outs, ups, both, downs):
    width = inputs.shape[1]
    quarter = inputs.shape[0] // 4
    hid = 2 * width
    local = outs[0].shape[0]
    in_place = lambda s, t: (t[0], 0)
    stat = fixed((quarter, LANES))
    part = (quarter, local)
    shapes = [(quarter, 3 * width + local), (quarter, 3 * width), (quarter, width + local)] + [(quarter, hid)] * 2 + [(quarter, width)] * 2
    kinds = [BF16] * 6 + [F32]
    shapes, kinds = shapes + [(8, width)] + [part] * 3, kinds + [F32] + [BF16] * 3
    return pl.pallas_call(
        feed_kernel,
        grid_spec=pltpu.PrefetchScalarGridSpec(
            num_scalar_prefetch=1,
            grid=(1,),
            in_specs=[fixed(part)] * 4
            + [pl.BlockSpec((quarter, width), in_place)] * 2
            + [stat, fixed((4, width)), fixed((4, width))]
            + [ANY] * 10,
            out_specs=[fixed(shape) for shape in shapes],
            scratch_shapes=[
                pltpu.VMEM((4, local, width), BF16),
                pltpu.VMEM((4, width, width), BF16),
                pltpu.VMEM((4, width, width), BF16),
                pltpu.VMEM((4, quarter, width), BF16),
            ]
            + [pltpu.VMEM((quarter, width), F32)] * 3
            + [pltpu.VMEM((quarter, LANES), F32)] * 2
            + [pltpu.VMEM((8, 8, width), F32), pltpu.SemaphoreType.DMA((12,))],
        ),
        out_shape=[shaped(shape, kind) for shape, kind in zip(shapes, kinds)],
        compiler_params=params(60),
        cost_estimate=cost(34),
        name="feed",
    )(place, *parts, inputs, cot, weight, gains, biases, *outs, *ups, *both, *downs)


def keep_and_send(own, bit, field, keep_ref, send_ref):
    blocks, rows = send_ref.shape[0], send_ref.shape[2]
    for j in range(blocks):
        low = j // bit * 2 * bit + j % bit
        for ref, value in ((keep_ref, own), (send_ref, 1 - own)):
            begin = pl.multiple_of((low + value * bit) * rows, 16)
            ref[j, 0] = field[pl.ds(begin, rows), :]


def weight_kernel(bits, own_ref, x1, x2, y1, y2, *more):
    outs, field_ref = more[-5:-1], more[-1]
    step = pl.program_id(0)
    field = lax.dot_general(x1[...], y1[...], TN, preferred_element_type=F32)
    field = field + lax.dot_general(x2[...], y2[...], TN, preferred_element_type=F32)
    field_ref[...] = field.astype(BF16)
    for half, bit in enumerate(bits):
        keep_ref, send_ref = outs[2 * half : 2 * half + 2]
        if bit == "y":
            rows = keep_ref.shape[2]
            for k, ref in enumerate((keep_ref, send_ref)):

                @pl.when(step == 2 * half + k)
                def _(ref=ref):
                    for j in range(ref.shape[0]):
                        ref[j, 0] = field_ref[j * rows : (j + 1) * rows, :]

        else:

            @pl.when(step // 2 == half)
            def _(bit=bit, keep_ref=keep_ref, send_ref=send_ref):
                keep_and_send(own_ref[own_ref.shape[0] - bit], bit, field_ref, keep_ref, send_ref)


def weight_grad(own_bits, bits, mine, got, y1, name, *deps):
    rows, width = mine.shape[0], y1.shape[1] // 2
    size = lax.axis_size("dp")
    y_spec = lambda first: pl.BlockSpec((rows, CHUNK), lambda s, o: (0, first + s // 2 + 2 * (s % 2)))
    shape = (size, 1, width // size, CHUNK)
    specs = []
    for half, bit in enumerate(bits):
        if bit == "y":
            specs += [fixed(shape)] * 2
        else:
            part = (size // 2,) + shape[1:]
            specs += [pl.BlockSpec(part, lambda s, o, half=half: (jnp.clip(s - 2 * half, 0, 1), 0, 0, 0))] * 2
    return pl.pallas_call(
        functools.partial(weight_kernel, bits),
        grid_spec=pltpu.PrefetchScalarGridSpec(
            num_scalar_prefetch=1,
            grid=(4,),
            in_specs=[fixed((rows, width))] * 2 + [y_spec(0), y_spec(width // CHUNK)] + [ANY] * len(deps),
            out_specs=specs,
            scratch_shapes=[pltpu.VMEM((width, CHUNK), BF16)],
        ),
        out_shape=[shaped(shape, BF16)] * 4,
        compiler_params=params(60),
        cost_estimate=cost(0),
        name=name,
    )(own_bits, mine, got, y1, got, *deps)


def out_weight_kernel(mine_ref, got_ref, own_ref, theirs_ref, own_sib_ref, *more):
    width = more[-1].shape[0] * more[-1].shape[2]
    x1, x2 = mine_ref[:, :width], got_ref[:, :width]
    for out_ref, left, right in ((more[-2], own_ref, own_sib_ref), (more[-1], theirs_ref, got_ref.at[:, width:])):
        field = lax.dot_general(x1, left[...], TN, preferred_element_type=F32)
        field = field + lax.dot_general(x2, right[...], TN, preferred_element_type=F32)
        blocks, unused, rows, unused = out_ref.shape
        for j in range(blocks):
            out_ref[j, 0] = field[j * rows : (j + 1) * rows].astype(BF16)


def out_weight_grad(mine, got, own, theirs, own_sib, *deps):
    rows, local = own.shape
    width = mine.shape[1] - local
    size = lax.axis_size("dp")
    shape = (size, 1, width // size, local)
    arrays = [mine, got, own, theirs, own_sib]
    return pl.pallas_call(
        out_weight_kernel,
        grid=(1,),
        in_specs=[fixed(a.shape) for a in arrays] + [ANY] * len(deps),
        out_specs=[fixed(shape)] * 2,
        out_shape=[shaped(shape, BF16)] * 2,
        compiler_params=params(60),
        cost_estimate=cost(0),
        name="out_weight_grad",
    )(*arrays, *deps)


def in_back_kernel(order_ref, p0, p1, w_ref, x_ref, feed_ref, *more):
    send_ref, keep_ref, sum_ref, sums, field_ref = more[-5:]
    step = pl.program_id(0)
    block = x_ref.shape[0]

    @pl.when(step == 0)
    def _():
        sums[...] = jnp.zeros_like(sums)

    field = None
    for c in range(3):
        cut = slice(c * LANES, (c + 1) * LANES)
        left = jnp.concatenate([p0[:, cut], p1[:, cut]], axis=1)
        term = product_nt(left, w_ref[c])
        field = term if field is None else field + term
    gain_part = bias_part = 0.0
    for begin in range(0, block, PART):
        r = slice(begin, begin + PART)
        unit, unused = normalize(x_ref[r, :].astype(F32))
        field_ref[r, :] = field[r].astype(BF16)
        scaled = field[r] * unit
        for i in range(0, PART, 8):
            gain_part = gain_part + scaled[i : i + 8]
            bias_part = bias_part + field[begin + i : begin + i + 8]
    sums[0] += gain_part
    sums[1] += bias_part

    @pl.when(step // 2 % 2 == 0)
    def _():
        send_ref[...] = field_ref[...]

    @pl.when(step // 2 % 2 == 1)
    def _():
        keep_ref[...] = field_ref[...]

    @pl.when(step == 7)
    def _():
        sum_ref[...] = feed_ref[...]
        for k in range(2):
            sum_ref[4 * k : 4 * k + 1, :] = column_sum(sums[k])


def in_back(place, parts, w_qkv, inputs, feed_sums, *deps):
    block = 256
    tokens, width = inputs.shape
    rows = lambda s, o: (2 * (o[0] ^ (3 - s // 2)) + s % 2, 0)
    shapes = [(tokens // 2, width), (tokens // 2, width), (8, width)]
    return pl.pallas_call(
        in_back_kernel,
        grid_spec=pltpu.PrefetchScalarGridSpec(
            num_scalar_prefetch=1,
            grid=(8,),
            in_specs=[pl.BlockSpec((block, 3 * LANES), rows)] * 2
            + [fixed(w_qkv.shape), pl.BlockSpec((block, width), rows), fixed((8, width))]
            + [ANY] * len(deps),
            out_specs=[
                pl.BlockSpec((block, width), lambda s, o: (s // 4 * 2 + jnp.minimum(s % 4, 1), 0)),
                pl.BlockSpec((block, width), lambda s, o: (s // 4 * 2 + jnp.maximum(s % 4 - 2, 0), 0)),
                fixed(shapes[2]),
            ],
            scratch_shapes=[pltpu.VMEM((2, 8, width), F32), pltpu.VMEM((block, width), BF16)],
        ),
        out_shape=[shaped(shapes[0], BF16), shaped(shapes[1], BF16), shaped(shapes[2], F32)],
        compiler_params=params(60),
        cost_estimate=cost(1),
        name="in_back",
    )(place, *parts, w_qkv, inputs, feed_sums, *deps)


def qkv_kernel(own_ref, n_ref, p_ref, *more):
    keep_ref, send_ref, field_ref = more[-3:]
    rows = n_ref.shape[0]
    for k in range(field_ref.shape[0] // rows):

        @pl.when(pl.program_id(0) == k)
        def _(k=k):
            field_ref[k * rows : (k + 1) * rows, :] = product(n_ref[...], p_ref[...]).astype(BF16)

    @pl.when(pl.program_id(0) == pl.num_programs(0) - 1)
    def _():
        keep_and_send(own_ref[own_ref.shape[0] - 3], 4, field_ref, keep_ref, send_ref)


def qkv_grad(own_bits, normed_turned, part, *deps):
    width, tokens = normed_turned.shape
    columns = part.shape[1]
    size = lax.axis_size("dp")
    steps = 2
    shape = (size // 2, 1, width // size, columns)
    return pl.pallas_call(
        qkv_kernel,
        grid_spec=pltpu.PrefetchScalarGridSpec(
            num_scalar_prefetch=1,
            grid=(steps,),
            in_specs=[pl.BlockSpec((width // steps, tokens), lambda i, o: (i, 0)), fixed(part.shape)] + [ANY] * len(deps),
            out_specs=[fixed(shape)] * 2,
            scratch_shapes=[pltpu.VMEM((width, columns), BF16)],
        ),
        out_shape=[shaped(shape, BF16)] * 2,
        compiler_params=params(60),
        cost_estimate=cost(0),
        name="qkv_grad",
    )(own_bits, normed_turned, part, *deps)


def add_kernel(keep_ref, got_ref, *more):
    for begin in range(0, keep_ref.shape[0], PART):
        r = slice(begin, begin + PART)
        more[-1][r, :] = total([keep_ref[r, :], got_ref[r, :]]).astype(BF16)


def add_core(keep, got, *deps):
    rows, width = keep.shape[0] // 2, keep.shape[1]
    block = rows // 2
    spec = pl.BlockSpec((block, width), lambda i: (i, 0))
    return pl.pallas_call(
        add_kernel,
        grid=(2,),
        in_specs=[spec, spec] + [ANY] * len(deps),
        out_specs=spec,
        out_shape=shaped((rows, width), BF16),
        compiler_params=params(60),
        cost_estimate=cost(3),
        name="add_core",
    )(keep, got, *deps)


def finish_kernel(place_ref, x_ref, state_ref, keep_ref, near_ref, far_ref, gain_ref, *more):
    out_ref = more[-1]
    for begin in range(0, x_ref.shape[0], PART):
        r = slice(begin, begin + PART)
        unit, inverse = normalize(x_ref[r, :].astype(F32))
        grad = total([keep_ref[r, :], near_ref[r, :], far_ref[r, :]])
        out_ref[r, :] = state_ref[r, :] + norm_back(grad, unit, inverse, gain_ref[0:1, :])


def finish(place, inputs, state, keep, near, far, gains, *deps):
    quarter, width = state.shape
    block = 128
    steps = quarter // block
    spec = pl.BlockSpec((block, width), lambda s, t: (s, 0))
    return pl.pallas_call(
        finish_kernel,
        grid_spec=pltpu.PrefetchScalarGridSpec(
            num_scalar_prefetch=1,
            grid=(steps,),
            in_specs=[pl.BlockSpec((block, width), lambda s, t: (t[0] * steps + s, 0)), spec]
            + [pl.BlockSpec((block, width), lambda s, t: (steps + s, 0))] * 2
            + [spec]
            + [fixed(gains.shape)]
            + [ANY] * len(deps),
            out_specs=spec,
        ),
        out_shape=shaped((quarter, width), F32),
        compiler_params=params(60),
        cost_estimate=cost(0),
        name="finish",
    )(place, inputs, state, keep, near, far, gains, *deps)


def per_device(
    inputs, w_qkv, w_out, w_up, w_down, norm_gains, norm_biases, out_cot, group_ids, group_weights
):
    tokens, width = inputs.shape
    quarter = tokens // 4
    place = lax.axis_index("tensor")
    where = place.astype(jnp.int32).reshape(1)
    dp_size = lax.axis_size("dp")
    cosine, sine = rotary_tables()

    dp_index = lax.axis_index("dp").astype(jnp.int32)
    mine = (dp_index % 4).reshape(1)
    owns = jnp.stack([jnp.int32(0)] + [(dp_index // kind) % 2 for kind in dp_kinds()])

    own_ids = lax.dynamic_slice_in_dim(group_ids, place * quarter, quarter, 0)
    groups = jnp.arange(group_weights.shape[0], dtype=jnp.int32)
    lookup = (own_ids[:, None] == groups[None, :]).astype(F32)
    row_weight = jnp.sum(lookup * group_weights[None, :], axis=1, keepdims=True)
    row_weight = jnp.broadcast_to(row_weight, (quarter, LANES))

    up_rows, out_rows, down_rows = w_up.shape[0] // 4, w_out.shape[0] // 4, w_down.shape[0] // 4
    zero = lambda m: 0
    up_sent, down_sent, down_last = move_rows(
        mine,
        [w_up, w_out, w_down],
        [(up_rows + out_rows, width), (down_rows, width), (down_rows, width)],
        [
            (0, lambda m: m * up_rows, 0, zero, up_rows),
            (1, lambda m: m * out_rows, 0, lambda m: up_rows, out_rows),
            (2, lambda m: m * down_rows, 1, zero, down_rows),
            (2, lambda m: (m ^ 3) * down_rows, 2, zero, down_rows),
        ],
        "take",
    )

    def halves(one, two, name):
        rows = one.shape[0] // 2
        moves = [(1, zero, 0, zero, rows), (0, lambda m: rows, 1, zero, rows)]
        low, high = move_rows(mine, [one, two], [(rows, width)] * 2, moves, name)
        return swap(low, "dp", 1), swap(high, "dp", 2), low

    def quarter_moves(target, first, rows, begin, count):
        return [
            (which, lambda m: begin, target, lambda m, which=which: first + (m ^ which) * rows, rows)
            for which in range(count)
        ]

    up_got = y_swap(up_sent)
    up_sib, down_sib, out_sib = core_swap(w_up), core_swap(w_down), core_swap(w_out)
    normed_turned, query, key_rows, value_rows = project(
        inputs, w_qkv, norm_gains, norm_biases, cosine, sine, up_sent
    )
    down_sent = gate(down_sent, normed_turned)
    down_got = y_swap(down_sent)
    up_got = gate(up_got, down_sent)
    up_one, up_two = swap(up_got, "dp", 1), swap(up_got, "dp", 2)

    *outs, more_first = attend(0, where, query, key_rows, value_rows, [], up_got, up_sib, down_sib, out_sib)
    down_got = gate(down_got, outs[0])
    down_one, down_two = swap(down_got, "dp", 1), swap(down_got, "dp", 2)
    down_last = gate(down_last, down_got)
    down_three = y_swap(down_last)
    up_one = gate(up_one, down_last)
    up_low, up_high, last = halves(up_one, up_two, "up_halves")
    *outs, more_second = attend(1, where, query, key_rows, value_rows, outs, last, down_last)
    fetched = (up_low, up_high, down_one, down_two, down_three)
    outs = outs[:1] + [gate(out, *fetched) for out in outs[1:]]
    rows = [outs[0], core_swap(outs[1]), y_swap(outs[2]), diagonal_swap(outs[3], 0, 3)]
    up_one = gate(up_one, outs[1], outs[2], outs[3])

    def last_moves(target, first, rows, begin, half):
        low = max(0, min(half - begin, rows))
        moves = [(3, lambda m: begin, target, lambda m: first + (m ^ 3) * rows, low)] if low else []
        start = begin + low - half
        return moves + [(4, lambda m: start, target, lambda m: first + (m ^ 3) * rows + low, rows - low)]

    half = (up_rows + out_rows) // 2
    (upout_y,) = move_rows(
        mine,
        [up_got, up_one, up_two, up_low, up_high],
        [(w_up.shape[0] + w_out.shape[0], width)],
        quarter_moves(0, 0, up_rows, 0, 3)
        + quarter_moves(0, w_up.shape[0], out_rows, up_rows, 3)
        + last_moves(0, 0, up_rows, 0, half)
        + last_moves(0, w_up.shape[0], out_rows, up_rows, half),
        "up_whole",
    )
    upout_sib_y = core_swap(upout_y)
    down_one = gate(down_one, upout_y)
    (down_y,) = move_rows(
        mine,
        [down_got, down_one, down_two, down_three],
        [w_down.shape],
        quarter_moves(0, 0, down_rows, 0, 4),
        "down_whole",
    )
    down_sib_y = core_swap(down_y)

    for_down, for_up, for_out, own_act, own_hidden, final_rows, state_grad, sums_feed, own, for_y, for_far = feed(
        where, [rows[0], rows[2], rows[1], rows[3]], inputs, out_cot, row_weight, norm_gains, norm_biases,
        [w_out, out_sib], [up_sib, w_up], [upout_sib_y, upout_y], [down_sib, down_sib_y, w_down, down_y],
    )

    down_got = core_swap(for_down)
    grads = [own, down_got, y_swap(for_y), diagonal_swap(for_far, 0, 3)]
    for_up = gate(for_up, down_got)
    up_got = core_swap(for_up)
    kinds = dp_kinds()
    both = ["y"] + kinds
    without = lambda bits, *gone: [b for b in bits if b not in gone]
    newest = lambda *items: [item.addends[-1][0] for item in items]
    d0_keep, d0_send, d1_keep, d1_send = weight_grad(
        owns, ("y", 1), for_down, down_got, own_act, "down_grad", for_up
    )
    d0 = Item(kinds, d0_keep, y_swap(d0_send))
    d1 = Item(without(both, 1), d1_keep, swap(d1_send, "dp", 1))
    u0_keep, u0_send, u1_keep, u1_send = weight_grad(
        owns, (1, 2), for_up, up_got, own_hidden, "up_grad", d0_send, d1_send, *grads[2:]
    )
    u1 = Item(without(both, 2), u1_keep, swap(u1_send, "dp", 2))
    for_out = gate(for_out, u1_send)
    out_got = core_swap(for_out)
    part_first = attend_back(
        0, where, key_rows, value_rows, more_first, grads, outs, cosine, sine, u1_send, for_out
    )
    u0_send = gate(u0_send, part_first)
    u0 = Item(without(both, 1), u0_keep, swap(u0_send, "dp", 1))
    out_keep, out_send = out_weight_grad(for_out, out_got, rows[0], rows[2], outs[1], u0_send)
    out_item = Item(kinds, out_keep, y_swap(out_send))

    def qkv_item(part, *deps):
        keep, send = qkv_grad(owns, normed_turned, part, *deps)
        return Item(without(kinds, 4), keep, swap(send, "dp", 4)), send

    q0, last = qkv_item(part_first, out_send)
    last = halve(owns, [d1], 2, last)
    part_second = attend_back(
        1, where, key_rows, value_rows, more_second, grads, outs, cosine, sine, last, *newest(d0, u1)
    )
    part_second = gate(part_second, *newest(u0), micros=3)
    parts = [part_first, part_second]

    send, keep, sums = in_back(where, parts, w_qkv, inputs, sums_feed, *newest(d1, q0, out_item))
    core_got = core_swap(send)
    last = halve(owns, [u1, d0], 1, send)
    last = halve(owns, [u0, out_item], 2, last)
    far = add_core(keep, core_got, last)
    far_got = y_swap(far)
    q1, last = qkv_item(part_second, far)
    last = gate(last, *newest(u1), micros=3)
    last = gate(last, *newest(u0), micros=3)
    last = send_last(owns, [d1, u0, u1], last, far_got)
    last = halve(owns, [q0, q1, out_item], 1, last)
    last = halve(owns, [d0], 2, last)
    input_grad = finish(where, inputs, state_grad, keep, core_got, far_got, norm_gains, last)
    last = send_last(owns, [q0, q1, d0, out_item], input_grad)
    share = width // (4 * dp_size)
    sums = gate(sums, last)
    sums = sums.reshape(8, 4 * dp_size, share).transpose(1, 0, 2)
    sums = jnp.sum(lax.all_to_all(sums, ("dp", "tensor"), 0, 0, tiled=True), axis=0)
    last = gate(last, *[a[0] for a in u0.addends[-3:]], micros=6)
    up_total, down_total, out_total, qkv_total = finals(
        owns, [[(u0, False), (u1, False)], [(d0, True), (d1, True)], [(out_item, True)]], [q0, q1], last
    )
    return (
        final_rows,
        input_grad,
        qkv_total,
        out_total,
        up_total,
        down_total,
        sums[:4],
        sums[4:],
    )


def solution(mesh):
    placed = (
        P("dp", None),
        P(None, None, "tensor"),
        P("tensor", None),
        P(None, "tensor"),
        P("tensor", None),
        P(),
        P(),
        P("dp", None),
        P("dp"),
        P(),
    )
    return jax.shard_map(
        per_device,
        mesh=mesh,
        in_specs=placed,
        out_specs=(
            P(("dp", "tensor"), None),
            P(("dp", "tensor"), None),
            P(None, "dp", "tensor"),
            P("tensor", "dp"),
            P("dp", "tensor"),
            P("tensor", "dp"),
            P(None, ("dp", "tensor")),
            P(None, ("dp", "tensor")),
        ),
        check_vma=False,
    )
```

```python
import functools
import math

import jax
import jax.numpy as jnp
import numpy as np
from jax import lax
from jax.experimental import pallas as pl
from jax.experimental.pallas import tpu as pltpu
from jax.sharding import PartitionSpec as P

DH = 64
SEQ = 2048
EPS = 1e-05
PART = 32
F32 = jnp.float32
BF16 = jnp.bfloat16
LANES = 128
NT = (((1,), (1,)), ((), ()))
TN = (((0,), (0,)), ((), ()))
ANY = pl.BlockSpec(memory_space=pl.ANY)


def params(mebibytes=60):
    return pltpu.CompilerParams(vmem_limit_bytes=mebibytes * 2**20)


def cost(micros):
    return pl.CostEstimate(flops=int(micros * 1.1e9), bytes_accessed=2**16, transcendentals=0)


def shaped(shape, kind):
    return jax.ShapeDtypeStruct(shape, kind)


def fixed(shape):
    return pl.BlockSpec(shape, lambda *unused: (0,) * len(shape))


def gate(field, *deps, micros=0):
    return pl.pallas_call(
        lambda *refs: None,
        in_specs=[ANY] * (1 + len(deps)),
        out_specs=ANY,
        out_shape=shaped(field.shape, field.dtype),
        input_output_aliases={0: 0},
        cost_estimate=cost(micros),
        name="gate",
    )(field, *deps)


def swap(field, axis, bit):
    size = lax.axis_size(axis)
    return lax.ppermute(field, axis, [(i, i ^ bit) for i in range(size)])


def core_swap(field):
    return swap(field, "tensor", 1)


def y_swap(field):
    return swap(field, "tensor", 2)


def total(addends):
    return sum(a.astype(F32) for a in addends)


def diagonal_swap(field, dp_bits, tensor_bits):
    mask = 4 * dp_bits + tensor_bits
    size = 4 * lax.axis_size("dp")
    return lax.ppermute(field, ("dp", "tensor"), [(i, i ^ mask) for i in range(size)])


def move_rows(number, sources, targets, moves, name):
    def kernel(number_ref, *refs):
        source_refs, target_refs, sems = refs[: len(sources)], refs[len(sources) : -1], refs[-1]
        copies = []
        for at, (source, begin, target, end, rows) in enumerate(moves):
            begin, end = (pl.multiple_of(f(number_ref[0]), 16) for f in (begin, end))
            copies.append(
                pltpu.make_async_copy(
                    source_refs[source].at[pl.ds(begin, rows)], target_refs[target].at[pl.ds(end, rows)], sems.at[at]
                )
            )
        for copy in copies:
            copy.start()
        for copy in copies:
            copy.wait()

    return pl.pallas_call(
        kernel,
        grid_spec=pltpu.PrefetchScalarGridSpec(
            num_scalar_prefetch=1,
            grid=(1,),
            in_specs=[ANY] * len(sources),
            out_specs=[fixed(t) for t in targets],
            scratch_shapes=[pltpu.SemaphoreType.DMA((len(moves),))],
        ),
        out_shape=[shaped(t, BF16) for t in targets],
        compiler_params=params(60),
        cost_estimate=cost(1.5),
        name=name,
    )(number, *sources)


def dp_kinds():
    return [1 << k for k in reversed(range(lax.axis_size("dp").bit_length() - 1))]


class Item:
    def __init__(self, left, *arrays):
        self.left = list(left)
        self.addends = [(array, 0, list(left)) for array in arrays]
        self.shape = arrays[0].shape[2:]


def block_index(kinds, bits, free, flips):
    def index(g, own_ref):
        at = 0
        for bit in bits:
            if bit in free:
                value = (g >> (len(free) - 1 - free.index(bit))) & 1
            else:
                value = own_ref[kinds.index(bit)]
                flip = flips(g, bit)
                value = value + flip - 2 * value * flip
            at = 2 * at + value
        return at

    return index


def addend_specs(items, kinds, frees, flips):
    specs, arrays = [], []
    for item, free in zip(items, frees):
        rows, columns = item.shape
        for array, first, bits in item.addends:
            at = block_index(kinds, bits, free, flips)
            fits = array.shape[3] % columns == 0 and first % columns == 0
            block, column = (columns, first // columns) if fits else (array.shape[3], 0)
            specs.append(
                pl.BlockSpec((1, 1, rows, block), lambda g, own_ref, at=at, column=column: (at(g, own_ref), 0, 0, column))
            )
            arrays.append(array)
    return specs, arrays


def sums_of(items, refs):
    refs = iter(refs)
    fields = []
    for item in items:
        terms = []
        for array, first, bits in item.addends:
            ref = next(refs)
            begin = first if ref.shape[3] > item.shape[1] else 0
            terms.append(ref[0, 0, :, begin : begin + item.shape[1]])
        fields.append(total(terms))
    return fields


def put_beside(out_ref, fields):
    begin = 0
    for field in fields:
        out_ref[0, 0, :, begin : begin + field.shape[1]] = field.astype(BF16)
        begin += field.shape[1]


def received(items, got, lefts):
    begin = 0
    for item, left in zip(items, lefts):
        item.addends.append((got, begin, list(left)))
        begin += item.shape[1]


def packed(items):
    return (1, items[0].shape[0], sum(item.shape[1] for item in items))


def halve(owns, items, kind, *deps):
    kinds = ["y"] + dp_kinds()
    frees = [[b for b in item.left if b != kind] for item in items]
    steps = 2 ** len(frees[0])
    specs, arrays = addend_specs(items, kinds, frees, lambda g, bit: 1 if bit == kind else 0)
    shape = packed(items)

    def kernel(own_ref, *refs):
        put_beside(refs[-1], sums_of(items, refs))

    sent = pl.pallas_call(
        kernel,
        grid_spec=pltpu.PrefetchScalarGridSpec(
            num_scalar_prefetch=1,
            grid=(steps,),
            in_specs=specs + [ANY] * len(deps),
            out_specs=pl.BlockSpec((1,) + shape, lambda g, own_ref: (g, 0, 0, 0)),
        ),
        out_shape=shaped((steps,) + shape, BF16),
        compiler_params=params(60),
        cost_estimate=cost(3),
        name="halve",
    )(owns, *arrays, *deps)
    got = y_swap(sent) if kind == "y" else swap(sent, "dp", kind)
    received(items, got, frees)
    for item, free in zip(items, frees):
        item.left = free
    return sent


def send_last(owns, items, *deps):
    pair = ["y", 4] if "y" in items[0].left else [4, 2]
    for item in items:
        while [b for b in item.left if b not in pair]:
            deps = (halve(owns, [item], [b for b in item.left if b not in pair][0], *deps),)
    kinds = ["y"] + dp_kinds()
    masks = [[pair[1]], [pair[0]], pair]
    takers = [[i for i, item in enumerate(items) if all(b in item.left for b in mask)] for mask in masks]
    masks, takers = [m for m, t in zip(masks, takers) if t], [t for t in takers if t]

    def flips(g, bit):
        value = 0
        for k, mask in enumerate(masks):
            if bit in mask:
                value = jnp.where(g == k, 1, value)
        return value

    specs, arrays = addend_specs(items, kinds, [[] for item in items], flips)
    shapes = [(1,) + packed([items[i] for i in taker]) for taker in takers]

    def kernel(own_ref, *refs):
        fields = sums_of(items, refs)
        for k, taker in enumerate(takers):

            @pl.when(pl.program_id(0) == k)
            def _(k=k, taker=taker):
                put_beside(refs[k - len(masks)], [fields[i] for i in taker])

    sent = pl.pallas_call(
        kernel,
        grid_spec=pltpu.PrefetchScalarGridSpec(
            num_scalar_prefetch=1,
            grid=(len(masks),),
            in_specs=specs + [ANY] * len(deps),
            out_specs=[fixed(shape) for shape in shapes],
        ),
        out_shape=[shaped(shape, BF16) for shape in shapes],
        compiler_params=params(60),
        cost_estimate=cost(2),
        name="send_last",
    )(owns, *arrays, *deps)
    for field, mask, taker in zip(sent, masks, takers):
        got = diagonal_swap(field, sum(b for b in mask if b != "y"), 2 if "y" in mask else 0)
        received([items[i] for i in taker], got, [[]] * len(taker))
    for item in items:
        item.left = []
    return sent[-1]


def finals(owns, groups, heads, *deps):
    kinds = ["y"] + dp_kinds()
    items = [item for group in groups for item, turned in group] + heads
    specs, arrays = addend_specs(items, kinds, [[] for item in items], lambda g, bit: 0)
    shapes = []
    for group in groups:
        rows, columns = group[0][0].shape
        shapes.append((columns * len(group), rows) if group[0][1] else (rows, columns * len(group)))

    shapes.append((3, heads[0].shape[0], LANES * len(heads)))

    def kernel(own_ref, *refs):
        fields = sums_of(items, refs)
        for at, field in enumerate(fields[-len(heads) :]):
            for c in range(3):
                refs[-1][c, :, at * LANES : (at + 1) * LANES] = field[:, c * LANES : (c + 1) * LANES]
        fields = iter(fields)
        for group, out_ref in zip(groups, refs[-len(groups) - 1 :]):
            for i, (item, turned) in enumerate(group):
                cut = slice(i * item.shape[1], (i + 1) * item.shape[1])
                field = next(fields)
                if turned:
                    out_ref[cut, :] = jnp.transpose(field)
                else:
                    out_ref[:, cut] = field

    return pl.pallas_call(
        kernel,
        grid_spec=pltpu.PrefetchScalarGridSpec(
            num_scalar_prefetch=1,
            grid=(1,),
            in_specs=specs + [ANY] * len(deps),
            out_specs=[fixed(shape) for shape in shapes],
        ),
        out_shape=[shaped(shape, F32) for shape in shapes],
        compiler_params=params(60),
        cost_estimate=cost(3),
        name="finals",
    )(owns, *arrays, *deps)


def normalize(field):
    mean = jnp.mean(field, axis=-1, keepdims=True)
    centred = field - mean
    inverse = lax.rsqrt(jnp.mean(centred * centred, axis=-1, keepdims=True) + EPS)
    return centred * inverse, inverse


def norm_back(grad, unit, inverse, gain):
    scaled = grad * gain
    mean_one = jnp.mean(scaled, axis=-1, keepdims=True)
    mean_two = jnp.mean(scaled * unit, axis=-1, keepdims=True)
    return inverse * (scaled - mean_one - unit * mean_two)


def rotary_tables():
    half = DH // 2
    frequency = np.exp(np.arange(half, dtype=np.float32) * np.float32(-math.log(10000.0) / half))
    angles = np.arange(SEQ, dtype=np.float32)[:, None] * frequency.astype(np.float32)[None, :]
    cosine, sine = np.cos(angles), np.sin(angles)
    return (
        jnp.asarray(np.concatenate([cosine] * 4, axis=1).astype(np.float32)),
        jnp.asarray(np.concatenate([-sine, sine, -sine, sine], axis=1).astype(np.float32)),
    )


def lanes_of(shape):
    return lax.broadcasted_iota(jnp.int32, shape, 1)


def partner_lanes(field):
    lane = lanes_of(field.shape)
    return jnp.where(lane % DH < DH // 2, pltpu.roll(field, 96, 1), pltpu.roll(field, 32, 1))


def rotate(field, cosine, sine):
    return field * cosine + partner_lanes(field) * sine


def rotate_back(field, cosine, sine):
    return field * cosine - partner_lanes(field) * sine


def split_three(field):
    high = field.astype(BF16).astype(F32)
    rest = field - high
    middle = rest.astype(BF16).astype(F32)
    return high, middle, rest - middle


def product(left, right):
    return jnp.dot(left, right, preferred_element_type=F32)


def product_nt(left, right):
    return lax.dot_general(left, right, NT, preferred_element_type=F32)


def column_sum(field):
    return jnp.sum(field, axis=0, keepdims=True)


def project_kernel(x_ref, w_ref, gain_ref, bias_ref, cos_ref, sin_ref, *more):
    n_ref, q_ref, k_ref, v_ref, normed_ref = more[-5:]
    rows, width = x_ref.shape
    for i in range(rows // PART):
        r = slice(i * PART, (i + 1) * PART)
        unit, unused = normalize(x_ref[r, :].astype(F32))
        normed_ref[r, :] = (unit * gain_ref[0:1, :] + bias_ref[0:1, :]).astype(BF16)
    for i in range(width // 256):
        c = slice(i * 256, (i + 1) * 256)
        n_ref[c, :] = jnp.transpose(normed_ref[:, c])
    lane = lanes_of((PART, LANES))
    ones = jnp.where(lane < DH + 3, 1.0, 0.0)
    for which, out_ref in enumerate((q_ref, k_ref, v_ref)):
        both = product(normed_ref[...], w_ref[which])
        for i in range(rows // PART):
            r = slice(i * PART, (i + 1) * PART)
            for pair in range(both.shape[1] // LANES):
                field = both[r, pair * LANES : (pair + 1) * LANES]
                if which < 2:
                    field = rotate(field, cos_ref[r, :], sin_ref[r, :])
                if which == 0:
                    field = field * (1.0 / math.sqrt(DH))
                extra = jnp.zeros_like(field) if which == 0 else ones
                out_ref[2 * pair, r, :] = jnp.where(lane < DH, field, extra).astype(BF16)
                out_ref[2 * pair + 1, r, :] = jnp.where(lane < DH, pltpu.roll(field, DH, 1), extra).astype(BF16)


def project(inputs, w_qkv, gain, bias, cosine, sine, *deps):
    block = 256
    tokens, width = inputs.shape
    local = w_qkv.shape[2]
    heads = local // DH
    rows = lambda i: (i, 0)
    per_head = pl.BlockSpec((heads, block, LANES), lambda i: (0, i, 0))
    headed = shaped((heads, tokens, LANES), BF16)
    return pl.pallas_call(
        project_kernel,
        grid=(tokens // block,),
        in_specs=[
            pl.BlockSpec((block, width), rows),
            fixed((3, width, local)),
            fixed((4, width)),
            fixed((4, width)),
            pl.BlockSpec((block, LANES), rows),
            pl.BlockSpec((block, LANES), rows),
        ]
        + [ANY] * len(deps),
        out_specs=[pl.BlockSpec((width, block), lambda i: (0, i)), per_head, per_head, per_head],
        out_shape=[shaped((width, tokens), BF16), headed, headed, headed],
        scratch_shapes=[pltpu.VMEM((block, width), BF16)],
        compiler_params=params(60),
        cost_estimate=cost(10),
        name="project",
    )(inputs, w_qkv, gain, bias, cosine, sine, *deps)


ROWS = 512
KEYS = 512
STRIP = 256


def hidden_keys(shape, down, across):
    return lax.broadcasted_iota(jnp.int32, shape, 0) + down > lax.broadcasted_iota(jnp.int32, shape, 1) + across


def attend_block(n, place_ref, q_ref, k_ref, v_ref, out_refs, qa_ref, score_ref, chance_ref):
    start, end = n * ROWS, (n + 1) * ROWS
    row = lax.broadcasted_iota(jnp.int32, (LANES, ROWS), 0)
    lane = lanes_of((ROWS, LANES))
    outs = []
    for h in range(2):
        most = None
        for begin in range(0, end, STRIP):
            scores = product_nt(k_ref[h, begin : begin + STRIP, :], q_ref[h])
            if begin >= start:
                scores = jnp.where(hidden_keys((STRIP, ROWS), begin, start), -1e30, scores)
            score_ref[h, begin : begin + STRIP, :] = scores
            for i in range(0, STRIP, 8):
                most = scores[i : i + 8] if most is None else jnp.maximum(most, scores[i : i + 8])
        top = jnp.max(most, axis=0, keepdims=True)
        for begin in range(0, end, PART):
            r = slice(begin, begin + PART)
            chance_ref[h, r, :] = jnp.exp(score_ref[h, r, :] - top).astype(BF16)
        both = lax.dot_general(v_ref[h, :end, :], chance_ref[h, :end, :], TN, preferred_element_type=F32)
        summed = both[DH : DH + 1, :]
        high, middle, low = split_three(-(top + jnp.log(summed)))
        extra = jnp.where(row == DH + 1, middle, jnp.where(row == DH + 2, low, 0.0))
        extra = jnp.where(row == DH, high, extra)
        turned = jnp.transpose(jnp.where(row < DH, both * (1.0 / summed), extra))
        qa_ref[h] = jnp.where(lane < DH, q_ref[h].astype(F32), turned).astype(BF16)
        outs.append(turned)
    both = jnp.where(lane < DH, outs[0], pltpu.roll(outs[1], DH, 1)).astype(BF16)
    for which, out_ref in enumerate(out_refs):

        @pl.when((place_ref[0] ^ which) == n)
        def _(out_ref=out_ref):
            out_ref[...] = both


def attend_kernel(place_ref, q_ref, k_ref, v_ref, *more):
    block = pl.program_id(0)
    keys_ref, values_ref = more[-2:]
    for n in range(SEQ // ROWS):

        @pl.when(block == n)
        def _(n=n):
            keys_ref[:, n * ROWS : (n + 1) * ROWS, :] = k_ref[...]
            values_ref[:, n * ROWS : (n + 1) * ROWS, :] = v_ref[...]
            attend_block(n, place_ref, q_ref, keys_ref, values_ref, more[-9:-5], *more[-5:-2])


def attend(pair, place, query, key_rows, value_rows, before, *deps):
    part = pl.BlockSpec((2, ROWS, LANES), lambda i, t: (pair, i, 0))
    return pl.pallas_call(
        attend_kernel,
        grid_spec=pltpu.PrefetchScalarGridSpec(
            num_scalar_prefetch=1,
            grid=(SEQ // ROWS,),
            in_specs=[part, part, part]
            + [ANY] * (len(before) + len(deps)),
            out_specs=[pl.BlockSpec((ROWS, LANES), lambda i, t: (0, pair))] * 4
            + [pl.BlockSpec((2, ROWS, LANES), lambda i, t: (0, i, 0))],
            scratch_shapes=[pltpu.VMEM((2, SEQ, ROWS), F32), pltpu.VMEM((2, SEQ, ROWS), BF16)]
            + [pltpu.VMEM((2, SEQ, LANES), BF16)] * 2,
        ),
        out_shape=[shaped((ROWS, 2 * LANES), BF16)] * 4 + [shaped((2, SEQ, LANES), BF16)],
        input_output_aliases={4 + k: k for k in range(len(before))},
        compiler_params=params(60),
        cost_estimate=cost(10),
        name="attend",
    )(place, query, key_rows, value_rows, *before, *deps)


def back_block(j, k_ref, v_ref, qa_ref, cos_ref, sin_ref, pg_ref, da_ref, dq_ref, chance_ref, score_ref):
    start, length = j * KEYS, SEQ - j * KEYS
    rows = slice(start, start + KEYS)
    lane = lanes_of((KEYS, LANES))
    key_grads, value_grads = [], []
    for h in range(2):
        keys, values = k_ref[h], v_ref[h]
        for begin in range(0, length, KEYS):
            cut = slice(begin, begin + KEYS)
            scores = product_nt(keys, qa_ref[h, start + begin : start + begin + KEYS, :])
            chance_grad = product_nt(values, da_ref[h, start + begin : start + begin + KEYS, :])
            for i in range(0, KEYS, 64):
                r = slice(i, i + 64)
                chance = jnp.exp(scores[r])
                if begin == 0:
                    chance = jnp.where(hidden_keys((64, KEYS), i, 0), 0.0, chance)
                chance_ref[h, r, cut] = chance.astype(BF16)
                score_ref[h, r, cut] = (chance * chance_grad[r]).astype(BF16)
        value_grads.append(product(chance_ref[h, :, :length], da_ref[h, start:, :]))
        key_grads.append(product(score_ref[h, :, :length], qa_ref[h, start:, :]))
        turned = lax.dot_general(keys[:, :DH], score_ref[h, :, :length], TN, preferred_element_type=F32)
        if j == 0:
            dq_ref[h] = turned
        else:
            dq_ref[h, :, start:] += turned
    key_grad = jnp.where(lane < DH, key_grads[0], pltpu.roll(key_grads[1], DH, 1))
    value_grad = jnp.where(lane < DH, value_grads[0], pltpu.roll(value_grads[1], DH, 1))
    pg_ref[:, LANES : 2 * LANES] = rotate_back(key_grad, cos_ref[...], sin_ref[...]).astype(BF16)
    pg_ref[:, 2 * LANES :] = value_grad.astype(BF16)
    for begin in range(0, KEYS, 256):
        cut = slice(begin, begin + 256)
        turned = [dq_ref[h, :, start + begin : start + begin + 256] for h in range(2)]
        field = jnp.transpose(jnp.concatenate(turned, axis=0)) * (1.0 / math.sqrt(DH))
        pg_ref[cut, :LANES] = rotate_back(field, cos_ref[cut, :], sin_ref[cut, :]).astype(BF16)


def back_kernel(place_ref, k_ref, v_ref, qa_ref, g0, g1, g2, g3, o0, o1, o2, o3, cos_ref, sin_ref, *more):
    pg_ref, da_ref, turned_ref, chance_ref, score_ref = more[-5:]
    step = pl.program_id(0)
    steps = SEQ // KEYS
    span = 64

    @pl.when(step == 0)
    def _():
        lane = lanes_of((span, LANES))
        for which, (grad_ref, out_ref) in enumerate(((g0, o0), (g1, o1), (g2, o2), (g3, o3))):
            begin = (place_ref[0] ^ which) * (SEQ // 4)
            for i in range(SEQ // 4 // span):
                rows = pl.ds(pl.multiple_of(begin + i * span, span), span)
                part = slice(i * span, (i + 1) * span)
                grad = grad_ref[part, :].astype(F32)
                both = grad * out_ref[part, :].astype(F32)
                for h in range(2):
                    inner = jnp.sum(jnp.where(lane // DH == h, both, 0.0), axis=1, keepdims=True)
                    high, middle, low = split_three(-inner)
                    own = grad if h == 0 else pltpu.roll(grad, DH, 1)
                    extra = jnp.where(lane == DH + 1, middle, jnp.where(lane == DH + 2, low, 0.0))
                    extra = jnp.where(lane == DH, high, extra)
                    da_ref[h, rows, :] = jnp.where(lane < DH, own, extra).astype(BF16)

    for j in range(steps):
        pl.when(step == j)(
            functools.partial(
                back_block, j, k_ref, v_ref, qa_ref, cos_ref, sin_ref, pg_ref, da_ref, turned_ref, chance_ref,
                score_ref,
            )
        )


def attend_back(pair, place, key_rows, value_rows, query_more, grads, outs, cosine, sine, *deps):
    keyed = pl.BlockSpec((2, KEYS, LANES), lambda i, s: (pair, i, 0))
    last = lambda g: g.shape[1] // LANES - 2
    quarters = [pl.BlockSpec((SEQ // 4, LANES), lambda i, s, at=last(g): (0, at + pair)) for g in (*grads, *outs)]
    table = pl.BlockSpec((KEYS, LANES), lambda i, s: (i, 0))
    return pl.pallas_call(
        back_kernel,
        grid_spec=pltpu.PrefetchScalarGridSpec(
            num_scalar_prefetch=1,
            grid=(SEQ // KEYS,),
            in_specs=[keyed, keyed, fixed((2, SEQ, LANES))] + quarters + [table, table] + [ANY] * len(deps),
            out_specs=pl.BlockSpec((KEYS, 3 * LANES), lambda i, s: (i, 0)),
            scratch_shapes=[
                pltpu.VMEM((2, SEQ, LANES), BF16),
                pltpu.VMEM((2, DH, SEQ), F32),
                pltpu.VMEM((2, KEYS, SEQ), BF16),
                pltpu.VMEM((2, KEYS, SEQ), BF16),
            ],
        ),
        out_shape=shaped((SEQ, 3 * LANES), BF16),
        compiler_params=params(60),
        cost_estimate=cost(0.5),
        name="attend_back",
    )(place, key_rows, value_rows, query_more, *grads, *outs, cosine, sine, *deps)


CHUNK = 512
HALF = 256
SCALE = math.sqrt(2.0 / math.pi)
CUBIC = 0.044715


def feed_kernel(place_ref, *refs):
    parts_in = refs[:4]
    x_ref, cot_ref, weight_ref, gain_ref, bias_ref = refs[4:9]
    (w_out, out_sib), (up_sib, w_up), (both_sib_y, both_y), downs = refs[9:11], refs[11:13], refs[13:15], refs[15:19]
    down_ref, up_ref, out_ref, own_act, own_hidden, final_ref, state_ref, sum_ref = refs[19:27]
    out_w, up_w, down_w, slope_ref, mid_ref, aunit_ref, munit_ref, ainv_ref, minv_ref, sums, sems = refs[30:]
    tokens, width = x_ref.shape
    local = out_w.shape[1]
    outs = [w_out, both_y.at[pl.ds(width, local)], out_sib, both_sib_y.at[pl.ds(width, local)]]
    ups = [up_sib, both_sib_y.at[pl.ds(0, width)], w_up, both_y.at[pl.ds(0, width)]]
    features = [refs[27], refs[28], down_ref.at[:, 3 * width :], refs[29]]
    mlp_ref, sib_act = down_ref.at[:, 0:width], down_ref.at[:, width : 3 * width]
    mn_ref, sib_hidden = up_ref.at[:, 0:width], up_ref.at[:, width : 3 * width]
    branch_ref = out_ref.at[:, 0:width]
    out_ref[:, width:] = parts_in[3][...]

    loads = []
    for at, (sources, target) in enumerate(((outs, out_w), (ups, up_w), (downs, down_w))):
        for k, source in enumerate(sources):
            loads.append(pltpu.make_async_copy(source, target.at[k], sems.at[4 * at + k]))
    for load in loads:
        load.start()
    sums[...] = jnp.zeros_like(sums)

    def add_sum(k, field):
        part = field[0:8]
        for i in range(8, field.shape[0], 8):
            part = part + field[i : i + 8]
        sums[k] += part

    halves = [range(h, h + HALF, PART) for h in range(0, tokens, HALF)]

    for load in loads[:4]:
        load.wait()
    for parts in halves:
        rows = slice(parts.start, parts.stop)
        branch = None
        for k, part_ref in enumerate(parts_in):
            term = product(part_ref[rows, :], out_w[k])
            branch = term if branch is None else branch + term
        for begin in parts:
            r = slice(begin, begin + PART)
            aunit, ainv = normalize(branch[begin - parts.start : begin - parts.start + PART])
            middle = x_ref[r, :].astype(F32) + aunit * gain_ref[1:2, :] + bias_ref[1:2, :]
            munit, minv = normalize(middle)
            mid_ref[r, :] = middle
            aunit_ref[r, :] = aunit
            munit_ref[r, :] = munit
            ainv_ref[r, :] = jnp.broadcast_to(ainv, (PART, LANES))
            minv_ref[r, :] = jnp.broadcast_to(minv, (PART, LANES))
            mn_ref[r, :] = (munit * gain_ref[2:3, :] + bias_ref[2:3, :]).astype(BF16)

    for k in range(4):
        loads[4 + k].wait()
        act_ref, columns = (sib_act, own_act)[k // 2], slice(k % 2 * width, (k % 2 + 1) * width)
        for parts in halves:
            value = product(mn_ref[parts.start : parts.stop, :], up_w[k])
            for i in range(0, HALF, 16):
                r = slice(parts.start + i, parts.start + i + 16)
                v = value[i : i + 16]
                square = v * v
                bent = jnp.tanh(v * (SCALE + (SCALE * CUBIC) * square))
                half = 0.5 + 0.5 * bent
                act_ref[r, columns] = (v * half).astype(BF16)
                slope = half + v * (1.0 - bent * bent) * (0.5 * SCALE + (1.5 * SCALE * CUBIC) * square)
                slope_ref[k, r, :] = slope.astype(BF16)

    for load in loads[8:]:
        load.wait()
    for parts in halves:
        rows = slice(parts.start, parts.stop)
        branch = None
        for k in range(4):
            act_ref, columns = (sib_act, own_act)[k // 2], slice(k % 2 * width, (k % 2 + 1) * width)
            term = product(act_ref[rows, columns], down_w[k])
            branch = term if branch is None else branch + term
        for begin in parts:
            r = slice(begin, begin + PART)
            unit, inverse = normalize(branch[begin - parts.start : begin - parts.start + PART])
            final_ref[r, :] = (mid_ref[r, :] + unit * gain_ref[3:4, :] + bias_ref[3:4, :]).astype(BF16)
            grad = cot_ref[r, :].astype(F32) * weight_ref[r, :1]
            add_sum(3, grad * unit)
            add_sum(7, grad)
            mlp_ref[r, :] = norm_back(grad, unit, inverse, gain_ref[3:4, :]).astype(BF16)

    mid_grads = []
    for parts in halves:
        rows = slice(parts.start, parts.stop)
        mid_grad = None
        for k in range(4):
            hid_ref, columns = (sib_hidden, own_hidden)[k // 2], slice(k % 2 * width, (k % 2 + 1) * width)
            act_grad = product_nt(mlp_ref[rows, :], down_w[k])
            hidden = (slope_ref[k, rows, :].astype(F32) * act_grad).astype(BF16)
            hid_ref[rows, columns] = hidden
            term = product_nt(hidden, up_w[k])
            mid_grad = term if mid_grad is None else mid_grad + term
        mid_grads.append(mid_grad)
    for parts, mid_all in zip(halves, mid_grads):
        rows = slice(parts.start, parts.stop)
        for begin in parts:
            r = slice(begin, begin + PART)
            mid_grad, munit, aunit = mid_all[begin - parts.start : begin - parts.start + PART], munit_ref[r, :], aunit_ref[r, :]
            grad = cot_ref[r, :].astype(F32) * weight_ref[r, :1]
            state = grad + norm_back(mid_grad, munit, minv_ref[r, :1], gain_ref[2:3, :])
            state_ref[r, :] = state
            branch_ref[r, :] = norm_back(state, aunit, ainv_ref[r, :1], gain_ref[1:2, :]).astype(BF16)
            for k, term in ((1, state * aunit), (2, mid_grad * munit), (5, state), (6, mid_grad)):
                add_sum(k, term)
        for k in (1, 2, 3, 0):
            features[k][rows, :] = product_nt(branch_ref[rows, :], out_w[k]).astype(BF16)
    for k in range(8):
        sum_ref[k : k + 1, :] = column_sum(sums[k])


def feed(place, parts, inputs, cot, weight, gains, biases, outs, ups, both, downs):
    width = inputs.shape[1]
    quarter = inputs.shape[0] // 4
    hid = 2 * width
    local = outs[0].shape[0]
    in_place = lambda s, t: (t[0], 0)
    stat = fixed((quarter, LANES))
    part = (quarter, local)
    shapes = [(quarter, 3 * width + local), (quarter, 3 * width), (quarter, width + local)] + [(quarter, hid)] * 2 + [(quarter, width)] * 2
    kinds = [BF16] * 6 + [F32]
    shapes, kinds = shapes + [(8, width)] + [part] * 3, kinds + [F32] + [BF16] * 3
    return pl.pallas_call(
        feed_kernel,
        grid_spec=pltpu.PrefetchScalarGridSpec(
            num_scalar_prefetch=1,
            grid=(1,),
            in_specs=[fixed(part)] * 4
            + [pl.BlockSpec((quarter, width), in_place)] * 2
            + [stat, fixed((4, width)), fixed((4, width))]
            + [ANY] * 10,
            out_specs=[fixed(shape) for shape in shapes],
            scratch_shapes=[
                pltpu.VMEM((4, local, width), BF16),
                pltpu.VMEM((4, width, width), BF16),
                pltpu.VMEM((4, width, width), BF16),
                pltpu.VMEM((4, quarter, width), BF16),
            ]
            + [pltpu.VMEM((quarter, width), F32)] * 3
            + [pltpu.VMEM((quarter, LANES), F32)] * 2
            + [pltpu.VMEM((8, 8, width), F32), pltpu.SemaphoreType.DMA((12,))],
        ),
        out_shape=[shaped(shape, kind) for shape, kind in zip(shapes, kinds)],
        compiler_params=params(60),
        cost_estimate=cost(34),
        name="feed",
    )(place, *parts, inputs, cot, weight, gains, biases, *outs, *ups, *both, *downs)


def keep_and_send(own, bit, field, keep_ref, send_ref):
    blocks, rows = send_ref.shape[0], send_ref.shape[2]
    for j in range(blocks):
        low = j // bit * 2 * bit + j % bit
        for ref, value in ((keep_ref, own), (send_ref, 1 - own)):
            begin = pl.multiple_of((low + value * bit) * rows, 16)
            ref[j, 0] = field[pl.ds(begin, rows), :]


def weight_kernel(bits, own_ref, x1, x2, y1, y2, *more):
    outs, field_ref = more[-5:-1], more[-1]
    step = pl.program_id(0)
    field = lax.dot_general(x1[...], y1[...], TN, preferred_element_type=F32)
    field = field + lax.dot_general(x2[...], y2[...], TN, preferred_element_type=F32)
    field_ref[...] = field.astype(BF16)
    for half, bit in enumerate(bits):
        keep_ref, send_ref = outs[2 * half : 2 * half + 2]
        if bit == "y":
            rows = keep_ref.shape[2]
            for k, ref in enumerate((keep_ref, send_ref)):

                @pl.when(step == 2 * half + k)
                def _(ref=ref):
                    for j in range(ref.shape[0]):
                        ref[j, 0] = field_ref[j * rows : (j + 1) * rows, :]

        else:

            @pl.when(step // 2 == half)
            def _(bit=bit, keep_ref=keep_ref, send_ref=send_ref):
                keep_and_send(own_ref[own_ref.shape[0] - bit], bit, field_ref, keep_ref, send_ref)


def weight_grad(own_bits, bits, mine, got, y1, name, *deps):
    rows, width = mine.shape[0], y1.shape[1] // 2
    size = lax.axis_size("dp")
    y_spec = lambda first: pl.BlockSpec((rows, CHUNK), lambda s, o: (0, first + s // 2 + 2 * (s % 2)))
    shape = (size, 1, width // size, CHUNK)
    specs = []
    for half, bit in enumerate(bits):
        if bit == "y":
            specs += [fixed(shape)] * 2
        else:
            part = (size // 2,) + shape[1:]
            specs += [pl.BlockSpec(part, lambda s, o, half=half: (jnp.clip(s - 2 * half, 0, 1), 0, 0, 0))] * 2
    return pl.pallas_call(
        functools.partial(weight_kernel, bits),
        grid_spec=pltpu.PrefetchScalarGridSpec(
            num_scalar_prefetch=1,
            grid=(4,),
            in_specs=[fixed((rows, width))] * 2 + [y_spec(0), y_spec(width // CHUNK)] + [ANY] * len(deps),
            out_specs=specs,
            scratch_shapes=[pltpu.VMEM((width, CHUNK), BF16)],
        ),
        out_shape=[shaped(shape, BF16)] * 4,
        compiler_params=params(60),
        cost_estimate=cost(0),
        name=name,
    )(own_bits, mine, got, y1, got, *deps)


def out_weight_kernel(mine_ref, got_ref, own_ref, theirs_ref, own_sib_ref, *more):
    width = more[-1].shape[0] * more[-1].shape[2]
    x1, x2 = mine_ref[:, :width], got_ref[:, :width]
    for out_ref, left, right in ((more[-2], own_ref, own_sib_ref), (more[-1], theirs_ref, got_ref.at[:, width:])):
        field = lax.dot_general(x1, left[...], TN, preferred_element_type=F32)
        field = field + lax.dot_general(x2, right[...], TN, preferred_element_type=F32)
        blocks, unused, rows, unused = out_ref.shape
        for j in range(blocks):
            out_ref[j, 0] = field[j * rows : (j + 1) * rows].astype(BF16)


def out_weight_grad(mine, got, own, theirs, own_sib, *deps):
    rows, local = own.shape
    width = mine.shape[1] - local
    size = lax.axis_size("dp")
    shape = (size, 1, width // size, local)
    arrays = [mine, got, own, theirs, own_sib]
    return pl.pallas_call(
        out_weight_kernel,
        grid=(1,),
        in_specs=[fixed(a.shape) for a in arrays] + [ANY] * len(deps),
        out_specs=[fixed(shape)] * 2,
        out_shape=[shaped(shape, BF16)] * 2,
        compiler_params=params(60),
        cost_estimate=cost(0),
        name="out_weight_grad",
    )(*arrays, *deps)


def in_back_kernel(order_ref, p0, p1, w_ref, x_ref, feed_ref, *more):
    send_ref, keep_ref, sum_ref, sums, field_ref = more[-5:]
    step = pl.program_id(0)
    block = x_ref.shape[0]

    @pl.when(step == 0)
    def _():
        sums[...] = jnp.zeros_like(sums)

    field = None
    for c in range(3):
        cut = slice(c * LANES, (c + 1) * LANES)
        left = jnp.concatenate([p0[:, cut], p1[:, cut]], axis=1)
        term = product_nt(left, w_ref[c])
        field = term if field is None else field + term
    gain_part = bias_part = 0.0
    for begin in range(0, block, PART):
        r = slice(begin, begin + PART)
        unit, unused = normalize(x_ref[r, :].astype(F32))
        field_ref[r, :] = field[r].astype(BF16)
        scaled = field[r] * unit
        for i in range(0, PART, 8):
            gain_part = gain_part + scaled[i : i + 8]
            bias_part = bias_part + field[begin + i : begin + i + 8]
    sums[0] += gain_part
    sums[1] += bias_part

    @pl.when(step // 2 % 2 == 0)
    def _():
        send_ref[...] = field_ref[...]

    @pl.when(step // 2 % 2 == 1)
    def _():
        keep_ref[...] = field_ref[...]

    @pl.when(step == 7)
    def _():
        sum_ref[...] = feed_ref[...]
        for k in range(2):
            sum_ref[4 * k : 4 * k + 1, :] = column_sum(sums[k])


def in_back(place, parts, w_qkv, inputs, feed_sums, *deps):
    block = 256
    tokens, width = inputs.shape
    rows = lambda s, o: (2 * (o[0] ^ (3 - s // 2)) + s % 2, 0)
    shapes = [(tokens // 2, width), (tokens // 2, width), (8, width)]
    return pl.pallas_call(
        in_back_kernel,
        grid_spec=pltpu.PrefetchScalarGridSpec(
            num_scalar_prefetch=1,
            grid=(8,),
            in_specs=[pl.BlockSpec((block, 3 * LANES), rows)] * 2
            + [fixed(w_qkv.shape), pl.BlockSpec((block, width), rows), fixed((8, width))]
            + [ANY] * len(deps),
            out_specs=[
                pl.BlockSpec((block, width), lambda s, o: (s // 4 * 2 + jnp.minimum(s % 4, 1), 0)),
                pl.BlockSpec((block, width), lambda s, o: (s // 4 * 2 + jnp.maximum(s % 4 - 2, 0), 0)),
                fixed(shapes[2]),
            ],
            scratch_shapes=[pltpu.VMEM((2, 8, width), F32), pltpu.VMEM((block, width), BF16)],
        ),
        out_shape=[shaped(shapes[0], BF16), shaped(shapes[1], BF16), shaped(shapes[2], F32)],
        compiler_params=params(60),
        cost_estimate=cost(1),
        name="in_back",
    )(place, *parts, w_qkv, inputs, feed_sums, *deps)


def qkv_kernel(own_ref, n_ref, p_ref, *more):
    keep_ref, send_ref, field_ref = more[-3:]
    rows = n_ref.shape[0]
    for k in range(field_ref.shape[0] // rows):

        @pl.when(pl.program_id(0) == k)
        def _(k=k):
            field_ref[k * rows : (k + 1) * rows, :] = product(n_ref[...], p_ref[...]).astype(BF16)

    @pl.when(pl.program_id(0) == pl.num_programs(0) - 1)
    def _():
        keep_and_send(own_ref[own_ref.shape[0] - 3], 4, field_ref, keep_ref, send_ref)


def qkv_grad(own_bits, normed_turned, part, *deps):
    width, tokens = normed_turned.shape
    columns = part.shape[1]
    size = lax.axis_size("dp")
    steps = 2
    shape = (size // 2, 1, width // size, columns)
    return pl.pallas_call(
        qkv_kernel,
        grid_spec=pltpu.PrefetchScalarGridSpec(
            num_scalar_prefetch=1,
            grid=(steps,),
            in_specs=[pl.BlockSpec((width // steps, tokens), lambda i, o: (i, 0)), fixed(part.shape)] + [ANY] * len(deps),
            out_specs=[fixed(shape)] * 2,
            scratch_shapes=[pltpu.VMEM((width, columns), BF16)],
        ),
        out_shape=[shaped(shape, BF16)] * 2,
        compiler_params=params(60),
        cost_estimate=cost(0),
        name="qkv_grad",
    )(own_bits, normed_turned, part, *deps)


def add_kernel(keep_ref, got_ref, *more):
    for begin in range(0, keep_ref.shape[0], PART):
        r = slice(begin, begin + PART)
        more[-1][r, :] = total([keep_ref[r, :], got_ref[r, :]]).astype(BF16)


def add_core(keep, got, *deps):
    rows, width = keep.shape[0] // 2, keep.shape[1]
    block = rows // 2
    spec = pl.BlockSpec((block, width), lambda i: (i, 0))
    return pl.pallas_call(
        add_kernel,
        grid=(2,),
        in_specs=[spec, spec] + [ANY] * len(deps),
        out_specs=spec,
        out_shape=shaped((rows, width), BF16),
        compiler_params=params(60),
        cost_estimate=cost(3),
        name="add_core",
    )(keep, got, *deps)


def finish_kernel(place_ref, x_ref, state_ref, keep_ref, near_ref, far_ref, gain_ref, *more):
    out_ref = more[-1]
    for begin in range(0, x_ref.shape[0], PART):
        r = slice(begin, begin + PART)
        unit, inverse = normalize(x_ref[r, :].astype(F32))
        grad = total([keep_ref[r, :], near_ref[r, :], far_ref[r, :]])
        out_ref[r, :] = state_ref[r, :] + norm_back(grad, unit, inverse, gain_ref[0:1, :])


def finish(place, inputs, state, keep, near, far, gains, *deps):
    quarter, width = state.shape
    block = 128
    steps = quarter // block
    spec = pl.BlockSpec((block, width), lambda s, t: (s, 0))
    return pl.pallas_call(
        finish_kernel,
        grid_spec=pltpu.PrefetchScalarGridSpec(
            num_scalar_prefetch=1,
            grid=(steps,),
            in_specs=[pl.BlockSpec((block, width), lambda s, t: (t[0] * steps + s, 0)), spec]
            + [pl.BlockSpec((block, width), lambda s, t: (steps + s, 0))] * 2
            + [spec]
            + [fixed(gains.shape)]
            + [ANY] * len(deps),
            out_specs=spec,
        ),
        out_shape=shaped((quarter, width), F32),
        compiler_params=params(60),
        cost_estimate=cost(0),
        name="finish",
    )(place, inputs, state, keep, near, far, gains, *deps)


def per_device(
    inputs, w_qkv, w_out, w_up, w_down, norm_gains, norm_biases, out_cot, group_ids, group_weights
):
    tokens, width = inputs.shape
    quarter = tokens // 4
    place = lax.axis_index("tensor")
    where = place.astype(jnp.int32).reshape(1)
    dp_size = lax.axis_size("dp")
    cosine, sine = rotary_tables()

    dp_index = lax.axis_index("dp").astype(jnp.int32)
    mine = (dp_index % 4).reshape(1)
    owns = jnp.stack([jnp.int32(0)] + [(dp_index // kind) % 2 for kind in dp_kinds()])

    own_ids = lax.dynamic_slice_in_dim(group_ids, place * quarter, quarter, 0)
    groups = jnp.arange(group_weights.shape[0], dtype=jnp.int32)
    lookup = (own_ids[:, None] == groups[None, :]).astype(F32)
    row_weight = jnp.sum(lookup * group_weights[None, :], axis=1, keepdims=True)
    row_weight = jnp.broadcast_to(row_weight, (quarter, LANES))

    up_rows, out_rows, down_rows = w_up.shape[0] // 4, w_out.shape[0] // 4, w_down.shape[0] // 4
    zero = lambda m: 0
    up_sent, down_sent, down_last = move_rows(
        mine,
        [w_up, w_out, w_down],
        [(up_rows + out_rows, width), (down_rows, width), (down_rows, width)],
        [
            (0, lambda m: m * up_rows, 0, zero, up_rows),
            (1, lambda m: m * out_rows, 0, lambda m: up_rows, out_rows),
            (2, lambda m: m * down_rows, 1, zero, down_rows),
            (2, lambda m: (m ^ 3) * down_rows, 2, zero, down_rows),
        ],
        "take",
    )

    def halves(one, two, name):
        rows = one.shape[0] // 2
        moves = [(1, zero, 0, zero, rows), (0, lambda m: rows, 1, zero, rows)]
        low, high = move_rows(mine, [one, two], [(rows, width)] * 2, moves, name)
        return swap(low, "dp", 1), swap(high, "dp", 2), low

    def quarter_moves(target, first, rows, begin, count):
        return [
            (which, lambda m: begin, target, lambda m, which=which: first + (m ^ which) * rows, rows)
            for which in range(count)
        ]

    up_got = y_swap(up_sent)
    up_sib, down_sib, out_sib = core_swap(w_up), core_swap(w_down), core_swap(w_out)
    normed_turned, query, key_rows, value_rows = project(
        inputs, w_qkv, norm_gains, norm_biases, cosine, sine, up_sent
    )
    down_sent = gate(down_sent, normed_turned)
    down_got = y_swap(down_sent)
    up_got = gate(up_got, down_sent)
    up_one, up_two = swap(up_got, "dp", 1), swap(up_got, "dp", 2)

    *outs, more_first = attend(0, where, query, key_rows, value_rows, [], up_got, up_sib, down_sib, out_sib)
    down_got = gate(down_got, outs[0])
    down_one, down_two = swap(down_got, "dp", 1), swap(down_got, "dp", 2)
    down_last = gate(down_last, down_got)
    down_three = y_swap(down_last)
    up_one = gate(up_one, down_last)
    up_low, up_high, last = halves(up_one, up_two, "up_halves")
    *outs, more_second = attend(1, where, query, key_rows, value_rows, outs, last, down_last)
    fetched = (up_low, up_high, down_one, down_two, down_three)
    outs = outs[:1] + [gate(out, *fetched) for out in outs[1:]]
    rows = [outs[0], core_swap(outs[1]), y_swap(outs[2]), diagonal_swap(outs[3], 0, 3)]
    up_one = gate(up_one, outs[1], outs[2], outs[3])

    def last_moves(target, first, rows, begin, half):
        low = max(0, min(half - begin, rows))
        moves = [(3, lambda m: begin, target, lambda m: first + (m ^ 3) * rows, low)] if low else []
        start = begin + low - half
        return moves + [(4, lambda m: start, target, lambda m: first + (m ^ 3) * rows + low, rows - low)]

    half = (up_rows + out_rows) // 2
    (upout_y,) = move_rows(
        mine,
        [up_got, up_one, up_two, up_low, up_high],
        [(w_up.shape[0] + w_out.shape[0], width)],
        quarter_moves(0, 0, up_rows, 0, 3)
        + quarter_moves(0, w_up.shape[0], out_rows, up_rows, 3)
        + last_moves(0, 0, up_rows, 0, half)
        + last_moves(0, w_up.shape[0], out_rows, up_rows, half),
        "up_whole",
    )
    upout_sib_y = core_swap(upout_y)
    down_one = gate(down_one, upout_y)
    (down_y,) = move_rows(
        mine,
        [down_got, down_one, down_two, down_three],
        [w_down.shape],
        quarter_moves(0, 0, down_rows, 0, 4),
        "down_whole",
    )
    down_sib_y = core_swap(down_y)
    row_weight = gate(row_weight, rows[1], rows[2], rows[3], micros=40)

    for_down, for_up, for_out, own_act, own_hidden, final_rows, state_grad, sums_feed, own, for_y, for_far = feed(
        where, [rows[0], rows[2], rows[1], rows[3]], inputs, out_cot, row_weight, norm_gains, norm_biases,
        [w_out, out_sib], [up_sib, w_up], [upout_sib_y, upout_y], [down_sib, down_sib_y, w_down, down_y],
    )

    down_got = core_swap(for_down)
    grads = [own, down_got, y_swap(for_y), diagonal_swap(for_far, 0, 3)]
    for_up = gate(for_up, down_got)
    up_got = core_swap(for_up)
    kinds = dp_kinds()
    both = ["y"] + kinds
    without = lambda bits, *gone: [b for b in bits if b not in gone]
    newest = lambda *items: [item.addends[-1][0] for item in items]
    d0_keep, d0_send, d1_keep, d1_send = weight_grad(
        owns, ("y", 1), for_down, down_got, own_act, "down_grad", for_up
    )
    d0 = Item(kinds, d0_keep, y_swap(d0_send))
    d1 = Item(without(both, 1), d1_keep, swap(d1_send, "dp", 1))
    u0_keep, u0_send, u1_keep, u1_send = weight_grad(
        owns, (1, 2), for_up, up_got, own_hidden, "up_grad", d0_send, d1_send, *grads[2:]
    )
    u1 = Item(without(both, 2), u1_keep, swap(u1_send, "dp", 2))
    for_out = gate(for_out, u1_send)
    out_got = core_swap(for_out)
    part_first = attend_back(
        0, where, key_rows, value_rows, more_first, grads, outs, cosine, sine, u1_send, for_out
    )
    u0_send = gate(u0_send, part_first)
    u0 = Item(without(both, 1), u0_keep, swap(u0_send, "dp", 1))
    out_keep, out_send = out_weight_grad(for_out, out_got, rows[0], rows[2], outs[1], u0_send)
    out_item = Item(kinds, out_keep, y_swap(out_send))

    def qkv_item(part, *deps):
        keep, send = qkv_grad(owns, normed_turned, part, *deps)
        return Item(without(kinds, 4), keep, swap(send, "dp", 4)), send

    q0, last = qkv_item(part_first, out_send)
    last = halve(owns, [d1], 2, last)
    part_second = attend_back(
        1, where, key_rows, value_rows, more_second, grads, outs, cosine, sine, last, *newest(d0, u1)
    )
    part_second = gate(part_second, *newest(u0), micros=3)
    parts = [part_first, part_second]

    send, keep, sums = in_back(where, parts, w_qkv, inputs, sums_feed, *newest(d1, q0, out_item))
    core_got = core_swap(send)
    last = halve(owns, [u1, d0], 1, send)
    last = halve(owns, [u0, out_item], 2, last)
    far = add_core(keep, core_got, last)
    far_got = y_swap(far)
    q1, last = qkv_item(part_second, far)
    last = gate(last, *newest(u1), micros=3)
    last = gate(last, *newest(u0), micros=3)
    last = send_last(owns, [d1, u0, u1], last, far_got)
    last = halve(owns, [q0, q1, out_item], 1, last)
    last = halve(owns, [d0], 2, last)
    input_grad = finish(where, inputs, state_grad, keep, core_got, far_got, norm_gains, last)
    last = send_last(owns, [q0, q1, d0, out_item], input_grad)
    share = width // (4 * dp_size)
    sums = gate(sums, last)
    sums = sums.reshape(8, 4 * dp_size, share).transpose(1, 0, 2)
    sums = jnp.sum(lax.all_to_all(sums, ("dp", "tensor"), 0, 0, tiled=True), axis=0)
    last = gate(last, *[a[0] for a in u0.addends[-3:]], micros=6)
    up_total, down_total, out_total, qkv_total = finals(
        owns, [[(u0, False), (u1, False)], [(d0, True), (d1, True)], [(out_item, True)]], [q0, q1], last
    )
    return (
        final_rows,
        input_grad,
        qkv_total,
        out_total,
        up_total,
        down_total,
        sums[:4],
        sums[4:],
    )


def solution(mesh):
    placed = (
        P("dp", None),
        P(None, None, "tensor"),
        P("tensor", None),
        P(None, "tensor"),
        P("tensor", None),
        P(),
        P(),
        P("dp", None),
        P("dp"),
        P(),
    )
    return jax.shard_map(
        per_device,
        mesh=mesh,
        in_specs=placed,
        out_specs=(
            P(("dp", "tensor"), None),
            P(("dp", "tensor"), None),
            P(None, "dp", "tensor"),
            P("tensor", "dp"),
            P("dp", "tensor"),
            P("tensor", "dp"),
            P(None, ("dp", "tensor")),
            P(None, ("dp", "tensor")),
        ),
        check_vma=False,
    )
```

```python
import functools
import math

import jax
import jax.numpy as jnp
import numpy as np
from jax import lax
from jax.experimental import pallas as pl
from jax.experimental.pallas import tpu as pltpu
from jax.sharding import PartitionSpec as P

DH = 64
SEQ = 2048
EPS = 1e-05
PART = 32
F32 = jnp.float32
BF16 = jnp.bfloat16
LANES = 128
NT = (((1,), (1,)), ((), ()))
TN = (((0,), (0,)), ((), ()))
ANY = pl.BlockSpec(memory_space=pl.ANY)


def params(mebibytes=60):
    return pltpu.CompilerParams(vmem_limit_bytes=mebibytes * 2**20)


def cost(micros):
    return pl.CostEstimate(flops=int(micros * 1.1e9), bytes_accessed=2**16, transcendentals=0)


def shaped(shape, kind):
    return jax.ShapeDtypeStruct(shape, kind)


def fixed(shape):
    return pl.BlockSpec(shape, lambda *unused: (0,) * len(shape))


def gate(field, *deps, micros=0):
    return pl.pallas_call(
        lambda *refs: None,
        in_specs=[ANY] * (1 + len(deps)),
        out_specs=ANY,
        out_shape=shaped(field.shape, field.dtype),
        input_output_aliases={0: 0},
        cost_estimate=cost(micros),
        name="gate",
    )(field, *deps)


def swap(field, axis, bit):
    size = lax.axis_size(axis)
    return lax.ppermute(field, axis, [(i, i ^ bit) for i in range(size)])


def core_swap(field):
    return swap(field, "tensor", 1)


def y_swap(field):
    return swap(field, "tensor", 2)


def total(addends):
    return sum(a.astype(F32) for a in addends)


def diagonal_swap(field, dp_bits, tensor_bits):
    mask = 4 * dp_bits + tensor_bits
    size = 4 * lax.axis_size("dp")
    return lax.ppermute(field, ("dp", "tensor"), [(i, i ^ mask) for i in range(size)])


def move_rows(number, sources, targets, moves, name):
    def kernel(number_ref, *refs):
        source_refs, target_refs, sems = refs[: len(sources)], refs[len(sources) : -1], refs[-1]
        copies = []
        for at, (source, begin, target, end, rows) in enumerate(moves):
            begin, end = (pl.multiple_of(f(number_ref[0]), 16) for f in (begin, end))
            copies.append(
                pltpu.make_async_copy(
                    source_refs[source].at[pl.ds(begin, rows)], target_refs[target].at[pl.ds(end, rows)], sems.at[at]
                )
            )
        for copy in copies:
            copy.start()
        for copy in copies:
            copy.wait()

    return pl.pallas_call(
        kernel,
        grid_spec=pltpu.PrefetchScalarGridSpec(
            num_scalar_prefetch=1,
            grid=(1,),
            in_specs=[ANY] * len(sources),
            out_specs=[fixed(t) for t in targets],
            scratch_shapes=[pltpu.SemaphoreType.DMA((len(moves),))],
        ),
        out_shape=[shaped(t, BF16) for t in targets],
        compiler_params=params(60),
        cost_estimate=cost(1.5),
        name=name,
    )(number, *sources)


def dp_kinds():
    return [1 << k for k in reversed(range(lax.axis_size("dp").bit_length() - 1))]


class Item:
    def __init__(self, left, *arrays):
        self.left = list(left)
        self.addends = [(array, 0, list(left)) for array in arrays]
        self.shape = arrays[0].shape[2:]


def block_index(kinds, bits, free, flips):
    def index(g, own_ref):
        at = 0
        for bit in bits:
            if bit in free:
                value = (g >> (len(free) - 1 - free.index(bit))) & 1
            else:
                value = own_ref[kinds.index(bit)]
                flip = flips(g, bit)
                value = value + flip - 2 * value * flip
            at = 2 * at + value
        return at

    return index


def addend_specs(items, kinds, frees, flips):
    specs, arrays = [], []
    for item, free in zip(items, frees):
        rows, columns = item.shape
        for array, first, bits in item.addends:
            at = block_index(kinds, bits, free, flips)
            fits = array.shape[3] % columns == 0 and first % columns == 0
            block, column = (columns, first // columns) if fits else (array.shape[3], 0)
            specs.append(
                pl.BlockSpec((1, 1, rows, block), lambda g, own_ref, at=at, column=column: (at(g, own_ref), 0, 0, column))
            )
            arrays.append(array)
    return specs, arrays


def sums_of(items, refs):
    refs = iter(refs)
    fields = []
    for item in items:
        terms = []
        for array, first, bits in item.addends:
            ref = next(refs)
            begin = first if ref.shape[3] > item.shape[1] else 0
            terms.append(ref[0, 0, :, begin : begin + item.shape[1]])
        fields.append(total(terms))
    return fields


def put_beside(out_ref, fields):
    begin = 0
    for field in fields:
        out_ref[0, 0, :, begin : begin + field.shape[1]] = field.astype(BF16)
        begin += field.shape[1]


def received(items, got, lefts):
    begin = 0
    for item, left in zip(items, lefts):
        item.addends.append((got, begin, list(left)))
        begin += item.shape[1]


def packed(items):
    return (1, items[0].shape[0], sum(item.shape[1] for item in items))


def halve(owns, items, kind, *deps):
    kinds = ["y"] + dp_kinds()
    frees = [[b for b in item.left if b != kind] for item in items]
    steps = 2 ** len(frees[0])
    specs, arrays = addend_specs(items, kinds, frees, lambda g, bit: 1 if bit == kind else 0)
    shape = packed(items)

    def kernel(own_ref, *refs):
        put_beside(refs[-1], sums_of(items, refs))

    sent = pl.pallas_call(
        kernel,
        grid_spec=pltpu.PrefetchScalarGridSpec(
            num_scalar_prefetch=1,
            grid=(steps,),
            in_specs=specs + [ANY] * len(deps),
            out_specs=pl.BlockSpec((1,) + shape, lambda g, own_ref: (g, 0, 0, 0)),
        ),
        out_shape=shaped((steps,) + shape, BF16),
        compiler_params=params(60),
        cost_estimate=cost(3),
        name="halve",
    )(owns, *arrays, *deps)
    got = y_swap(sent) if kind == "y" else swap(sent, "dp", kind)
    received(items, got, frees)
    for item, free in zip(items, frees):
        item.left = free
    return sent


def send_last(owns, items, *deps):
    pair = ["y", 4] if "y" in items[0].left else [4, 2]
    for item in items:
        while [b for b in item.left if b not in pair]:
            deps = (halve(owns, [item], [b for b in item.left if b not in pair][0], *deps),)
    kinds = ["y"] + dp_kinds()
    masks = [[pair[1]], [pair[0]], pair]
    takers = [[i for i, item in enumerate(items) if all(b in item.left for b in mask)] for mask in masks]
    masks, takers = [m for m, t in zip(masks, takers) if t], [t for t in takers if t]

    def flips(g, bit):
        value = 0
        for k, mask in enumerate(masks):
            if bit in mask:
                value = jnp.where(g == k, 1, value)
        return value

    specs, arrays = addend_specs(items, kinds, [[] for item in items], flips)
    shapes = [(1,) + packed([items[i] for i in taker]) for taker in takers]

    def kernel(own_ref, *refs):
        fields = sums_of(items, refs)
        for k, taker in enumerate(takers):

            @pl.when(pl.program_id(0) == k)
            def _(k=k, taker=taker):
                put_beside(refs[k - len(masks)], [fields[i] for i in taker])

    sent = pl.pallas_call(
        kernel,
        grid_spec=pltpu.PrefetchScalarGridSpec(
            num_scalar_prefetch=1,
            grid=(len(masks),),
            in_specs=specs + [ANY] * len(deps),
            out_specs=[fixed(shape) for shape in shapes],
        ),
        out_shape=[shaped(shape, BF16) for shape in shapes],
        compiler_params=params(60),
        cost_estimate=cost(2),
        name="send_last",
    )(owns, *arrays, *deps)
    for field, mask, taker in zip(sent, masks, takers):
        got = diagonal_swap(field, sum(b for b in mask if b != "y"), 2 if "y" in mask else 0)
        received([items[i] for i in taker], got, [[]] * len(taker))
    for item in items:
        item.left = []
    return sent[-1]


def finals(owns, groups, heads, *deps):
    kinds = ["y"] + dp_kinds()
    items = [item for group in groups for item, turned in group] + heads
    specs, arrays = addend_specs(items, kinds, [[] for item in items], lambda g, bit: 0)
    shapes = []
    for group in groups:
        rows, columns = group[0][0].shape
        shapes.append((columns * len(group), rows) if group[0][1] else (rows, columns * len(group)))

    shapes.append((3, heads[0].shape[0], LANES * len(heads)))

    def kernel(own_ref, *refs):
        fields = sums_of(items, refs)
        for at, field in enumerate(fields[-len(heads) :]):
            for c in range(3):
                refs[-1][c, :, at * LANES : (at + 1) * LANES] = field[:, c * LANES : (c + 1) * LANES]
        fields = iter(fields)
        for group, out_ref in zip(groups, refs[-len(groups) - 1 :]):
            for i, (item, turned) in enumerate(group):
                cut = slice(i * item.shape[1], (i + 1) * item.shape[1])
                field = next(fields)
                if turned:
                    out_ref[cut, :] = jnp.transpose(field)
                else:
                    out_ref[:, cut] = field

    return pl.pallas_call(
        kernel,
        grid_spec=pltpu.PrefetchScalarGridSpec(
            num_scalar_prefetch=1,
            grid=(1,),
            in_specs=specs + [ANY] * len(deps),
            out_specs=[fixed(shape) for shape in shapes],
        ),
        out_shape=[shaped(shape, F32) for shape in shapes],
        compiler_params=params(60),
        cost_estimate=cost(3),
        name="finals",
    )(owns, *arrays, *deps)


def normalize(field):
    mean = jnp.mean(field, axis=-1, keepdims=True)
    centred = field - mean
    inverse = lax.rsqrt(jnp.mean(centred * centred, axis=-1, keepdims=True) + EPS)
    return centred * inverse, inverse


def norm_back(grad, unit, inverse, gain):
    scaled = grad * gain
    mean_one = jnp.mean(scaled, axis=-1, keepdims=True)
    mean_two = jnp.mean(scaled * unit, axis=-1, keepdims=True)
    return inverse * (scaled - mean_one - unit * mean_two)


def rotary_tables():
    half = DH // 2
    frequency = np.exp(np.arange(half, dtype=np.float32) * np.float32(-math.log(10000.0) / half))
    angles = np.arange(SEQ, dtype=np.float32)[:, None] * frequency.astype(np.float32)[None, :]
    cosine, sine = np.cos(angles), np.sin(angles)
    return (
        jnp.asarray(np.concatenate([cosine] * 4, axis=1).astype(np.float32)),
        jnp.asarray(np.concatenate([-sine, sine, -sine, sine], axis=1).astype(np.float32)),
    )


def lanes_of(shape):
    return lax.broadcasted_iota(jnp.int32, shape, 1)


def partner_lanes(field):
    lane = lanes_of(field.shape)
    return jnp.where(lane % DH < DH // 2, pltpu.roll(field, 96, 1), pltpu.roll(field, 32, 1))


def rotate(field, cosine, sine):
    return field * cosine + partner_lanes(field) * sine


def rotate_back(field, cosine, sine):
    return field * cosine - partner_lanes(field) * sine


def split_three(field):
    high = field.astype(BF16).astype(F32)
    rest = field - high
    middle = rest.astype(BF16).astype(F32)
    return high, middle, rest - middle


def product(left, right):
    return jnp.dot(left, right, preferred_element_type=F32)


def product_nt(left, right):
    return lax.dot_general(left, right, NT, preferred_element_type=F32)


def column_sum(field):
    return jnp.sum(field, axis=0, keepdims=True)


def project_kernel(x_ref, w_ref, gain_ref, bias_ref, cos_ref, sin_ref, *more):
    n_ref, q_ref, k_ref, v_ref, normed_ref = more[-5:]
    rows, width = x_ref.shape
    for i in range(rows // PART):
        r = slice(i * PART, (i + 1) * PART)
        unit, unused = normalize(x_ref[r, :].astype(F32))
        normed_ref[r, :] = (unit * gain_ref[0:1, :] + bias_ref[0:1, :]).astype(BF16)
    for i in range(width // 256):
        c = slice(i * 256, (i + 1) * 256)
        n_ref[c, :] = jnp.transpose(normed_ref[:, c])
    lane = lanes_of((PART, LANES))
    ones = jnp.where(lane < DH + 3, 1.0, 0.0)
    for which, out_ref in enumerate((q_ref, k_ref, v_ref)):
        both = product(normed_ref[...], w_ref[which])
        for i in range(rows // PART):
            r = slice(i * PART, (i + 1) * PART)
            for pair in range(both.shape[1] // LANES):
                field = both[r, pair * LANES : (pair + 1) * LANES]
                if which < 2:
                    field = rotate(field, cos_ref[r, :], sin_ref[r, :])
                if which == 0:
                    field = field * (1.0 / math.sqrt(DH))
                extra = jnp.zeros_like(field) if which == 0 else ones
                out_ref[2 * pair, r, :] = jnp.where(lane < DH, field, extra).astype(BF16)
                out_ref[2 * pair + 1, r, :] = jnp.where(lane < DH, pltpu.roll(field, DH, 1), extra).astype(BF16)


def project(inputs, w_qkv, gain, bias, cosine, sine, *deps):
    block = 256
    tokens, width = inputs.shape
    local = w_qkv.shape[2]
    heads = local // DH
    rows = lambda i: (i, 0)
    per_head = pl.BlockSpec((heads, block, LANES), lambda i: (0, i, 0))
    headed = shaped((heads, tokens, LANES), BF16)
    return pl.pallas_call(
        project_kernel,
        grid=(tokens // block,),
        in_specs=[
            pl.BlockSpec((block, width), rows),
            fixed((3, width, local)),
            fixed((4, width)),
            fixed((4, width)),
            pl.BlockSpec((block, LANES), rows),
            pl.BlockSpec((block, LANES), rows),
        ]
        + [ANY] * len(deps),
        out_specs=[pl.BlockSpec((width, block), lambda i: (0, i)), per_head, per_head, per_head],
        out_shape=[shaped((width, tokens), BF16), headed, headed, headed],
        scratch_shapes=[pltpu.VMEM((block, width), BF16)],
        compiler_params=params(60),
        cost_estimate=cost(10),
        name="project",
    )(inputs, w_qkv, gain, bias, cosine, sine, *deps)


ROWS = 512
KEYS = 512
STRIP = 256


def hidden_keys(shape, down, across):
    return lax.broadcasted_iota(jnp.int32, shape, 0) + down > lax.broadcasted_iota(jnp.int32, shape, 1) + across


def attend_block(n, place_ref, q_ref, k_ref, v_ref, out_refs, qa_ref, score_ref, chance_ref):
    start, end = n * ROWS, (n + 1) * ROWS
    row = lax.broadcasted_iota(jnp.int32, (LANES, ROWS), 0)
    lane = lanes_of((ROWS, LANES))
    outs = []
    for h in range(2):
        most = None
        for begin in range(0, end, STRIP):
            scores = product_nt(k_ref[h, begin : begin + STRIP, :], q_ref[h])
            if begin >= start:
                scores = jnp.where(hidden_keys((STRIP, ROWS), begin, start), -1e30, scores)
            score_ref[h, begin : begin + STRIP, :] = scores
            for i in range(0, STRIP, 8):
                most = scores[i : i + 8] if most is None else jnp.maximum(most, scores[i : i + 8])
        top = jnp.max(most, axis=0, keepdims=True)
        for begin in range(0, end, PART):
            r = slice(begin, begin + PART)
            chance_ref[h, r, :] = jnp.exp(score_ref[h, r, :] - top).astype(BF16)
        both = lax.dot_general(v_ref[h, :end, :], chance_ref[h, :end, :], TN, preferred_element_type=F32)
        summed = both[DH : DH + 1, :]
        high, middle, low = split_three(-(top + jnp.log(summed)))
        extra = jnp.where(row == DH + 1, middle, jnp.where(row == DH + 2, low, 0.0))
        extra = jnp.where(row == DH, high, extra)
        turned = jnp.transpose(jnp.where(row < DH, both * (1.0 / summed), extra))
        qa_ref[h] = jnp.where(lane < DH, q_ref[h].astype(F32), turned).astype(BF16)
        outs.append(turned)
    both = jnp.where(lane < DH, outs[0], pltpu.roll(outs[1], DH, 1)).astype(BF16)
    for which, out_ref in enumerate(out_refs):

        @pl.when((place_ref[0] ^ which) == n)
        def _(out_ref=out_ref):
            out_ref[...] = both


def attend_kernel(place_ref, q_ref, k_ref, v_ref, *more):
    block = pl.program_id(0)
    keys_ref, values_ref = more[-2:]
    for n in range(SEQ // ROWS):

        @pl.when(block == n)
        def _(n=n):
            keys_ref[:, n * ROWS : (n + 1) * ROWS, :] = k_ref[...]
            values_ref[:, n * ROWS : (n + 1) * ROWS, :] = v_ref[...]
            attend_block(n, place_ref, q_ref, keys_ref, values_ref, more[-9:-5], *more[-5:-2])


def attend(pair, place, query, key_rows, value_rows, before, *deps):
    part = pl.BlockSpec((2, ROWS, LANES), lambda i, t: (pair, i, 0))
    return pl.pallas_call(
        attend_kernel,
        grid_spec=pltpu.PrefetchScalarGridSpec(
            num_scalar_prefetch=1,
            grid=(SEQ // ROWS,),
            in_specs=[part, part, part]
            + [ANY] * (len(before) + len(deps)),
            out_specs=[pl.BlockSpec((ROWS, LANES), lambda i, t: (0, pair))] * 4
            + [pl.BlockSpec((2, ROWS, LANES), lambda i, t: (0, i, 0))],
            scratch_shapes=[pltpu.VMEM((2, SEQ, ROWS), F32), pltpu.VMEM((2, SEQ, ROWS), BF16)]
            + [pltpu.VMEM((2, SEQ, LANES), BF16)] * 2,
        ),
        out_shape=[shaped((ROWS, 2 * LANES), BF16)] * 4 + [shaped((2, SEQ, LANES), BF16)],
        input_output_aliases={4 + k: k for k in range(len(before))},
        compiler_params=params(60),
        cost_estimate=cost(10),
        name="attend",
    )(place, query, key_rows, value_rows, *before, *deps)


def back_block(j, k_ref, v_ref, qa_ref, cos_ref, sin_ref, pg_ref, da_ref, dq_ref, chance_ref, score_ref):
    start, length = j * KEYS, SEQ - j * KEYS
    rows = slice(start, start + KEYS)
    lane = lanes_of((KEYS, LANES))
    key_grads, value_grads = [], []
    for h in range(2):
        keys, values = k_ref[h], v_ref[h]
        half = KEYS // 2
        chance_ref[h, half:, :half] = jnp.zeros((half, half), BF16)
        score_ref[h, half:, :half] = jnp.zeros((half, half), BF16)
        for begin in range(0, length, KEYS):
            for top in (0, half) if begin == 0 else (0,):
                low, high = (top, top + half) if begin == 0 else (0, KEYS)
                cut = slice(begin + top, begin + KEYS)
                scores = product_nt(keys[low:high], qa_ref[h, start + begin + top : start + begin + KEYS, :])
                chance_grad = product_nt(values[low:high], da_ref[h, start + begin + top : start + begin + KEYS, :])
                for i in range(0, high - low, 64):
                    r, into = slice(i, i + 64), slice(low + i, low + i + 64)
                    chance = jnp.exp(scores[r])
                    if begin == 0:
                        chance = jnp.where(hidden_keys((64, KEYS - top), low + i, top), 0.0, chance)
                    chance_ref[h, into, cut] = chance.astype(BF16)
                    score_ref[h, into, cut] = (chance * chance_grad[r]).astype(BF16)
        value_grads.append(product(chance_ref[h, :, :length], da_ref[h, start:, :]))
        key_grads.append(product(score_ref[h, :, :length], qa_ref[h, start:, :]))
        turned = lax.dot_general(keys[:, :DH], score_ref[h, :, :length], TN, preferred_element_type=F32)
        if j == 0:
            dq_ref[h] = turned
        else:
            dq_ref[h, :, start:] += turned
    key_grad = jnp.where(lane < DH, key_grads[0], pltpu.roll(key_grads[1], DH, 1))
    value_grad = jnp.where(lane < DH, value_grads[0], pltpu.roll(value_grads[1], DH, 1))
    pg_ref[:, LANES : 2 * LANES] = rotate_back(key_grad, cos_ref[...], sin_ref[...]).astype(BF16)
    pg_ref[:, 2 * LANES :] = value_grad.astype(BF16)
    for begin in range(0, KEYS, 256):
        cut = slice(begin, begin + 256)
        turned = [dq_ref[h, :, start + begin : start + begin + 256] for h in range(2)]
        field = jnp.transpose(jnp.concatenate(turned, axis=0)) * (1.0 / math.sqrt(DH))
        pg_ref[cut, :LANES] = rotate_back(field, cos_ref[cut, :], sin_ref[cut, :]).astype(BF16)


def back_kernel(place_ref, k_ref, v_ref, qa_ref, g0, g1, g2, g3, o0, o1, o2, o3, cos_ref, sin_ref, *more):
    pg_ref, da_ref, turned_ref, chance_ref, score_ref = more[-5:]
    step = pl.program_id(0)
    steps = SEQ // KEYS
    span = 64

    @pl.when(step == 0)
    def _():
        lane = lanes_of((span, LANES))
        for which, (grad_ref, out_ref) in enumerate(((g0, o0), (g1, o1), (g2, o2), (g3, o3))):
            begin = (place_ref[0] ^ which) * (SEQ // 4)
            for i in range(SEQ // 4 // span):
                rows = pl.ds(pl.multiple_of(begin + i * span, span), span)
                part = slice(i * span, (i + 1) * span)
                grad = grad_ref[part, :].astype(F32)
                both = grad * out_ref[part, :].astype(F32)
                for h in range(2):
                    inner = jnp.sum(jnp.where(lane // DH == h, both, 0.0), axis=1, keepdims=True)
                    high, middle, low = split_three(-inner)
                    own = grad if h == 0 else pltpu.roll(grad, DH, 1)
                    extra = jnp.where(lane == DH + 1, middle, jnp.where(lane == DH + 2, low, 0.0))
                    extra = jnp.where(lane == DH, high, extra)
                    da_ref[h, rows, :] = jnp.where(lane < DH, own, extra).astype(BF16)

    for j in range(steps):
        pl.when(step == j)(
            functools.partial(
                back_block, j, k_ref, v_ref, qa_ref, cos_ref, sin_ref, pg_ref, da_ref, turned_ref, chance_ref,
                score_ref,
            )
        )


def attend_back(pair, place, key_rows, value_rows, query_more, grads, outs, cosine, sine, *deps):
    keyed = pl.BlockSpec((2, KEYS, LANES), lambda i, s: (pair, i, 0))
    last = lambda g: g.shape[1] // LANES - 2
    quarters = [pl.BlockSpec((SEQ // 4, LANES), lambda i, s, at=last(g): (0, at + pair)) for g in (*grads, *outs)]
    table = pl.BlockSpec((KEYS, LANES), lambda i, s: (i, 0))
    return pl.pallas_call(
        back_kernel,
        grid_spec=pltpu.PrefetchScalarGridSpec(
            num_scalar_prefetch=1,
            grid=(SEQ // KEYS,),
            in_specs=[keyed, keyed, fixed((2, SEQ, LANES))] + quarters + [table, table] + [ANY] * len(deps),
            out_specs=pl.BlockSpec((KEYS, 3 * LANES), lambda i, s: (i, 0)),
            scratch_shapes=[
                pltpu.VMEM((2, SEQ, LANES), BF16),
                pltpu.VMEM((2, DH, SEQ), F32),
                pltpu.VMEM((2, KEYS, SEQ), BF16),
                pltpu.VMEM((2, KEYS, SEQ), BF16),
            ],
        ),
        out_shape=shaped((SEQ, 3 * LANES), BF16),
        compiler_params=params(60),
        cost_estimate=cost(0.5),
        name="attend_back",
    )(place, key_rows, value_rows, query_more, *grads, *outs, cosine, sine, *deps)


CHUNK = 512
HALF = 256
SCALE = math.sqrt(2.0 / math.pi)
CUBIC = 0.044715


def feed_kernel(place_ref, *refs):
    parts_in = refs[:4]
    x_ref, cot_ref, weight_ref, gain_ref, bias_ref = refs[4:9]
    (w_out, out_sib), (up_sib, w_up), (both_sib_y, both_y), downs = refs[9:11], refs[11:13], refs[13:15], refs[15:19]
    down_ref, up_ref, out_ref, own_act, own_hidden, final_ref, state_ref, sum_ref = refs[19:27]
    out_w, up_w, down_w, slope_ref, mid_ref, aunit_ref, munit_ref, ainv_ref, minv_ref, sums, sems = refs[30:]
    tokens, width = x_ref.shape
    local = out_w.shape[1]
    outs = [w_out, both_y.at[pl.ds(width, local)], out_sib, both_sib_y.at[pl.ds(width, local)]]
    ups = [up_sib, both_sib_y.at[pl.ds(0, width)], w_up, both_y.at[pl.ds(0, width)]]
    features = [refs[27], refs[28], down_ref.at[:, 3 * width :], refs[29]]
    mlp_ref, sib_act = down_ref.at[:, 0:width], down_ref.at[:, width : 3 * width]
    mn_ref, sib_hidden = up_ref.at[:, 0:width], up_ref.at[:, width : 3 * width]
    branch_ref = out_ref.at[:, 0:width]
    out_ref[:, width:] = parts_in[3][...]

    loads = []
    for at, (sources, target) in enumerate(((outs, out_w), (ups, up_w), (downs, down_w))):
        for k, source in enumerate(sources):
            loads.append(pltpu.make_async_copy(source, target.at[k], sems.at[4 * at + k]))
    for load in loads:
        load.start()
    sums[...] = jnp.zeros_like(sums)

    def add_sum(k, field):
        part = field[0:8]
        for i in range(8, field.shape[0], 8):
            part = part + field[i : i + 8]
        sums[k] += part

    halves = [range(h, h + HALF, PART) for h in range(0, tokens, HALF)]

    for load in loads[:4]:
        load.wait()
    for parts in halves:
        rows = slice(parts.start, parts.stop)
        branch = None
        for k, part_ref in enumerate(parts_in):
            term = product(part_ref[rows, :], out_w[k])
            branch = term if branch is None else branch + term
        for begin in parts:
            r = slice(begin, begin + PART)
            aunit, ainv = normalize(branch[begin - parts.start : begin - parts.start + PART])
            middle = x_ref[r, :].astype(F32) + aunit * gain_ref[1:2, :] + bias_ref[1:2, :]
            munit, minv = normalize(middle)
            mid_ref[r, :] = middle
            aunit_ref[r, :] = aunit
            munit_ref[r, :] = munit
            ainv_ref[r, :] = jnp.broadcast_to(ainv, (PART, LANES))
            minv_ref[r, :] = jnp.broadcast_to(minv, (PART, LANES))
            mn_ref[r, :] = (munit * gain_ref[2:3, :] + bias_ref[2:3, :]).astype(BF16)

    for k in range(4):
        loads[4 + k].wait()
        act_ref, columns = (sib_act, own_act)[k // 2], slice(k % 2 * width, (k % 2 + 1) * width)
        for parts in halves:
            value = product(mn_ref[parts.start : parts.stop, :], up_w[k])
            for i in range(0, HALF, 16):
                r = slice(parts.start + i, parts.start + i + 16)
                v = value[i : i + 16]
                square = v * v
                bent = jnp.tanh(v * (SCALE + (SCALE * CUBIC) * square))
                half = 0.5 + 0.5 * bent
                act_ref[r, columns] = (v * half).astype(BF16)
                slope = half + v * (1.0 - bent * bent) * (0.5 * SCALE + (1.5 * SCALE * CUBIC) * square)
                slope_ref[k, r, :] = slope.astype(BF16)

    for load in loads[8:]:
        load.wait()
    for parts in halves:
        rows = slice(parts.start, parts.stop)
        branch = None
        for k in range(4):
            act_ref, columns = (sib_act, own_act)[k // 2], slice(k % 2 * width, (k % 2 + 1) * width)
            term = product(act_ref[rows, columns], down_w[k])
            branch = term if branch is None else branch + term
        for begin in parts:
            r = slice(begin, begin + PART)
            unit, inverse = normalize(branch[begin - parts.start : begin - parts.start + PART])
            final_ref[r, :] = (mid_ref[r, :] + unit * gain_ref[3:4, :] + bias_ref[3:4, :]).astype(BF16)
            grad = cot_ref[r, :].astype(F32) * weight_ref[r, :1]
            add_sum(3, grad * unit)
            add_sum(7, grad)
            mlp_ref[r, :] = norm_back(grad, unit, inverse, gain_ref[3:4, :]).astype(BF16)

    mid_grads = []
    for parts in halves:
        rows = slice(parts.start, parts.stop)
        mid_grad = None
        for k in range(4):
            hid_ref, columns = (sib_hidden, own_hidden)[k // 2], slice(k % 2 * width, (k % 2 + 1) * width)
            act_grad = product_nt(mlp_ref[rows, :], down_w[k])
            hidden = (slope_ref[k, rows, :].astype(F32) * act_grad).astype(BF16)
            hid_ref[rows, columns] = hidden
            term = product_nt(hidden, up_w[k])
            mid_grad = term if mid_grad is None else mid_grad + term
        mid_grads.append(mid_grad)
    for parts, mid_all in zip(halves, mid_grads):
        rows = slice(parts.start, parts.stop)
        for begin in parts:
            r = slice(begin, begin + PART)
            mid_grad, munit, aunit = mid_all[begin - parts.start : begin - parts.start + PART], munit_ref[r, :], aunit_ref[r, :]
            grad = cot_ref[r, :].astype(F32) * weight_ref[r, :1]
            state = grad + norm_back(mid_grad, munit, minv_ref[r, :1], gain_ref[2:3, :])
            state_ref[r, :] = state
            branch_ref[r, :] = norm_back(state, aunit, ainv_ref[r, :1], gain_ref[1:2, :]).astype(BF16)
            for k, term in ((1, state * aunit), (2, mid_grad * munit), (5, state), (6, mid_grad)):
                add_sum(k, term)
        for k in (1, 2, 3, 0):
            features[k][rows, :] = product_nt(branch_ref[rows, :], out_w[k]).astype(BF16)
    for k in range(8):
        sum_ref[k : k + 1, :] = column_sum(sums[k])


def feed(place, parts, inputs, cot, weight, gains, biases, outs, ups, both, downs):
    width = inputs.shape[1]
    quarter = inputs.shape[0] // 4
    hid = 2 * width
    local = outs[0].shape[0]
    in_place = lambda s, t: (t[0], 0)
    stat = fixed((quarter, LANES))
    part = (quarter, local)
    shapes = [(quarter, 3 * width + local), (quarter, 3 * width), (quarter, width + local)] + [(quarter, hid)] * 2 + [(quarter, width)] * 2
    kinds = [BF16] * 6 + [F32]
    shapes, kinds = shapes + [(8, width)] + [part] * 3, kinds + [F32] + [BF16] * 3
    return pl.pallas_call(
        feed_kernel,
        grid_spec=pltpu.PrefetchScalarGridSpec(
            num_scalar_prefetch=1,
            grid=(1,),
            in_specs=[fixed(part)] * 4
            + [pl.BlockSpec((quarter, width), in_place)] * 2
            + [stat, fixed((4, width)), fixed((4, width))]
            + [ANY] * 10,
            out_specs=[fixed(shape) for shape in shapes],
            scratch_shapes=[
                pltpu.VMEM((4, local, width), BF16),
                pltpu.VMEM((4, width, width), BF16),
                pltpu.VMEM((4, width, width), BF16),
                pltpu.VMEM((4, quarter, width), BF16),
            ]
            + [pltpu.VMEM((quarter, width), F32)] * 3
            + [pltpu.VMEM((quarter, LANES), F32)] * 2
            + [pltpu.VMEM((8, 8, width), F32), pltpu.SemaphoreType.DMA((12,))],
        ),
        out_shape=[shaped(shape, kind) for shape, kind in zip(shapes, kinds)],
        compiler_params=params(60),
        cost_estimate=cost(34),
        name="feed",
    )(place, *parts, inputs, cot, weight, gains, biases, *outs, *ups, *both, *downs)


def keep_and_send(own, bit, field, keep_ref, send_ref):
    blocks, rows = send_ref.shape[0], send_ref.shape[2]
    for j in range(blocks):
        low = j // bit * 2 * bit + j % bit
        for ref, value in ((keep_ref, own), (send_ref, 1 - own)):
            begin = pl.multiple_of((low + value * bit) * rows, 16)
            ref[j, 0] = field[pl.ds(begin, rows), :]


def weight_kernel(bits, own_ref, x1, x2, y1, y2, *more):
    outs, field_ref = more[-5:-1], more[-1]
    step = pl.program_id(0)
    field = lax.dot_general(x1[...], y1[...], TN, preferred_element_type=F32)
    field = field + lax.dot_general(x2[...], y2[...], TN, preferred_element_type=F32)
    field_ref[...] = field.astype(BF16)
    for half, bit in enumerate(bits):
        keep_ref, send_ref = outs[2 * half : 2 * half + 2]
        if bit == "y":
            rows = keep_ref.shape[2]
            for k, ref in enumerate((keep_ref, send_ref)):

                @pl.when(step == 2 * half + k)
                def _(ref=ref):
                    for j in range(ref.shape[0]):
                        ref[j, 0] = field_ref[j * rows : (j + 1) * rows, :]

        else:

            @pl.when(step // 2 == half)
            def _(bit=bit, keep_ref=keep_ref, send_ref=send_ref):
                keep_and_send(own_ref[own_ref.shape[0] - bit], bit, field_ref, keep_ref, send_ref)


def weight_grad(own_bits, bits, mine, got, y1, name, *deps):
    rows, width = mine.shape[0], y1.shape[1] // 2
    size = lax.axis_size("dp")
    y_spec = lambda first: pl.BlockSpec((rows, CHUNK), lambda s, o: (0, first + s // 2 + 2 * (s % 2)))
    shape = (size, 1, width // size, CHUNK)
    specs = []
    for half, bit in enumerate(bits):
        if bit == "y":
            specs += [fixed(shape)] * 2
        else:
            part = (size // 2,) + shape[1:]
            specs += [pl.BlockSpec(part, lambda s, o, half=half: (jnp.clip(s - 2 * half, 0, 1), 0, 0, 0))] * 2
    return pl.pallas_call(
        functools.partial(weight_kernel, bits),
        grid_spec=pltpu.PrefetchScalarGridSpec(
            num_scalar_prefetch=1,
            grid=(4,),
            in_specs=[fixed((rows, width))] * 2 + [y_spec(0), y_spec(width // CHUNK)] + [ANY] * len(deps),
            out_specs=specs,
            scratch_shapes=[pltpu.VMEM((width, CHUNK), BF16)],
        ),
        out_shape=[shaped(shape, BF16)] * 4,
        compiler_params=params(60),
        cost_estimate=cost(0),
        name=name,
    )(own_bits, mine, got, y1, got, *deps)


def out_weight_kernel(mine_ref, got_ref, own_ref, theirs_ref, own_sib_ref, *more):
    width = more[-1].shape[0] * more[-1].shape[2]
    x1, x2 = mine_ref[:, :width], got_ref[:, :width]
    for out_ref, left, right in ((more[-2], own_ref, own_sib_ref), (more[-1], theirs_ref, got_ref.at[:, width:])):
        field = lax.dot_general(x1, left[...], TN, preferred_element_type=F32)
        field = field + lax.dot_general(x2, right[...], TN, preferred_element_type=F32)
        blocks, unused, rows, unused = out_ref.shape
        for j in range(blocks):
            out_ref[j, 0] = field[j * rows : (j + 1) * rows].astype(BF16)


def out_weight_grad(mine, got, own, theirs, own_sib, *deps):
    rows, local = own.shape
    width = mine.shape[1] - local
    size = lax.axis_size("dp")
    shape = (size, 1, width // size, local)
    arrays = [mine, got, own, theirs, own_sib]
    return pl.pallas_call(
        out_weight_kernel,
        grid=(1,),
        in_specs=[fixed(a.shape) for a in arrays] + [ANY] * len(deps),
        out_specs=[fixed(shape)] * 2,
        out_shape=[shaped(shape, BF16)] * 2,
        compiler_params=params(60),
        cost_estimate=cost(0),
        name="out_weight_grad",
    )(*arrays, *deps)


def in_back_kernel(order_ref, p0, p1, w_ref, x_ref, feed_ref, *more):
    send_ref, keep_ref, sum_ref, sums, field_ref = more[-5:]
    step = pl.program_id(0)
    block = x_ref.shape[0]

    @pl.when(step == 0)
    def _():
        sums[...] = jnp.zeros_like(sums)

    field = None
    for c in range(3):
        cut = slice(c * LANES, (c + 1) * LANES)
        left = jnp.concatenate([p0[:, cut], p1[:, cut]], axis=1)
        term = product_nt(left, w_ref[c])
        field = term if field is None else field + term
    gain_part = bias_part = 0.0
    for begin in range(0, block, PART):
        r = slice(begin, begin + PART)
        unit, unused = normalize(x_ref[r, :].astype(F32))
        field_ref[r, :] = field[r].astype(BF16)
        scaled = field[r] * unit
        for i in range(0, PART, 8):
            gain_part = gain_part + scaled[i : i + 8]
            bias_part = bias_part + field[begin + i : begin + i + 8]
    sums[0] += gain_part
    sums[1] += bias_part

    @pl.when(step // 2 % 2 == 0)
    def _():
        send_ref[...] = field_ref[...]

    @pl.when(step // 2 % 2 == 1)
    def _():
        keep_ref[...] = field_ref[...]

    @pl.when(step == 7)
    def _():
        sum_ref[...] = feed_ref[...]
        for k in range(2):
            sum_ref[4 * k : 4 * k + 1, :] = column_sum(sums[k])


def in_back(place, parts, w_qkv, inputs, feed_sums, *deps):
    block = 256
    tokens, width = inputs.shape
    rows = lambda s, o: (2 * (o[0] ^ (3 - s // 2)) + s % 2, 0)
    shapes = [(tokens // 2, width), (tokens // 2, width), (8, width)]
    return pl.pallas_call(
        in_back_kernel,
        grid_spec=pltpu.PrefetchScalarGridSpec(
            num_scalar_prefetch=1,
            grid=(8,),
            in_specs=[pl.BlockSpec((block, 3 * LANES), rows)] * 2
            + [fixed(w_qkv.shape), pl.BlockSpec((block, width), rows), fixed((8, width))]
            + [ANY] * len(deps),
            out_specs=[
                pl.BlockSpec((block, width), lambda s, o: (s // 4 * 2 + jnp.minimum(s % 4, 1), 0)),
                pl.BlockSpec((block, width), lambda s, o: (s // 4 * 2 + jnp.maximum(s % 4 - 2, 0), 0)),
                fixed(shapes[2]),
            ],
            scratch_shapes=[pltpu.VMEM((2, 8, width), F32), pltpu.VMEM((block, width), BF16)],
        ),
        out_shape=[shaped(shapes[0], BF16), shaped(shapes[1], BF16), shaped(shapes[2], F32)],
        compiler_params=params(60),
        cost_estimate=cost(1),
        name="in_back",
    )(place, *parts, w_qkv, inputs, feed_sums, *deps)


def qkv_kernel(own_ref, n_ref, p_ref, *more):
    keep_ref, send_ref, field_ref = more[-3:]
    rows = n_ref.shape[0]
    for k in range(field_ref.shape[0] // rows):

        @pl.when(pl.program_id(0) == k)
        def _(k=k):
            field_ref[k * rows : (k + 1) * rows, :] = product(n_ref[...], p_ref[...]).astype(BF16)

    @pl.when(pl.program_id(0) == pl.num_programs(0) - 1)
    def _():
        keep_and_send(own_ref[own_ref.shape[0] - 3], 4, field_ref, keep_ref, send_ref)


def qkv_grad(own_bits, normed_turned, part, *deps):
    width, tokens = normed_turned.shape
    columns = part.shape[1]
    size = lax.axis_size("dp")
    steps = 2
    shape = (size // 2, 1, width // size, columns)
    return pl.pallas_call(
        qkv_kernel,
        grid_spec=pltpu.PrefetchScalarGridSpec(
            num_scalar_prefetch=1,
            grid=(steps,),
            in_specs=[pl.BlockSpec((width // steps, tokens), lambda i, o: (i, 0)), fixed(part.shape)] + [ANY] * len(deps),
            out_specs=[fixed(shape)] * 2,
            scratch_shapes=[pltpu.VMEM((width, columns), BF16)],
        ),
        out_shape=[shaped(shape, BF16)] * 2,
        compiler_params=params(60),
        cost_estimate=cost(0),
        name="qkv_grad",
    )(own_bits, normed_turned, part, *deps)


def add_kernel(keep_ref, got_ref, *more):
    for begin in range(0, keep_ref.shape[0], PART):
        r = slice(begin, begin + PART)
        more[-1][r, :] = total([keep_ref[r, :], got_ref[r, :]]).astype(BF16)


def add_core(keep, got, *deps):
    rows, width = keep.shape[0] // 2, keep.shape[1]
    block = rows // 2
    spec = pl.BlockSpec((block, width), lambda i: (i, 0))
    return pl.pallas_call(
        add_kernel,
        grid=(2,),
        in_specs=[spec, spec] + [ANY] * len(deps),
        out_specs=spec,
        out_shape=shaped((rows, width), BF16),
        compiler_params=params(60),
        cost_estimate=cost(3),
        name="add_core",
    )(keep, got, *deps)


def finish_kernel(place_ref, x_ref, state_ref, keep_ref, near_ref, far_ref, gain_ref, *more):
    out_ref = more[-1]
    for begin in range(0, x_ref.shape[0], PART):
        r = slice(begin, begin + PART)
        unit, inverse = normalize(x_ref[r, :].astype(F32))
        grad = total([keep_ref[r, :], near_ref[r, :], far_ref[r, :]])
        out_ref[r, :] = state_ref[r, :] + norm_back(grad, unit, inverse, gain_ref[0:1, :])


def finish(place, inputs, state, keep, near, far, gains, *deps):
    quarter, width = state.shape
    block = 128
    steps = quarter // block
    spec = pl.BlockSpec((block, width), lambda s, t: (s, 0))
    return pl.pallas_call(
        finish_kernel,
        grid_spec=pltpu.PrefetchScalarGridSpec(
            num_scalar_prefetch=1,
            grid=(steps,),
            in_specs=[pl.BlockSpec((block, width), lambda s, t: (t[0] * steps + s, 0)), spec]
            + [pl.BlockSpec((block, width), lambda s, t: (steps + s, 0))] * 2
            + [spec]
            + [fixed(gains.shape)]
            + [ANY] * len(deps),
            out_specs=spec,
        ),
        out_shape=shaped((quarter, width), F32),
        compiler_params=params(60),
        cost_estimate=cost(0),
        name="finish",
    )(place, inputs, state, keep, near, far, gains, *deps)


def per_device(
    inputs, w_qkv, w_out, w_up, w_down, norm_gains, norm_biases, out_cot, group_ids, group_weights
):
    tokens, width = inputs.shape
    quarter = tokens // 4
    place = lax.axis_index("tensor")
    where = place.astype(jnp.int32).reshape(1)
    dp_size = lax.axis_size("dp")
    cosine, sine = rotary_tables()

    dp_index = lax.axis_index("dp").astype(jnp.int32)
    mine = (dp_index % 4).reshape(1)
    owns = jnp.stack([jnp.int32(0)] + [(dp_index // kind) % 2 for kind in dp_kinds()])

    own_ids = lax.dynamic_slice_in_dim(group_ids, place * quarter, quarter, 0)
    groups = jnp.arange(group_weights.shape[0], dtype=jnp.int32)
    lookup = (own_ids[:, None] == groups[None, :]).astype(F32)
    row_weight = jnp.sum(lookup * group_weights[None, :], axis=1, keepdims=True)
    row_weight = jnp.broadcast_to(row_weight, (quarter, LANES))

    up_rows, out_rows, down_rows = w_up.shape[0] // 4, w_out.shape[0] // 4, w_down.shape[0] // 4
    zero = lambda m: 0
    up_sent, down_sent, down_last = move_rows(
        mine,
        [w_up, w_out, w_down],
        [(up_rows + out_rows, width), (down_rows, width), (down_rows, width)],
        [
            (0, lambda m: m * up_rows, 0, zero, up_rows),
            (1, lambda m: m * out_rows, 0, lambda m: up_rows, out_rows),
            (2, lambda m: m * down_rows, 1, zero, down_rows),
            (2, lambda m: (m ^ 3) * down_rows, 2, zero, down_rows),
        ],
        "take",
    )

    def halves(one, two, name):
        rows = one.shape[0] // 2
        moves = [(1, zero, 0, zero, rows), (0, lambda m: rows, 1, zero, rows)]
        low, high = move_rows(mine, [one, two], [(rows, width)] * 2, moves, name)
        return swap(low, "dp", 1), swap(high, "dp", 2), low

    def quarter_moves(target, first, rows, begin, count):
        return [
            (which, lambda m: begin, target, lambda m, which=which: first + (m ^ which) * rows, rows)
            for which in range(count)
        ]

    up_got = y_swap(up_sent)
    up_sib, down_sib, out_sib = core_swap(w_up), core_swap(w_down), core_swap(w_out)
    normed_turned, query, key_rows, value_rows = project(
        inputs, w_qkv, norm_gains, norm_biases, cosine, sine, up_sent
    )
    down_sent = gate(down_sent, normed_turned)
    down_got = y_swap(down_sent)
    up_got = gate(up_got, down_sent)
    up_one, up_two = swap(up_got, "dp", 1), swap(up_got, "dp", 2)

    *outs, more_first = attend(0, where, query, key_rows, value_rows, [], up_got, up_sib, down_sib, out_sib)
    down_got = gate(down_got, outs[0])
    down_one, down_two = swap(down_got, "dp", 1), swap(down_got, "dp", 2)
    down_last = gate(down_last, down_got)
    down_three = y_swap(down_last)
    up_one = gate(up_one, down_last)
    up_low, up_high, last = halves(up_one, up_two, "up_halves")
    *outs, more_second = attend(1, where, query, key_rows, value_rows, outs, last, down_last)
    fetched = (up_low, up_high, down_one, down_two, down_three)
    outs = outs[:1] + [gate(out, *fetched) for out in outs[1:]]
    rows = [outs[0], core_swap(outs[1]), y_swap(outs[2]), diagonal_swap(outs[3], 0, 3)]
    up_one = gate(up_one, outs[1], outs[2], outs[3])

    def last_moves(target, first, rows, begin, half):
        low = max(0, min(half - begin, rows))
        moves = [(3, lambda m: begin, target, lambda m: first + (m ^ 3) * rows, low)] if low else []
        start = begin + low - half
        return moves + [(4, lambda m: start, target, lambda m: first + (m ^ 3) * rows + low, rows - low)]

    half = (up_rows + out_rows) // 2
    (upout_y,) = move_rows(
        mine,
        [up_got, up_one, up_two, up_low, up_high],
        [(w_up.shape[0] + w_out.shape[0], width)],
        quarter_moves(0, 0, up_rows, 0, 3)
        + quarter_moves(0, w_up.shape[0], out_rows, up_rows, 3)
        + last_moves(0, 0, up_rows, 0, half)
        + last_moves(0, w_up.shape[0], out_rows, up_rows, half),
        "up_whole",
    )
    upout_sib_y = core_swap(upout_y)
    down_one = gate(down_one, upout_y)
    (down_y,) = move_rows(
        mine,
        [down_got, down_one, down_two, down_three],
        [w_down.shape],
        quarter_moves(0, 0, down_rows, 0, 4),
        "down_whole",
    )
    down_sib_y = core_swap(down_y)
    row_weight = gate(row_weight, rows[1], rows[2], rows[3], micros=40)

    for_down, for_up, for_out, own_act, own_hidden, final_rows, state_grad, sums_feed, own, for_y, for_far = feed(
        where, [rows[0], rows[2], rows[1], rows[3]], inputs, out_cot, row_weight, norm_gains, norm_biases,
        [w_out, out_sib], [up_sib, w_up], [upout_sib_y, upout_y], [down_sib, down_sib_y, w_down, down_y],
    )

    down_got = core_swap(for_down)
    grads = [own, down_got, y_swap(for_y), diagonal_swap(for_far, 0, 3)]
    for_up = gate(for_up, down_got)
    up_got = core_swap(for_up)
    kinds = dp_kinds()
    both = ["y"] + kinds
    without = lambda bits, *gone: [b for b in bits if b not in gone]
    newest = lambda *items: [item.addends[-1][0] for item in items]
    d0_keep, d0_send, d1_keep, d1_send = weight_grad(
        owns, ("y", 1), for_down, down_got, own_act, "down_grad", for_up
    )
    d0 = Item(kinds, d0_keep, y_swap(d0_send))
    d1 = Item(without(both, 1), d1_keep, swap(d1_send, "dp", 1))
    u0_keep, u0_send, u1_keep, u1_send = weight_grad(
        owns, (1, 2), for_up, up_got, own_hidden, "up_grad", d0_send, d1_send, *grads[2:]
    )
    u1 = Item(without(both, 2), u1_keep, swap(u1_send, "dp", 2))
    for_out = gate(for_out, u1_send)
    out_got = core_swap(for_out)
    part_first = attend_back(
        0, where, key_rows, value_rows, more_first, grads, outs, cosine, sine, u1_send, for_out
    )
    u0_send = gate(u0_send, part_first)
    u0 = Item(without(both, 1), u0_keep, swap(u0_send, "dp", 1))
    out_keep, out_send = out_weight_grad(for_out, out_got, rows[0], rows[2], outs[1], u0_send)
    out_item = Item(kinds, out_keep, y_swap(out_send))

    def qkv_item(part, *deps):
        keep, send = qkv_grad(owns, normed_turned, part, *deps)
        return Item(without(kinds, 4), keep, swap(send, "dp", 4)), send

    q0, last = qkv_item(part_first, out_send)
    last = halve(owns, [d1], 2, last)
    part_second = attend_back(
        1, where, key_rows, value_rows, more_second, grads, outs, cosine, sine, last, *newest(d0, u1)
    )
    part_second = gate(part_second, *newest(u0), micros=3)
    parts = [part_first, part_second]

    send, keep, sums = in_back(where, parts, w_qkv, inputs, sums_feed, *newest(d1, q0, out_item))
    core_got = core_swap(send)
    last = halve(owns, [u1, d0], 1, send)
    last = halve(owns, [u0, out_item], 2, last)
    far = add_core(keep, core_got, last)
    far_got = y_swap(far)
    q1, last = qkv_item(part_second, far)
    last = gate(last, *newest(u1), micros=3)
    last = gate(last, *newest(u0), micros=3)
    last = send_last(owns, [d1, u0, u1], last, far_got)
    last = halve(owns, [q0, q1, out_item], 1, last)
    last = halve(owns, [d0], 2, last)
    input_grad = finish(where, inputs, state_grad, keep, core_got, far_got, norm_gains, last)
    last = send_last(owns, [q0, q1, d0, out_item], input_grad)
    share = width // (4 * dp_size)
    sums = gate(sums, last)
    sums = sums.reshape(8, 4 * dp_size, share).transpose(1, 0, 2)
    sums = jnp.sum(lax.all_to_all(sums, ("dp", "tensor"), 0, 0, tiled=True), axis=0)
    last = gate(last, *[a[0] for a in u0.addends[-3:]], micros=6)
    up_total, down_total, out_total, qkv_total = finals(
        owns, [[(u0, False), (u1, False)], [(d0, True), (d1, True)], [(out_item, True)]], [q0, q1], last
    )
    return (
        final_rows,
        input_grad,
        qkv_total,
        out_total,
        up_total,
        down_total,
        sums[:4],
        sums[4:],
    )


def solution(mesh):
    placed = (
        P("dp", None),
        P(None, None, "tensor"),
        P("tensor", None),
        P(None, "tensor"),
        P("tensor", None),
        P(),
        P(),
        P("dp", None),
        P("dp"),
        P(),
    )
    return jax.shard_map(
        per_device,
        mesh=mesh,
        in_specs=placed,
        out_specs=(
            P(("dp", "tensor"), None),
            P(("dp", "tensor"), None),
            P(None, "dp", "tensor"),
            P("tensor", "dp"),
            P("dp", "tensor"),
            P("tensor", "dp"),
            P(None, ("dp", "tensor")),
            P(None, ("dp", "tensor")),
        ),
        check_vma=False,
    )
```
